32 devices in a mesh: row: 8 (over z, x), col: 4 (over y, core).
Axes of the slice: x: 2, y: 2, z: 4, core: 2. Of those that a mesh axis runs over, the one named last changes fastest.
Arguments:
- features: bfloat16 [4, 1024, 256], P('col', 'row'), may hold values from -6 to 6
- weight: bfloat16 [256, 256], replicated, may hold values from -0.375 to 0.375
- tile_values: bfloat16 [8, 4, 32, 128, 128], P('row', 'col'), may hold values from -0.125 to 0.125
- tile_slots: int32 [8, 4, 32], P('row', 'col'), may hold values from 0 to 31, as said below
- tile_counts: int32 [8, 4], P('row', 'col'), may hold values from 1 to 32, as said below
- cotangent: bfloat16 [8, 512, 256], P('row', 'col'), may hold values from -6 to 6
Outputs:
- layer_out: bfloat16 [8, 512, 256], P('row', 'col')
- feature_grad: bfloat16 [4, 1024, 256], P('col', 'row')
- weight_grad: float32 [256, 256], replicated
The draws below stay inside these ranges and needn't reach their ends.
Inputs may be any that keep to these rules, and one draw needn't show every extreme that they name: `tile_slots`: within one grid block the 32 slot positions are distinct; slots from tile_counts on carry no edges. `tile_counts`: some grid block uses all 32 slots.
All inputs are finite; a program needn't handle non-finite values.
Results may differ from the reference program's by a relative error of at most 0.022.
Values may be sent and summed in bfloat16 or wider, within the bound.
No kernel may reach another device: no remote copies, remote signals or barrier semaphores. Data moves between devices by JAX's collectives and lax.ppermute only.
A program may use at most 64 MiB of HBM per device.

```python
import math
import jax
import jax.numpy as jnp
from jax import lax

F = 256
TILE = 128
ST = 1
GROUP = 32
NRB = 512
NCB = 1024
NODES = 4096
K_MAX = 32
N_ROW = 8
N_COL = 4


def draw_tile_slots(key, part):
    positions = N_ROW * ST * N_COL * ST
    subkeys = jax.random.split(jax.random.fold_in(key, 23), N_ROW * N_COL)
    orders = jax.vmap(lambda subkey: jax.random.permutation(subkey, positions)[:K_MAX])(subkeys)
    return orders.reshape(N_ROW, N_COL, K_MAX).astype(jnp.int32)


def draw_tile_counts(key, part):
    first_key, second_key = jax.random.split(jax.random.fold_in(key, 11))
    spread = K_MAX - K_MAX // 8
    ranked = jax.random.randint(first_key, (N_ROW * N_COL,), 0, spread + 1)
    counts_drawn = K_MAX // 8 + ranked * ranked * ranked // (spread * spread)
    chosen = jax.random.randint(second_key, (), 0, N_ROW * N_COL)
    filled = jnp.where(jnp.arange(N_ROW * N_COL) == chosen, K_MAX, counts_drawn)
    return filled.reshape(N_ROW, N_COL).astype(jnp.int32)


def levels(stream_key, dims, pieces, smallest, high):
    def one(dim, parts):
        heights = jax.random.uniform(jax.random.fold_in(jax.random.fold_in(stream_key, 6), dim), (parts,), jnp.float32, smallest / len(pieces), high / len(pieces))
        return jnp.repeat(jnp.exp(heights), dims[dim] // parts).reshape((-1,) + (1,) * (len(dims) - dim - 1))

    loudness = one(*pieces[0])
    for cut in pieces[1:]:
        loudness = loudness * one(*cut)
    return loudness


def noise(own_key, shape, scale, reach, cuts=(), kind=jnp.bfloat16):
    values = scale * jax.random.normal(own_key, shape, jnp.float32)
    if cuts:
        values = values * levels(own_key, shape, cuts, -0.22, 0.18)
    return jnp.clip(values, -reach, reach).astype(kind)


def setup_inputs(seed: int = 0) -> dict:
    seeds = jax.random.split(jax.random.key(seed), 7)
    return {
        "features": noise(seeds[0], (N_COL, NCB, F), 1.0, 6.0, ((0, 4), (1, 8))),
        "weight": noise(seeds[1], (F, F), F ** -0.5, 0.375),
        "tile_values": noise(seeds[2], (N_ROW, N_COL, K_MAX, TILE, TILE), (TILE * K_MAX // (2 * ST)) ** -0.5, 0.125, ((0, 8), (1, 4))),
        "tile_slots": draw_tile_slots(jax.random.fold_in(seeds[6], 71), 0),
        "tile_counts": draw_tile_counts(jax.random.fold_in(seeds[6], 71), 0),
        "cotangent": noise(seeds[5], (N_ROW, NRB, F), 1.0, 6.0, ((0, 8), (1, 4))),
    }


def tile_products(values, in_index, out_index, live_count, source, out_tiles, pattern):
    tile_size = values.shape[1]
    feat_width = source.shape[2]

    def one_group(step_index, running):
        first_slot = (step_index * GROUP).astype(jnp.int32)
        blocks = lax.dynamic_slice_in_dim(values, first_slot, GROUP, 0).astype(jnp.float32)
        picked = lax.dynamic_slice_in_dim(in_index, first_slot, GROUP, 0)
        target = lax.dynamic_slice_in_dim(out_index, first_slot, GROUP, 0)
        active = first_slot + jnp.arange(GROUP, dtype=jnp.int32) < live_count
        operands = jnp.take(source, picked, axis=0).astype(jnp.float32)
        products = jnp.einsum(pattern, blocks, operands)
        placing = ((target[None, :] == jnp.arange(out_tiles, dtype=jnp.int32)[:, None]) & active[None, :]).astype(jnp.float32)
        return running + jnp.einsum('rk,kaf->raf', placing, products, precision=lax.Precision.HIGHEST)
    groups = ((live_count + GROUP - 1) // GROUP).astype(jnp.int32)
    start_value = jnp.zeros((out_tiles, tile_size, feat_width), jnp.float32)
    return lax.fori_loop(jnp.int32(0), groups, one_group, start_value)

def reference(features, weight, tile_values, tile_slots, tile_counts, cotangent):
    row_tiles = NRB // TILE
    col_tiles = NCB // TILE

    def forward_part(row_index, col_index):
        slots = tile_slots[row_index, col_index]
        tile_rows = slots // col_tiles
        tile_cols = slots % col_tiles
        column = features[col_index].reshape(col_tiles, TILE, F)
        result = tile_products(tile_values[row_index, col_index], tile_cols, tile_rows, tile_counts[row_index, col_index], column, row_tiles, 'kab,kbf->kaf')
        return result.reshape(NRB, F)

    def row_block(row_index):

        def add_part(running, col_index):
            partial_value = forward_part(row_index, col_index)
            partial_value = lax.optimization_barrier(partial_value.astype(jnp.bfloat16)).astype(jnp.float32)
            return (running + partial_value, None)
        running, _ = lax.scan(add_part, jnp.zeros((NRB, F), jnp.float32), jnp.arange(N_COL, dtype=jnp.int32))
        return running.astype(jnp.bfloat16)
    aggregated = lax.map(row_block, jnp.arange(N_ROW, dtype=jnp.int32))
    flattened = aggregated.reshape(NODES, F)
    layer_out = jnp.dot(flattened, weight, preferred_element_type=jnp.float32).astype(jnp.bfloat16).reshape(N_ROW, NRB, F)
    cot_flat = cotangent.reshape(NODES, F)
    back_grad = jnp.dot(cot_flat, weight.T, preferred_element_type=jnp.float32).astype(jnp.bfloat16).reshape(N_ROW, NRB, F)

    def backward_part(row_index, col_index):
        slots = tile_slots[row_index, col_index]
        tile_rows = slots // col_tiles
        tile_cols = slots % col_tiles
        back_tiles = back_grad[row_index].reshape(row_tiles, TILE, F)
        result = tile_products(tile_values[row_index, col_index], tile_rows, tile_cols, tile_counts[row_index, col_index], back_tiles, col_tiles, 'kab,kaf->kbf')
        return result.reshape(NCB, F)

    def col_block(col_index):

        def add_part(running, row_index):
            partial_value = backward_part(row_index, col_index)
            partial_value = lax.optimization_barrier(partial_value.astype(jnp.bfloat16)).astype(jnp.float32)
            return (running + partial_value, None)
        running, _ = lax.scan(add_part, jnp.zeros((NCB, F), jnp.float32), jnp.arange(N_ROW, dtype=jnp.int32))
        return running.astype(jnp.bfloat16)
    feature_grad = lax.map(col_block, jnp.arange(N_COL, dtype=jnp.int32))
    weight_grad = jnp.dot(flattened.T, cot_flat, preferred_element_type=jnp.float32) * (1.0 / math.sqrt(NODES))
    return (layer_out, feature_grad, weight_grad)
```

```python
import math

import jax
import jax.numpy as jnp
from jax import lax
from jax.experimental import pallas as pl
from jax.experimental.pallas import tpu as pltpu
from jax.sharding import PartitionSpec as P

F32 = jnp.float32
BF16 = jnp.bfloat16
VMEM = pl.BlockSpec(memory_space=pltpu.VMEM)
SMEM = pl.BlockSpec(memory_space=pltpu.SMEM)
PARAMS = pltpu.CompilerParams(vmem_limit_bytes=56 * 2**20)


def dense_kernel(slots_ref, count_ref, tiles_ref, out_ref):
    slot_count, tile, _ = tiles_ref.shape
    col_tiles = out_ref.shape[1] // tile
    out_ref[...] = jnp.zeros_like(out_ref)

    def place(k, carry):
        slot = slots_ref[k]
        row = pl.multiple_of((slot // col_tiles) * tile, tile)
        col = pl.multiple_of((slot % col_tiles) * tile, tile)
        out_ref[pl.ds(row, tile), pl.ds(col, tile)] = tiles_ref[k]
        return carry

    lax.fori_loop(0, jnp.minimum(count_ref[0], slot_count), place, 0)


def dense_block(tiles, slots, count, rows, cols):
    return pl.pallas_call(
        dense_kernel,
        out_shape=jax.ShapeDtypeStruct((rows, cols), BF16),
        in_specs=[SMEM, SMEM, VMEM],
        out_specs=VMEM,
        compiler_params=PARAMS,
        name="dense_block",
    )(slots, count, tiles)


def backward_kernel(adj_ref, cot_ref, out_ref):
    out_ref[...] = lax.dot_general(
        adj_ref[...], cot_ref[...], (((0,), (0,)), ((), ())), preferred_element_type=F32
    ).astype(BF16)


def backward(adj, cot):
    return pl.pallas_call(
        backward_kernel,
        out_shape=jax.ShapeDtypeStruct((adj.shape[1], cot.shape[1]), BF16),
        in_specs=[VMEM, VMEM],
        out_specs=VMEM,
        compiler_params=PARAMS,
        name="backward",
    )(adj, cot)


def forward_kernel(me_ref, adj_ref, cot_ref, *refs):
    *shards, part_ref, grad_ref, column = refs
    slab = shards[0].shape[0]
    for k, shard in enumerate(shards):
        owner = lax.rem(me_ref[0] + len(shards) - k, len(shards))
        column[pl.ds(pl.multiple_of(owner * slab, slab), slab), :] = shard[...]
    part = jnp.dot(adj_ref[...], column[...], preferred_element_type=F32).astype(BF16)
    part_ref[...] = part
    grad_ref[...] = lax.dot_general(
        part, cot_ref[...], (((0,), (0,)), ((), ())), preferred_element_type=F32
    ).astype(BF16)


def forward(me, adj, cot, shards):
    width = cot.shape[1]
    return pl.pallas_call(
        forward_kernel,
        out_shape=(
            jax.ShapeDtypeStruct((adj.shape[0], width), BF16),
            jax.ShapeDtypeStruct((width, width), BF16),
        ),
        in_specs=[SMEM] + [VMEM] * (2 + len(shards)),
        out_specs=(VMEM, VMEM),
        scratch_shapes=[pltpu.VMEM((adj.shape[1], width), BF16)],
        compiler_params=PARAMS,
        name="forward",
    )(me, adj, cot, *shards)


def body(features, weight, tile_values, tile_slots, tile_counts, cotangent):
    row_devices = lax.axis_size("row")
    col_devices = lax.axis_size("col")
    devices = row_devices * col_devices
    slab, width = features.shape[1:]
    rows, cols = col_devices * slab, row_devices * slab
    me = lax.axis_index("row").astype(jnp.int32).reshape(1)

    own = features[0]
    shards = [own] + [
        lax.ppermute(own, "row", [(i, (i + k) % row_devices) for i in range(row_devices)])
        for k in range(1, row_devices)
    ]
    cot_block = lax.all_gather(cotangent[0], "col", axis=0, tiled=True)
    adj = dense_block(tile_values[0, 0], tile_slots[0, 0], tile_counts[0], rows, cols)
    column_part = backward(adj, cot_block).reshape(row_devices, slab, width)
    column_terms = lax.all_to_all(column_part, "row", 0, 0, tiled=True)

    part, grad = forward(me, adj, cot_block, shards)
    grad_shape = (
        (devices, width // devices, width)
        if width % devices == 0
        else (devices, 1, width * width // devices)
    )
    grad_terms = lax.all_to_all(grad.reshape(grad_shape), ("row", "col"), 0, 0, tiled=True)
    row_terms = lax.all_to_all(
        part.reshape(col_devices, slab, width), "col", 0, 0, tiled=True
    )

    grad_chunk = jnp.sum(grad_terms.astype(F32), axis=0) * (1.0 / math.sqrt(devices * slab))
    grad_all = lax.all_to_all(
        jnp.broadcast_to(grad_chunk.astype(BF16)[None], grad_shape),
        ("row", "col"), 0, 0, tiled=True,
    )
    weight_grad = grad_all.astype(F32).reshape(width, width)

    aggregated = jnp.sum(row_terms.astype(F32), axis=0).astype(BF16)
    layer_out = jnp.dot(aggregated, weight, preferred_element_type=F32).astype(BF16)
    column_sum = jnp.sum(column_terms.astype(F32), axis=0).astype(BF16)
    feature_grad = jnp.dot(column_sum, weight.T, preferred_element_type=F32).astype(BF16)
    return (layer_out[None], feature_grad[None], weight_grad)


def solution(mesh):
    placed = (
        P("col", "row", None),
        P(),
        P("row", "col", None, None, None),
        P("row", "col", None),
        P("row", "col"),
        P("row", "col", None),
    )
    return jax.shard_map(
        body,
        mesh=mesh,
        in_specs=placed,
        out_specs=(P("row", "col", None), P("col", "row", None), P()),
        check_vma=False,
    )
```

```python
import math

import jax
import jax.numpy as jnp
from jax import lax
from jax.experimental import pallas as pl
from jax.experimental.pallas import tpu as pltpu
from jax.sharding import PartitionSpec as P

F32 = jnp.float32
BF16 = jnp.bfloat16
VMEM = pl.BlockSpec(memory_space=pltpu.VMEM)
SMEM = pl.BlockSpec(memory_space=pltpu.SMEM)


def params(rows, cols):
    return pltpu.CompilerParams(vmem_limit_bytes=min(8 * 2**20 + 6 * rows * cols, 56 * 2**20))


def shape(*dims, dtype=BF16):
    return jax.ShapeDtypeStruct(dims, dtype)


def rows_of(index, slab):
    return pl.ds(pl.multiple_of(index * slab, slab), slab)


def backward_kernel(me_ref, slots_ref, count_ref, tiles_ref, *refs):
    *cot_refs, adj_ref, cot_ref, keep_ref, send_ref, total = refs
    slot_count, tile, _ = tiles_ref.shape
    half, slab, _ = keep_ref.shape
    col_tiles = adj_ref.shape[1] // tile
    adj_ref[...] = jnp.zeros_like(adj_ref)

    def place(k, carry):
        slot = slots_ref[k]
        row = pl.multiple_of((slot // col_tiles) * tile, tile)
        col = pl.multiple_of((slot % col_tiles) * tile, tile)
        adj_ref[pl.ds(row, tile), pl.ds(col, tile)] = tiles_ref[k]
        return carry

    lax.fori_loop(0, jnp.minimum(count_ref[0], slot_count), place, 0)
    for k, ref in enumerate(cot_refs):
        cot_ref[rows_of(me_ref[1] ^ k, slab), :] = ref[...]
    total[...] = lax.dot_general(
        adj_ref[...], cot_ref[...], (((0,), (0,)), ((), ())), preferred_element_type=F32
    ).astype(BF16)
    side = me_ref[0] & 1
    for m in range(half):
        keep_ref[m] = total[rows_of(2 * m + side, slab), :]
        send_ref[m] = total[rows_of(2 * m + 1 - side, slab), :]


def pair_sum_kernel(me_ref, keep_ref, got_ref, *chunk_refs):
    for k, ref in enumerate(chunk_refs):
        m = (me_ref[0] >> 1) ^ k
        ref[...] = (keep_ref[m].astype(F32) + got_ref[m].astype(F32)).astype(BF16)


def forward_kernel(me_ref, adj_ref, column_ref, cot_ref, *refs):
    *chunk_refs, grad_ref, total = refs
    slab = chunk_refs[0].shape[0]
    part = jnp.dot(adj_ref[...], column_ref[...], preferred_element_type=F32).astype(BF16)
    total[...] = part
    grad_ref[...] = lax.dot_general(
        part, cot_ref[...], (((0,), (0,)), ((), ())), preferred_element_type=F32
    ).astype(BF16)
    for k, ref in enumerate(chunk_refs):
        ref[...] = total[rows_of(me_ref[1] ^ k, slab), :]


def grad_sum_kernel(terms_ref, *refs, scale):
    out_ref = refs[-1]
    total = jnp.sum(terms_ref[...].astype(F32), axis=0) * scale
    out_ref[...] = jnp.broadcast_to(total.astype(BF16)[None], out_ref.shape)


def product_kernel(weight_ref, *refs, contract):
    *term_refs, out_ref = refs
    total = term_refs[0][...].astype(F32)
    for ref in term_refs[1:]:
        total = total + ref[...].astype(F32)
    out_ref[...] = lax.dot_general(
        total.astype(BF16),
        weight_ref[...],
        (((1,), (contract,)), ((), ())),
        preferred_element_type=F32,
    ).astype(BF16)


def summed_product(weight, terms, contract, name, compiler_params):
    return pl.pallas_call(
        lambda *refs: product_kernel(*refs, contract=contract),
        out_shape=shape(*terms[0].shape),
        in_specs=[VMEM] * (1 + len(terms)),
        out_specs=VMEM,
        compiler_params=compiler_params,
        name=name,
    )(weight, *terms)


def swap(array, axis, distance):
    pairs = [(i, i ^ distance) for i in range(lax.axis_size(axis))]
    return lax.ppermute(array, axis, pairs)


def exchange(chunks, axis, stride=1):
    return [chunks[0]] + [swap(chunks[k], axis, k * stride) for k in range(1, len(chunks))]


def body(features, weight, tile_values, tile_slots, tile_counts, cotangent):
    row_devices = lax.axis_size("row")
    col_devices = lax.axis_size("col")
    devices = row_devices * col_devices
    slab, width = features.shape[1:]
    rows, cols = col_devices * slab, row_devices * slab
    limits = params(rows, cols)
    me = jnp.stack([lax.axis_index("row"), lax.axis_index("col")]).astype(jnp.int32)

    column = lax.all_to_all(
        jnp.broadcast_to(features, (row_devices, slab, width)), "row", 0, 0, tiled=True
    ).reshape(cols, width)
    cots = exchange([cotangent[0]] * col_devices, "col")

    half = row_devices // 2
    adj, cot_block, keep, send = pl.pallas_call(
        backward_kernel,
        out_shape=[shape(rows, cols), shape(rows, width)] + [shape(half, slab, width)] * 2,
        in_specs=[SMEM] * 3 + [VMEM] * (1 + col_devices),
        out_specs=[VMEM] * 4,
        scratch_shapes=[pltpu.VMEM((cols, width), BF16)],
        compiler_params=limits,
        name="backward",
    )(me, tile_slots[0, 0], tile_counts[0], tile_values[0, 0], *cots)
    column_chunks = pl.pallas_call(
        pair_sum_kernel,
        out_shape=[shape(slab, width)] * half,
        in_specs=[SMEM, VMEM, VMEM],
        out_specs=[VMEM] * half,
        compiler_params=limits,
        name="pair_sum",
    )(me, keep, swap(send, "row", 1))
    column_terms = exchange(column_chunks, "row", 2)

    *row_chunks, grad = pl.pallas_call(
        forward_kernel,
        out_shape=[shape(slab, width)] * col_devices + [shape(width, width)],
        in_specs=[SMEM] + [VMEM] * 3,
        out_specs=[VMEM] * (col_devices + 1),
        scratch_shapes=[pltpu.VMEM((rows, width), BF16)],
        compiler_params=limits,
        name="forward",
    )(me, adj, column, cot_block)
    row_terms = exchange(row_chunks, "col")

    chunk_shape = (
        (width // devices, width) if width % devices == 0 else (1, width * width // devices)
    )
    grad_terms = lax.all_to_all(
        grad.reshape(devices, *chunk_shape), ("row", "col"), 0, 0, tiled=True
    )
    scale = 1.0 / math.sqrt(devices * slab)
    grad_chunks = pl.pallas_call(
        lambda *refs: grad_sum_kernel(*refs, scale=scale),
        out_shape=shape(devices, *chunk_shape),
        in_specs=[VMEM] + [pl.BlockSpec(memory_space=pl.ANY)] * half,
        out_specs=VMEM,
        compiler_params=limits,
        name="grad_sum",
    )(grad_terms, *column_chunks)
    grad_all = lax.all_to_all(grad_chunks, ("row", "col"), 0, 0, tiled=True)
    weight_grad = grad_all.astype(F32).reshape(width, width)

    layer_out = summed_product(weight, row_terms, 0, "layer_out", limits)
    feature_grad = summed_product(weight, column_terms, 1, "feature_grad", limits)
    return (layer_out[None], feature_grad[None], weight_grad)


def solution(mesh):
    placed = (
        P("col", "row", None),
        P(),
        P("row", "col", None, None, None),
        P("row", "col", None),
        P("row", "col"),
        P("row", "col", None),
    )
    return jax.shard_map(
        body,
        mesh=mesh,
        in_specs=placed,
        out_specs=(P("row", "col", None), P("col", "row", None), P()),
        check_vma=False,
    )
```

```python
import math

import jax
import jax.numpy as jnp
from jax import lax
from jax.experimental import pallas as pl
from jax.experimental.pallas import tpu as pltpu
from jax.sharding import PartitionSpec as P

F32 = jnp.float32
BF16 = jnp.bfloat16
VMEM = pl.BlockSpec(memory_space=pltpu.VMEM)
SMEM = pl.BlockSpec(memory_space=pltpu.SMEM)


def params(rows, cols):
    return pltpu.CompilerParams(vmem_limit_bytes=min(8 * 2**20 + 6 * rows * cols, 56 * 2**20))


def hint(microseconds):
    return pl.CostEstimate(
        flops=int(microseconds * 1e9), bytes_accessed=int(microseconds * 3.6e6), transcendentals=0
    )


def shape(*dims, dtype=BF16):
    return jax.ShapeDtypeStruct(dims, dtype)


def rows_of(index, slab):
    return pl.ds(pl.multiple_of(index * slab, slab), slab)


def backward_kernel(me_ref, slots_ref, count_ref, tiles_ref, *refs, col_devices):
    cot_refs, (adj_ref, cot_ref, *pair_refs, total) = refs[:col_devices], refs[col_devices:]
    slot_count, tile, _ = tiles_ref.shape
    half, slab = len(pair_refs), pair_refs[0].shape[1]
    col_tiles = adj_ref.shape[1] // tile
    adj_ref[...] = jnp.zeros_like(adj_ref)

    def place(k, carry):
        slot = slots_ref[k]
        row = pl.multiple_of((slot // col_tiles) * tile, tile)
        col = pl.multiple_of((slot % col_tiles) * tile, tile)
        adj_ref[pl.ds(row, tile), pl.ds(col, tile)] = tiles_ref[k]
        return carry

    lax.fori_loop(0, jnp.minimum(count_ref[0], slot_count), place, 0)
    for k, ref in enumerate(cot_refs):
        cot_ref[rows_of(me_ref[1] ^ k, slab), :] = ref[...]
    total[...] = lax.dot_general(
        adj_ref[...], cot_ref[...], (((0,), (0,)), ((), ())), preferred_element_type=F32
    ).astype(BF16)
    for k, ref in enumerate(pair_refs):
        ref[0] = total[rows_of(me_ref[0] ^ k, slab), :]
        ref[1] = total[rows_of(me_ref[0] ^ k ^ half, slab), :]


def forward_kernel(me_ref, adj_ref, cot_ref, *refs, half):
    pair_refs, (grad_ref, *chunk_refs, column, total) = refs[:half], refs[half:]
    slab = chunk_refs[0].shape[0]
    for k, ref in enumerate(pair_refs):
        column[rows_of(me_ref[0] ^ k, slab), :] = ref[0]
        column[rows_of(me_ref[0] ^ k ^ half, slab), :] = ref[1]
    part = jnp.dot(adj_ref[...], column[...], preferred_element_type=F32).astype(BF16)
    total[...] = part
    grad_ref[...] = lax.dot_general(
        part, cot_ref[...], (((0,), (0,)), ((), ())), preferred_element_type=F32
    ).astype(BF16)
    for k, ref in enumerate(chunk_refs):
        ref[...] = total[rows_of(me_ref[1] ^ k, slab), :]


def pair_sum_kernel(*refs):
    *pair_refs, keep_ref, send_ref = refs
    total = pair_refs[0][...].astype(F32)
    for ref in pair_refs[1:]:
        total = total + ref[...].astype(F32)
    keep_ref[...] = total[0]
    send_ref[...] = total[1].astype(BF16)


def grad_sum_kernel(terms_ref, *refs, scale):
    out_ref = refs[-1]
    total = jnp.sum(terms_ref[...].astype(F32), axis=0) * scale
    out_ref[...] = jnp.broadcast_to(total.astype(BF16)[None], out_ref.shape)


def product_kernel(weight_ref, *refs, contract):
    *term_refs, out_ref = refs
    total = term_refs[0][...].astype(F32)
    for ref in term_refs[1:]:
        total = total + ref[...].astype(F32)
    out_ref[...] = lax.dot_general(
        total.astype(BF16),
        weight_ref[...],
        (((1,), (contract,)), ((), ())),
        preferred_element_type=F32,
    ).astype(BF16)


def summed_product(weight, terms, contract, name, compiler_params):
    return pl.pallas_call(
        lambda *refs: product_kernel(*refs, contract=contract),
        out_shape=shape(*terms[0].shape),
        in_specs=[VMEM] * (1 + len(terms)),
        out_specs=VMEM,
        compiler_params=compiler_params,
        name=name,
    )(weight, *terms)


def swap(array, axis, distance):
    pairs = [(i, i ^ distance) for i in range(lax.axis_size(axis))]
    return lax.ppermute(array, axis, pairs)


def exchange(chunks, axis, stride=1):
    return [chunks[0]] + [swap(chunks[k], axis, k * stride) for k in range(1, len(chunks))]


def body(features, weight, tile_values, tile_slots, tile_counts, cotangent):
    row_devices = lax.axis_size("row")
    col_devices = lax.axis_size("col")
    devices = row_devices * col_devices
    slab, width = features.shape[1:]
    rows, cols = col_devices * slab, row_devices * slab
    limits = params(rows, cols)
    me = jnp.stack([lax.axis_index("row"), lax.axis_index("col")]).astype(jnp.int32)

    half = row_devices // 2
    own = features[0]
    far = swap(own, "row", half)
    cots = exchange([cotangent[0]] * col_devices, "col")
    features_got = exchange([jnp.stack([own, far])] * half, "row")

    adj, cot_block, *column_pairs = pl.pallas_call(
        lambda *refs: backward_kernel(*refs, col_devices=col_devices),
        out_shape=[shape(rows, cols), shape(rows, width)] + [shape(2, slab, width)] * half,
        in_specs=[SMEM] * 3 + [VMEM] * (1 + col_devices),
        out_specs=[VMEM] * (2 + half),
        scratch_shapes=[pltpu.VMEM((cols, width), BF16)],
        compiler_params=limits,
        name="backward",
    )(me, tile_slots[0, 0], tile_counts[0], tile_values[0, 0], *cots)
    column_got = exchange(column_pairs, "row")
    column_keep, column_send = pl.pallas_call(
        pair_sum_kernel,
        out_shape=[shape(slab, width, dtype=F32), shape(slab, width)],
        in_specs=[VMEM] * half,
        out_specs=[VMEM] * 2,
        compiler_params=limits,
        cost_estimate=hint(20),
        name="pair_sum",
    )(*column_got)
    grad, *row_chunks = pl.pallas_call(
        lambda *refs: forward_kernel(*refs, half=half),
        out_shape=[shape(width, width)] + [shape(slab, width)] * col_devices,
        in_specs=[SMEM] + [VMEM] * (2 + half),
        out_specs=[VMEM] * (1 + col_devices),
        scratch_shapes=[pltpu.VMEM((cols, width), BF16), pltpu.VMEM((rows, width), BF16)],
        compiler_params=limits,
        name="forward",
    )(me, adj, cot_block, *features_got)
    column_terms = [column_keep, swap(column_send, "row", half)]
    row_terms = exchange(row_chunks, "col")

    chunk_shape = (
        (width // devices, width) if width % devices == 0 else (1, width * width // devices)
    )
    grad_terms = lax.all_to_all(
        grad.reshape(devices, *chunk_shape), ("row", "col"), 0, 0, tiled=True
    )
    scale = 1.0 / math.sqrt(devices * slab)
    grad_chunks = pl.pallas_call(
        lambda *refs: grad_sum_kernel(*refs, scale=scale),
        out_shape=shape(devices, *chunk_shape),
        in_specs=[VMEM] + [pl.BlockSpec(memory_space=pl.ANY)],
        out_specs=VMEM,
        compiler_params=limits,
        name="grad_sum",
    )(grad_terms, column_send)
    grad_all = lax.all_to_all(grad_chunks, ("row", "col"), 0, 0, tiled=True)
    weight_grad = grad_all.astype(F32).reshape(width, width)

    layer_out = summed_product(weight, row_terms, 0, "layer_out", limits)
    feature_grad = summed_product(weight, column_terms, 1, "feature_grad", limits)
    return (layer_out[None], feature_grad[None], weight_grad)


def solution(mesh):
    placed = (
        P("col", "row", None),
        P(),
        P("row", "col", None, None, None),
        P("row", "col", None),
        P("row", "col"),
        P("row", "col", None),
    )
    return jax.shard_map(
        body,
        mesh=mesh,
        in_specs=placed,
        out_specs=(P("row", "col", None), P("col", "row", None), P()),
        check_vma=False,
    )
```

```python
import math

import jax
import jax.numpy as jnp
from jax import lax
from jax.experimental import pallas as pl
from jax.experimental.pallas import tpu as pltpu
from jax.sharding import PartitionSpec as P

F32 = jnp.float32
BF16 = jnp.bfloat16
VMEM = pl.BlockSpec(memory_space=pltpu.VMEM)
SMEM = pl.BlockSpec(memory_space=pltpu.SMEM)
ANY = pl.BlockSpec(memory_space=pl.ANY)


def hint(microseconds):
    return pl.CostEstimate(
        flops=int(microseconds * 1e9), bytes_accessed=int(microseconds * 3.6e6), transcendentals=0
    )


def shape(*dims, dtype=BF16):
    return jax.ShapeDtypeStruct(dims, dtype)


def rows_of(index, slab):
    return pl.ds(pl.multiple_of(index * slab, slab), slab)


def summed(refs):
    total = refs[0][...].astype(F32)
    for ref in refs[1:]:
        total = total + ref[...].astype(F32)
    return total


def dense_kernel(slots_ref, count_ref, tiles_ref, adj_ref, sems):
    slot_count, tile, _ = tiles_ref.shape
    col_tiles = adj_ref.shape[1] // tile
    live = jnp.minimum(count_ref[0], slot_count)
    adj_ref[...] = jnp.zeros_like(adj_ref)

    def copy(k):
        slot = slots_ref[k]
        row = pl.multiple_of((slot // col_tiles) * tile, tile)
        col = pl.multiple_of((slot % col_tiles) * tile, tile)
        place = adj_ref.at[pl.ds(row, tile), pl.ds(col, tile)]
        return pltpu.make_async_copy(tiles_ref.at[k], place, sems.at[k])

    def start(k, carry):
        copy(k).start()
        return carry

    def wait(k, carry):
        copy(k).wait()
        return carry

    lax.fori_loop(0, live, start, 0)
    lax.fori_loop(0, live, wait, 0)


def stack_kernel(own_ref, far_ref, _, pair_ref):
    pair_ref[0] = own_ref[...]
    pair_ref[1] = far_ref[...]


def backward_kernel(me_ref, adj_ref, *refs, col_devices):
    cot_refs, (cot_ref, *pair_refs, total) = refs[:col_devices], refs[col_devices:]
    half, slab = len(pair_refs), pair_refs[0].shape[1]
    for k, ref in enumerate(cot_refs):
        cot_ref[rows_of(me_ref[1] ^ k, slab), :] = ref[...]
    total[...] = lax.dot_general(
        adj_ref[...], cot_ref[...], (((0,), (0,)), ((), ())), preferred_element_type=F32
    ).astype(BF16)
    for k, ref in enumerate(pair_refs):
        ref[0] = total[rows_of(me_ref[0] ^ k, slab), :]
        ref[1] = total[rows_of(me_ref[0] ^ k ^ half, slab), :]


def forward_kernel(me_ref, adj_ref, cot_ref, *refs, half):
    pair_refs, (*chunk_refs, column, part, grad) = refs[:half], refs[half:]
    slab = pair_refs[0].shape[1]
    piece = chunk_refs[0].shape[0] - slab
    for k, ref in enumerate(pair_refs):
        column[rows_of(me_ref[0] ^ k, slab), :] = ref[0]
        column[rows_of(me_ref[0] ^ k ^ half, slab), :] = ref[1]
    product = jnp.dot(adj_ref[...], column[...], preferred_element_type=F32).astype(BF16)
    part[...] = product
    grad[...] = lax.dot_general(
        product, cot_ref[...], (((0,), (0,)), ((), ())), preferred_element_type=F32
    ).astype(BF16)
    for k, ref in enumerate(chunk_refs):
        ref[:slab, :] = part[rows_of(me_ref[1] ^ k, slab), :]
        ref[slab:, :] = grad[rows_of(me_ref[1] ^ k, piece), :]


def pair_sum_kernel(*refs):
    *pair_refs, keep_ref, send_ref = refs
    total = summed(pair_refs)
    keep_ref[...] = total[0]
    send_ref[...] = total[1].astype(BF16)


def output_kernel(weight_ref, *refs):
    *chunk_refs, out_ref, piece_ref = refs
    slab = out_ref.shape[0]
    total = summed(chunk_refs).astype(BF16)
    piece_ref[...] = total[slab:]
    out_ref[...] = jnp.dot(
        total[:slab], weight_ref[...], preferred_element_type=F32
    ).astype(BF16)


def feature_kernel(weight_ref, keep_ref, got_ref, out_ref):
    total = summed([keep_ref, got_ref]).astype(BF16)
    out_ref[...] = lax.dot_general(
        total, weight_ref[...], (((1,), (1,)), ((), ())), preferred_element_type=F32
    ).astype(BF16)


def sum_kernel(*refs, terms):
    refs[-1][...] = summed(refs[:terms]).astype(BF16)


def gather_kernel(me_ref, *refs, scale):
    *piece_refs, out_ref = refs
    piece = piece_refs[0].shape[0]
    for k, ref in enumerate(piece_refs):
        out_ref[rows_of(me_ref[1] ^ k, piece), :] = ref[...].astype(F32) * scale


def swap(array, axis, distance):
    pairs = [(i, i ^ distance) for i in range(lax.axis_size(axis))]
    return lax.ppermute(array, axis, pairs)


def exchange(chunks, axis):
    return [chunks[0]] + [swap(chunks[k], axis, k) for k in range(1, len(chunks))]


def body(features, weight, tile_values, tile_slots, tile_counts, cotangent):
    row_devices = lax.axis_size("row")
    col_devices = lax.axis_size("col")
    half = row_devices // 2
    slots, tile = tile_values.shape[2:4]
    slab, width = features.shape[1:]
    rows, cols = col_devices * slab, row_devices * slab
    piece = width // col_devices
    me = jnp.stack([lax.axis_index("row"), lax.axis_index("col")]).astype(jnp.int32)

    def call(kernel, name, out_shape, in_specs, args, scratch=(), micros=None):
        many = isinstance(out_shape, list)
        return pl.pallas_call(
            kernel,
            out_shape=out_shape,
            in_specs=in_specs,
            out_specs=[VMEM] * len(out_shape) if many else VMEM,
            scratch_shapes=scratch,
            compiler_params=pltpu.CompilerParams(
                vmem_limit_bytes=min(8 * 2**20 + 6 * rows * cols, 56 * 2**20)
            ),
            cost_estimate=None if micros is None else hint(micros),
            name=name,
        )(*args)

    own = features[0]
    cots = exchange([cotangent[0]] * col_devices, "col")
    far = swap(own, "row", half)
    adj = call(
        dense_kernel, "dense", shape(rows, cols), [SMEM, SMEM, ANY],
        (tile_slots[0, 0], tile_counts[0], tile_values[0, 0]),
        scratch=[pltpu.SemaphoreType.DMA((slots,))],
    )
    pair = call(
        stack_kernel, "stack", shape(2, slab, width), [VMEM, VMEM, ANY], (own, far, adj)
    )
    features_got = exchange([pair] * half, "row")

    cot_block, *column_pairs = call(
        lambda *refs: backward_kernel(*refs, col_devices=col_devices), "backward",
        [shape(rows, width)] + [shape(2, slab, width)] * half,
        [SMEM] + [VMEM] * (1 + col_devices), (me, adj, *cots),
        scratch=[pltpu.VMEM((cols, width), BF16)],
    )
    column_got = exchange(column_pairs, "row")
    column_keep, column_send = call(
        pair_sum_kernel, "pair_sum", [shape(slab, width, dtype=F32), shape(slab, width)],
        [VMEM] * half, column_got, micros=20,
    )
    column_far = swap(column_send, "row", half)

    chunks = call(
        lambda *refs: forward_kernel(*refs, half=half), "forward",
        [shape(slab + piece, width)] * col_devices,
        [SMEM] + [VMEM] * (2 + half), (me, adj, cot_block, *features_got),
        scratch=[
            pltpu.VMEM((cols, width), BF16),
            pltpu.VMEM((rows, width), BF16),
            pltpu.VMEM((width, width), BF16),
        ],
    )
    layer_out, grad_col = call(
        output_kernel, "layer_out", [shape(slab, width), shape(piece, width)],
        [VMEM] * (1 + col_devices), (weight, *exchange(chunks, "col")),
    )
    grad_near = call(
        lambda *refs: sum_kernel(*refs, terms=half), "grad_near", shape(piece, width),
        [VMEM] * half + [ANY], (*exchange([grad_col] * half, "row"), column_far),
    )
    grad_row = call(
        lambda *refs: sum_kernel(*refs, terms=2), "grad_row", shape(piece, width),
        [VMEM] * 2, (grad_near, swap(grad_near, "row", half)),
    )
    scale = 1.0 / math.sqrt(row_devices * col_devices * slab)
    weight_grad = call(
        lambda *refs: gather_kernel(*refs, scale=scale), "weight_grad",
        shape(width, width, dtype=F32),
        [SMEM] + [VMEM] * col_devices, (me, *exchange([grad_row] * col_devices, "col")),
    )
    feature_grad = call(
        feature_kernel, "feature_grad", shape(slab, width), [VMEM] * 3,
        (weight, column_keep, column_far),
    )
    return (layer_out[None], feature_grad[None], weight_grad)


def solution(mesh):
    placed = (
        P("col", "row", None),
        P(),
        P("row", "col", None, None, None),
        P("row", "col", None),
        P("row", "col"),
        P("row", "col", None),
    )
    return jax.shard_map(
        body,
        mesh=mesh,
        in_specs=placed,
        out_specs=(P("row", "col", None), P("col", "row", None), P()),
        check_vma=False,
    )
```

```python
import math

import jax
import jax.numpy as jnp
from jax import lax
from jax.experimental import pallas as pl
from jax.experimental.pallas import tpu as pltpu
from jax.sharding import PartitionSpec as P

F32 = jnp.float32
BF16 = jnp.bfloat16
VMEM = pl.BlockSpec(memory_space=pltpu.VMEM)
SMEM = pl.BlockSpec(memory_space=pltpu.SMEM)
ANY = pl.BlockSpec(memory_space=pl.ANY)


def hint(microseconds):
    return pl.CostEstimate(
        flops=int(microseconds * 1e9), bytes_accessed=int(microseconds * 3.6e6), transcendentals=0
    )


def shape(*dims, dtype=BF16):
    return jax.ShapeDtypeStruct(dims, dtype)


def rows_of(index, slab):
    return pl.ds(pl.multiple_of(index * slab, slab), slab)


def summed(refs):
    total = refs[0][...].astype(F32)
    for ref in refs[1:]:
        total = total + ref[...].astype(F32)
    return total


def dense_kernel(slots_ref, count_ref, tiles_ref, adj_ref, sems):
    slot_count, tile, _ = tiles_ref.shape
    col_tiles = adj_ref.shape[1] // tile
    live = jnp.minimum(count_ref[0], slot_count)
    adj_ref[...] = jnp.zeros_like(adj_ref)

    def copy(k):
        slot = slots_ref[k]
        row = pl.multiple_of((slot // col_tiles) * tile, tile)
        col = pl.multiple_of((slot % col_tiles) * tile, tile)
        place = adj_ref.at[pl.ds(row, tile), pl.ds(col, tile)]
        return pltpu.make_async_copy(tiles_ref.at[k], place, sems.at[k])

    def start(k, carry):
        copy(k).start()
        return carry

    def wait(k, carry):
        copy(k).wait()
        return carry

    lax.fori_loop(0, live, start, 0)
    lax.fori_loop(0, live, wait, 0)


def stack_kernel(*refs):
    out_ref = refs[-1]
    for k in range(out_ref.shape[0]):
        out_ref[k] = refs[k][...]


def forward_kernel(me_ref, adj_ref, near_ref, other_ref, *refs, half):
    pair_refs, refs = refs[:half], refs[half:]
    grad_ref, cot_ref, *chunk_refs, column, part = refs
    slab = pair_refs[0].shape[1]
    for k in range(near_ref.shape[0]):
        cot_ref[rows_of(me_ref[1] ^ (2 * k), slab), :] = near_ref[k]
        cot_ref[rows_of(me_ref[1] ^ (2 * k + 1), slab), :] = other_ref[k]
    for k, ref in enumerate(pair_refs):
        column[rows_of(me_ref[0] ^ k, slab), :] = ref[0]
        column[rows_of(me_ref[0] ^ k ^ half, slab), :] = ref[1]
    product = jnp.dot(adj_ref[...], column[...], preferred_element_type=F32).astype(BF16)
    part[...] = product
    grad_ref[...] = lax.dot_general(
        product, cot_ref[...], (((0,), (0,)), ((), ())), preferred_element_type=F32
    ).astype(BF16)
    for k, ref in enumerate(chunk_refs):
        ref[...] = part[rows_of(me_ref[1] ^ k, slab), :]


def backward_kernel(me_ref, adj_ref, cot_ref, *refs):
    *pair_refs, total = refs
    half, slab = len(pair_refs), pair_refs[0].shape[1]
    total[...] = lax.dot_general(
        adj_ref[...], cot_ref[...], (((0,), (0,)), ((), ())), preferred_element_type=F32
    ).astype(BF16)
    for k, ref in enumerate(pair_refs):
        ref[0] = total[rows_of(me_ref[0] ^ k, slab), :]
        ref[1] = total[rows_of(me_ref[0] ^ k ^ half, slab), :]


def pair_sum_kernel(*refs):
    *pair_refs, keep_ref, send_ref = refs
    total = summed(pair_refs)
    keep_ref[...] = total[0]
    send_ref[...] = total[1].astype(BF16)


def product_kernel(weight_ref, *refs, contract):
    *term_refs, out_ref = refs
    out_ref[...] = lax.dot_general(
        summed(term_refs).astype(BF16),
        weight_ref[...],
        (((1,), (contract,)), ((), ())),
        preferred_element_type=F32,
    ).astype(BF16)


def grad_sum_kernel(terms_ref, *refs, scale):
    out_ref = refs[-1]
    total = jnp.sum(terms_ref[...].astype(F32), axis=0) * scale
    out_ref[...] = jnp.broadcast_to(total.astype(BF16)[None], out_ref.shape)


def swap(array, axis, distance):
    pairs = [(i, i ^ distance) for i in range(lax.axis_size(axis))]
    return lax.ppermute(array, axis, pairs)


def exchange(chunks, axis, stride=1):
    return [chunks[0]] + [swap(chunks[k], axis, k * stride) for k in range(1, len(chunks))]


def body(features, weight, tile_values, tile_slots, tile_counts, cotangent):
    row_devices = lax.axis_size("row")
    col_devices = lax.axis_size("col")
    half = row_devices // 2
    slots, tile = tile_values.shape[2:4]
    slab, width = features.shape[1:]
    rows, cols = col_devices * slab, row_devices * slab
    me = jnp.stack([lax.axis_index("row"), lax.axis_index("col")]).astype(jnp.int32)

    def call(kernel, name, out_shape, in_specs, args, scratch=(), micros=None):
        many = isinstance(out_shape, list)
        return pl.pallas_call(
            kernel,
            out_shape=out_shape,
            in_specs=in_specs,
            out_specs=[VMEM] * len(out_shape) if many else VMEM,
            scratch_shapes=scratch,
            compiler_params=pltpu.CompilerParams(
                vmem_limit_bytes=min(8 * 2**20 + 6 * rows * cols, 56 * 2**20)
            ),
            cost_estimate=None if micros is None else hint(micros),
            name=name,
        )(*args)

    own = features[0]
    far = swap(own, "row", half)
    adj = call(
        dense_kernel, "dense", shape(rows, cols), [SMEM, SMEM, ANY],
        (tile_slots[0, 0], tile_counts[0], tile_values[0, 0]),
        scratch=[pltpu.SemaphoreType.DMA((slots,))],
    )

    def stack(arrays, name, after=()):
        return call(
            stack_kernel, name, shape(len(arrays), slab, width),
            [VMEM] * len(arrays) + [ANY] * len(after), (*arrays, *after),
        )

    pair = stack([stack([own], "own").reshape(own.shape), far], "pair")
    features_got = exchange([pair] * half, "row")
    cot_near = stack(exchange([cotangent[0]] * (col_devices // 2), "col", 2), "cot_near", [pair])
    cot_other = swap(cot_near, "col", 1)

    grad, cot_block, *chunks = call(
        lambda *refs: forward_kernel(*refs, half=half), "forward",
        [shape(width, width), shape(rows, width)] + [shape(slab, width)] * col_devices,
        [SMEM] + [VMEM] * (3 + half), (me, adj, cot_near, cot_other, *features_got),
        scratch=[pltpu.VMEM((cols, width), BF16), pltpu.VMEM((rows, width), BF16)],
    )
    column_pairs = call(
        backward_kernel, "backward", [shape(2, slab, width)] * half,
        [SMEM, VMEM, VMEM], (me, adj, cot_block),
        scratch=[pltpu.VMEM((cols, width), BF16)],
    )
    column_got = exchange(column_pairs, "row")
    column_keep, column_send = call(
        pair_sum_kernel, "pair_sum", [shape(slab, width, dtype=F32), shape(slab, width)],
        [VMEM] * half, column_got, micros=12,
    )
    column_far = swap(column_send, "row", half)

    row_got = exchange(chunks, "col")
    devices = row_devices * col_devices
    chunk_shape = (
        (width // devices, width) if width % devices == 0 else (1, width * width // devices)
    )
    grad_terms = lax.all_to_all(
        grad.reshape(devices, *chunk_shape), ("row", "col"), 0, 0, tiled=True
    )
    scale = 1.0 / math.sqrt(devices * slab)
    after = []
    grad_chunks = call(
        lambda *refs: grad_sum_kernel(*refs, scale=scale), "grad_sum",
        shape(devices, *chunk_shape), [VMEM] + [ANY] * len(after), (grad_terms, *after),
    )
    grad_all = lax.all_to_all(grad_chunks, ("row", "col"), 0, 0, tiled=True)
    weight_grad = grad_all.astype(F32).reshape(width, width)
    layer_out = call(
        lambda *refs: product_kernel(*refs, contract=0), "layer_out", shape(slab, width),
        [VMEM] * (1 + col_devices), (weight, *row_got),
    )
    feature_grad = call(
        lambda *refs: product_kernel(*refs, contract=1), "feature_grad", shape(slab, width),
        [VMEM] * 3, (weight, column_keep, column_far),
    )
    return (layer_out[None], feature_grad[None], weight_grad)


def solution(mesh):
    placed = (
        P("col", "row", None),
        P(),
        P("row", "col", None, None, None),
        P("row", "col", None),
        P("row", "col"),
        P("row", "col", None),
    )
    return jax.shard_map(
        body,
        mesh=mesh,
        in_specs=placed,
        out_specs=(P("row", "col", None), P("col", "row", None), P()),
        check_vma=False,
    )
```

```python
import math

import jax
import jax.numpy as jnp
from jax import lax
from jax.experimental import pallas as pl
from jax.experimental.pallas import tpu as pltpu
from jax.sharding import PartitionSpec as P

F32 = jnp.float32
BF16 = jnp.bfloat16
VMEM = pl.BlockSpec(memory_space=pltpu.VMEM)
SMEM = pl.BlockSpec(memory_space=pltpu.SMEM)
ANY = pl.BlockSpec(memory_space=pl.ANY)


def hint(microseconds):
    return pl.CostEstimate(
        flops=int(microseconds * 1e9), bytes_accessed=int(microseconds * 3.6e6), transcendentals=0
    )


def shape(*dims, dtype=BF16):
    return jax.ShapeDtypeStruct(dims, dtype)


def rows_of(index, slab):
    return pl.ds(pl.multiple_of(index * slab, slab), slab)


def summed(refs):
    total = refs[0][...].astype(F32)
    for ref in refs[1:]:
        total = total + ref[...].astype(F32)
    return total


def dense_kernel(slots_ref, count_ref, tiles_ref, adj_ref, sems):
    slot_count, tile, _ = tiles_ref.shape
    col_tiles = adj_ref.shape[1] // tile
    live = jnp.minimum(count_ref[0], slot_count)
    adj_ref[...] = jnp.zeros_like(adj_ref)

    def copy(k):
        slot = slots_ref[k]
        row = pl.multiple_of((slot // col_tiles) * tile, tile)
        col = pl.multiple_of((slot % col_tiles) * tile, tile)
        place = adj_ref.at[pl.ds(row, tile), pl.ds(col, tile)]
        return pltpu.make_async_copy(tiles_ref.at[k], place, sems.at[k])

    def start(k, carry):
        copy(k).start()
        return carry

    def wait(k, carry):
        copy(k).wait()
        return carry

    lax.fori_loop(0, live, start, 0)
    lax.fori_loop(0, live, wait, 0)


def stack_kernel(*refs):
    out_ref = refs[-1]
    for k in range(out_ref.shape[0]):
        out_ref[k] = refs[k][...]


def place_cots(me_ref, near_ref, other_ref, out_ref):
    slab = near_ref.shape[1]
    for k in range(near_ref.shape[0]):
        out_ref[rows_of(me_ref[1] ^ (2 * k), slab), :] = near_ref[k]
        out_ref[rows_of(me_ref[1] ^ (2 * k + 1), slab), :] = other_ref[k]


def forward_kernel(me_ref, adj_ref, near_ref, other_ref, *refs, half):
    shard_refs, pair_refs, refs = refs[:4], refs[4 : 2 + half], refs[2 + half :]
    *out_refs, column, cots, part, grad = refs
    slab = shard_refs[0].shape[0]
    col_devices = len(out_refs) // 2
    place_cots(me_ref, near_ref, other_ref, cots)
    for distance, ref in zip((0, half, 1, half ^ 1), shard_refs):
        column[rows_of(me_ref[0] ^ distance, slab), :] = ref[...]
    for k, ref in enumerate(pair_refs, 2):
        column[rows_of(me_ref[0] ^ k, slab), :] = ref[0]
        column[rows_of(me_ref[0] ^ k ^ half, slab), :] = ref[1]
    product = jnp.dot(adj_ref[...], column[...], preferred_element_type=F32).astype(BF16)
    part[...] = product
    grad[...] = lax.dot_general(
        product, cots[...], (((0,), (0,)), ((), ())), preferred_element_type=F32
    ).astype(BF16)
    for k in range(col_devices):
        chunk_ref, piece_ref = out_refs[k], out_refs[col_devices + k]
        chunk_ref[...] = part[rows_of(me_ref[1] ^ k, slab), :]
        piece_ref[...] = grad[rows_of(me_ref[1] ^ k, piece_ref.shape[0]), :]


def backward_kernel(me_ref, adj_ref, near_ref, other_ref, _, keep_ref, *refs):
    *send_refs, cots, total = refs
    half, slab, _ = keep_ref.shape
    place_cots(me_ref, near_ref, other_ref, cots)
    total[...] = lax.dot_general(
        adj_ref[...], cots[...], (((0,), (0,)), ((), ())), preferred_element_type=F32
    ).astype(BF16)
    sends = [ref.at[m] for ref in send_refs for m in range(ref.shape[0])]
    for m in range(half):
        keep_ref[m] = total[rows_of(me_ref[0] ^ (2 * m), slab), :]
        sends[m][...] = total[rows_of(me_ref[0] ^ (2 * m + 1), slab), :]


def halve_kernel(held_ref, *refs):
    *got_refs, _, keep_ref, send_ref = refs
    got = [ref.at[m] for ref in got_refs for m in range(ref.shape[0])]
    for m in range(keep_ref.shape[0]):
        keep_ref[m] = summed([held_ref.at[2 * m], got[2 * m]]).astype(BF16)
        send_ref[m] = summed([held_ref.at[2 * m + 1], got[2 * m + 1]]).astype(BF16)


def product_kernel(weight_ref, *refs, contract):
    *term_refs, out_ref = refs
    out_ref[...] = lax.dot_general(
        summed(term_refs).astype(BF16),
        weight_ref[...],
        (((1,), (contract,)), ((), ())),
        preferred_element_type=F32,
    ).astype(BF16)


def sum_kernel(*refs, terms):
    refs[-1][...] = summed(refs[:terms]).astype(BF16)


def gather_kernel(me_ref, *refs, scale):
    *piece_refs, _, out_ref, held, sems = refs
    piece = piece_refs[0].shape[0]
    copies = []
    for k, ref in enumerate(piece_refs):
        held[k] = ref[...].astype(F32) * scale
        place = out_ref.at[rows_of(me_ref[1] ^ k, piece), :]
        copies.append(pltpu.make_async_copy(held.at[k], place, sems.at[k]))
        copies[k].start()
    for copy in copies:
        copy.wait()


def swap(array, axis, distance):
    pairs = [(i, i ^ distance) for i in range(lax.axis_size(axis))]
    return lax.ppermute(array, axis, pairs)


def exchange(chunks, axis, stride=1):
    return [chunks[0]] + [swap(chunks[k], axis, k * stride) for k in range(1, len(chunks))]


def body(features, weight, tile_values, tile_slots, tile_counts, cotangent):
    row_devices = lax.axis_size("row")
    col_devices = lax.axis_size("col")
    half = row_devices // 2
    slots, tile = tile_values.shape[2:4]
    slab, width = features.shape[1:]
    rows, cols = col_devices * slab, row_devices * slab
    piece = width // col_devices
    me = jnp.stack([lax.axis_index("row"), lax.axis_index("col")]).astype(jnp.int32)

    def call(kernel, name, out_shape, in_specs, args, scratch=(), micros=None, out_space=VMEM):
        many = isinstance(out_shape, list)
        return pl.pallas_call(
            kernel,
            out_shape=out_shape,
            in_specs=in_specs,
            out_specs=[VMEM] * len(out_shape) if many else out_space,
            scratch_shapes=scratch,
            compiler_params=pltpu.CompilerParams(
                vmem_limit_bytes=min(8 * 2**20 + 6 * rows * cols, 56 * 2**20)
            ),
            cost_estimate=None if micros is None else hint(micros),
            name=name,
        )(*args)

    own = features[0]
    far = swap(own, "row", half)
    adj = call(
        dense_kernel, "dense", shape(rows, cols), [SMEM, SMEM, ANY],
        (tile_slots[0, 0], tile_counts[0], tile_values[0, 0]),
        scratch=[pltpu.SemaphoreType.DMA((slots,))],
    )

    def stack(arrays, name, after=()):
        return call(
            stack_kernel, name, shape(len(arrays), slab, width),
            [VMEM] * len(arrays) + [ANY] * len(after), (*arrays, *after), micros=3,
        )

    beside = swap(own, "row", 1)
    pair = stack([stack([own], "own").reshape(own.shape), far], "pair", [beside])
    features_got = [own, far, beside, swap(far, "row", 1)] + [
        swap(pair, "row", k) for k in range(2, half)
    ]
    cot_near = stack(exchange([cotangent[0]] * (col_devices // 2), "col", 2), "cot_near", [pair])
    cot_other = swap(cot_near, "col", 1)

    outs = call(
        lambda *refs: forward_kernel(*refs, half=half), "forward",
        [shape(slab, width)] * col_devices + [shape(piece, width)] * col_devices,
        [SMEM] + [VMEM] * (5 + half), (me, adj, cot_near, cot_other, *features_got),
        scratch=[
            pltpu.VMEM((cols, width), BF16),
            pltpu.VMEM((rows, width), BF16),
            pltpu.VMEM((rows, width), BF16),
            pltpu.VMEM((width, width), BF16),
        ],
    )
    keep, *send = call(
        backward_kernel, "backward",
        [shape(half, slab, width)] + [shape(half // 2, slab, width)] * 2,
        [SMEM] + [VMEM] * 3 + [ANY], (me, adj, cot_near, cot_other, features_got[3]),
        scratch=[pltpu.VMEM((rows, width), BF16), pltpu.VMEM((cols, width), BF16)],
    )
    row_got = exchange(outs[:col_devices], "col")

    def add(name, terms, after=()):
        return call(
            lambda *refs: sum_kernel(*refs, terms=len(terms)), name, shape(piece, width),
            [VMEM] * len(terms) + [ANY] * len(after), (*terms, *after),
        )

    grad_col = add("grad_col", exchange(outs[col_devices:], "col"))
    distance, sends = 1, []
    while distance < half:
        got = [swap(array, "row", distance) for array in send]
        keep, *send = call(
            halve_kernel, "halve", [shape(half // (2 * distance), slab, width)] * 2,
            [VMEM] * (1 + len(got)) + [ANY], (keep, *got, grad_col), micros=None,
        )
        sends.append(send[0])
        distance *= 2
    column_far = swap(send[0][0], "row", half)
    grad_near = add("grad_near", exchange([grad_col] * half, "row"), [sends[0]])
    grad_row = add(
        "grad_row", [grad_near, swap(grad_near, "row", half)], [sends[1]]
    )
    scale = 1.0 / math.sqrt(row_devices * col_devices * slab)
    layer_out = call(
        lambda *refs: product_kernel(*refs, contract=0), "layer_out", shape(slab, width),
        [VMEM] * (1 + col_devices), (weight, *row_got),
    )
    feature_grad = call(
        lambda *refs: product_kernel(*refs, contract=1), "feature_grad", shape(slab, width),
        [VMEM] * 3, (weight, keep[0], column_far),
    )
    weight_grad = call(
        lambda *refs: gather_kernel(*refs, scale=scale), "weight_grad",
        shape(width, width, dtype=F32), [SMEM] + [VMEM] * col_devices + [ANY],
        (me, *exchange([grad_row] * col_devices, "col"), feature_grad),
        scratch=[
            pltpu.VMEM((col_devices, piece, width), F32),
            pltpu.SemaphoreType.DMA((col_devices,)),
        ],
        out_space=ANY,
    )
    return (layer_out[None], feature_grad[None], weight_grad)


def solution(mesh):
    placed = (
        P("col", "row", None),
        P(),
        P("row", "col", None, None, None),
        P("row", "col", None),
        P("row", "col"),
        P("row", "col", None),
    )
    return jax.shard_map(
        body,
        mesh=mesh,
        in_specs=placed,
        out_specs=(P("row", "col", None), P("col", "row", None), P()),
        check_vma=False,
    )
```

```python
import math

import jax
import jax.numpy as jnp
from jax import lax
from jax.experimental import pallas as pl
from jax.experimental.pallas import tpu as pltpu
from jax.sharding import PartitionSpec as P

F32 = jnp.float32
BF16 = jnp.bfloat16
VMEM = pl.BlockSpec(memory_space=pltpu.VMEM)
SMEM = pl.BlockSpec(memory_space=pltpu.SMEM)
ANY = pl.BlockSpec(memory_space=pl.ANY)


def hint(microseconds):
    return pl.CostEstimate(
        flops=int(microseconds * 1e9), bytes_accessed=int(microseconds * 3.6e6), transcendentals=0
    )


def shape(*dims, dtype=BF16):
    return jax.ShapeDtypeStruct(dims, dtype)


def rows_of(index, slab):
    return pl.ds(pl.multiple_of(index * slab, slab), slab)


def summed(refs):
    total = refs[0][...].astype(F32)
    for ref in refs[1:]:
        total = total + ref[...].astype(F32)
    return total


def dense_kernel(slots_ref, count_ref, tiles_ref, adj_ref, sems):
    slot_count, tile, _ = tiles_ref.shape
    col_tiles = adj_ref.shape[1] // tile
    live = jnp.minimum(count_ref[0], slot_count)
    adj_ref[...] = jnp.zeros_like(adj_ref)

    def copy(k):
        slot = slots_ref[k]
        row = pl.multiple_of((slot // col_tiles) * tile, tile)
        col = pl.multiple_of((slot % col_tiles) * tile, tile)
        place = adj_ref.at[pl.ds(row, tile), pl.ds(col, tile)]
        return pltpu.make_async_copy(tiles_ref.at[k], place, sems.at[k])

    def start(k, carry):
        copy(k).start()
        return carry

    def wait(k, carry):
        copy(k).wait()
        return carry

    lax.fori_loop(0, live, start, 0)
    lax.fori_loop(0, live, wait, 0)


def stack_kernel(*refs):
    out_ref = refs[-1]
    for k in range(out_ref.shape[0]):
        out_ref[k] = refs[k][...]


def place_cots(me_ref, near_ref, other_ref, out_ref):
    slab = near_ref.shape[1]
    for k in range(near_ref.shape[0]):
        out_ref[rows_of(me_ref[1] ^ (2 * k), slab), :] = near_ref[k]
        out_ref[rows_of(me_ref[1] ^ (2 * k + 1), slab), :] = other_ref[k]


def forward_kernel(me_ref, adj_ref, near_ref, other_ref, *refs, half):
    pair_refs, (*out_refs, column, cots, part, grad) = refs[:half], refs[half:]
    slab = near_ref.shape[1]
    col_devices = len(out_refs) // 2
    place_cots(me_ref, near_ref, other_ref, cots)
    for k, ref in enumerate(pair_refs):
        column[rows_of(me_ref[0] ^ k, slab), :] = ref[0]
        column[rows_of(me_ref[0] ^ k ^ half, slab), :] = ref[1]
    product = jnp.dot(adj_ref[...], column[...], preferred_element_type=F32).astype(BF16)
    part[...] = product
    grad[...] = lax.dot_general(
        product, cots[...], (((0,), (0,)), ((), ())), preferred_element_type=F32
    ).astype(BF16)
    for k in range(col_devices):
        chunk_ref, piece_ref = out_refs[k], out_refs[col_devices + k]
        chunk_ref[...] = part[rows_of(me_ref[1] ^ k, slab), :]
        piece_ref[...] = grad[rows_of(me_ref[1] ^ k, piece_ref.shape[0]), :]


def backward_kernel(me_ref, adj_ref, near_ref, other_ref, *refs):
    *pair_refs, cots, total = refs
    half, slab = len(pair_refs), pair_refs[0].shape[1]
    place_cots(me_ref, near_ref, other_ref, cots)
    total[...] = lax.dot_general(
        adj_ref[...], cots[...], (((0,), (0,)), ((), ())), preferred_element_type=F32
    ).astype(BF16)
    for k, ref in enumerate(pair_refs):
        ref[0] = total[rows_of(me_ref[0] ^ k, slab), :]
        ref[1] = total[rows_of(me_ref[0] ^ k ^ half, slab), :]


def pair_sum_kernel(*refs):
    *pair_refs, keep_ref, send_ref = refs
    total = summed(pair_refs)
    keep_ref[...] = total[0]
    send_ref[...] = total[1].astype(BF16)


def weighted(weight_ref, term_refs, contract):
    return lax.dot_general(
        summed(term_refs).astype(BF16),
        weight_ref[...],
        (((1,), (contract,)), ((), ())),
        preferred_element_type=F32,
    ).astype(BF16)


def output_kernel(weight_ref, *refs):
    *term_refs, out_ref = refs
    out_ref[...] = weighted(weight_ref, term_refs, 0)


def hold_kernel(*refs):
    count = len(refs) // 2
    for src_ref, dst_ref in zip(refs[:count], refs[count + 1 :]):
        dst_ref[...] = src_ref[...]


def sum_kernel(*refs, terms):
    refs[-1][...] = summed(refs[:terms]).astype(BF16)


def finish_kernel(me_ref, weight_ref, keep_ref, got_ref, *refs, scale):
    *piece_refs, feature_ref, grad_ref = refs
    piece = piece_refs[0].shape[0]
    for k, ref in enumerate(piece_refs):
        grad_ref[rows_of(me_ref[1] ^ k, piece), :] = ref[...].astype(F32) * scale
    feature_ref[...] = weighted(weight_ref, [keep_ref, got_ref], 1)


def swap(array, axis, distance):
    pairs = [(i, i ^ distance) for i in range(lax.axis_size(axis))]
    return lax.ppermute(array, axis, pairs)


def exchange(chunks, axis, stride=1):
    return [chunks[0]] + [swap(chunks[k], axis, k * stride) for k in range(1, len(chunks))]


def body(features, weight, tile_values, tile_slots, tile_counts, cotangent):
    row_devices = lax.axis_size("row")
    col_devices = lax.axis_size("col")
    half = row_devices // 2
    slots, tile = tile_values.shape[2:4]
    slab, width = features.shape[1:]
    rows, cols = col_devices * slab, row_devices * slab
    piece = width // col_devices
    me = jnp.stack([lax.axis_index("row"), lax.axis_index("col")]).astype(jnp.int32)

    def call(kernel, name, out_shape, in_specs, args, scratch=(), micros=None):
        many = isinstance(out_shape, list)
        return pl.pallas_call(
            kernel,
            out_shape=out_shape,
            in_specs=in_specs,
            out_specs=[VMEM] * len(out_shape) if many else VMEM,
            scratch_shapes=scratch,
            compiler_params=pltpu.CompilerParams(
                vmem_limit_bytes=min(8 * 2**20 + 6 * rows * cols, 56 * 2**20)
            ),
            cost_estimate=None if micros is None else hint(micros),
            name=name,
        )(*args)

    own = features[0]
    far = swap(own, "row", half)
    adj = call(
        dense_kernel, "dense", shape(rows, cols), [SMEM, SMEM, ANY],
        (tile_slots[0, 0], tile_counts[0], tile_values[0, 0]),
        scratch=[pltpu.SemaphoreType.DMA((slots,))],
    )

    def stack(arrays, name, after=()):
        return call(
            stack_kernel, name, shape(len(arrays), slab, width),
            [VMEM] * len(arrays) + [ANY] * len(after), (*arrays, *after), micros=3,
        )

    pair = stack([stack([own], "own").reshape(own.shape), far], "pair")
    features_got = exchange([pair] * half, "row")
    cot_near = stack(exchange([cotangent[0]] * (col_devices // 2), "col", 2), "cot_near", [pair])
    cot_other = swap(cot_near, "col", 1)

    outs = call(
        lambda *refs: forward_kernel(*refs, half=half), "forward",
        [shape(slab, width)] * col_devices + [shape(piece, width)] * col_devices,
        [SMEM] + [VMEM] * (3 + half), (me, adj, cot_near, cot_other, *features_got),
        scratch=[
            pltpu.VMEM((cols, width), BF16),
            pltpu.VMEM((rows, width), BF16),
            pltpu.VMEM((rows, width), BF16),
            pltpu.VMEM((width, width), BF16),
        ],
    )
    column_pairs = call(
        backward_kernel, "backward", [shape(2, slab, width)] * half,
        [SMEM] + [VMEM] * 3, (me, adj, cot_near, cot_other),
        scratch=[pltpu.VMEM((rows, width), BF16), pltpu.VMEM((cols, width), BF16)],
    )
    column_keep, column_send = call(
        pair_sum_kernel, "pair_sum", [shape(slab, width, dtype=F32), shape(slab, width)],
        [VMEM] * half, exchange(column_pairs, "row"), micros=5,
    )
    column_far = swap(column_send, "row", half)
    def add(name, terms, after=()):
        return call(
            lambda *refs: sum_kernel(*refs, terms=len(terms)), name, shape(piece, width),
            [VMEM] * len(terms) + [ANY] * len(after), (*terms, *after),
        )

    grad_col = add("grad_col", exchange(outs[col_devices:], "col"), [column_send])
    grad_near = add("grad_near", exchange([grad_col] * half, "row"), [])
    chunks = call(
        hold_kernel, "hold", [shape(slab, width)] * (col_devices - 1),
        [VMEM] * (col_devices - 1) + [ANY], (*outs[1:col_devices], grad_near),
    )
    row_got = exchange([outs[0], *chunks], "col")
    grad_row = add(
        "grad_row", [grad_near, swap(grad_near, "row", half)], [column_far]
    )
    scale = 1.0 / math.sqrt(row_devices * col_devices * slab)
    layer_out = call(
        output_kernel, "layer_out", shape(slab, width),
        [VMEM] * (1 + col_devices), (weight, *row_got),
    )
    feature_grad, weight_grad = call(
        lambda *refs: finish_kernel(*refs, scale=scale), "finish",
        [shape(slab, width), shape(width, width, dtype=F32)],
        [SMEM] + [VMEM] * (3 + col_devices),
        (me, weight, column_keep, column_far, *exchange([grad_row] * col_devices, "col")),
    )
    return (layer_out[None], feature_grad[None], weight_grad)


def solution(mesh):
    placed = (
        P("col", "row", None),
        P(),
        P("row", "col", None, None, None),
        P("row", "col", None),
        P("row", "col"),
        P("row", "col", None),
    )
    return jax.shard_map(
        body,
        mesh=mesh,
        in_specs=placed,
        out_specs=(P("row", "col", None), P("col", "row", None), P()),
        check_vma=False,
    )
```

```python
import math

import jax
import jax.numpy as jnp
from jax import lax
from jax.experimental import pallas as pl
from jax.experimental.pallas import tpu as pltpu
from jax.sharding import PartitionSpec as P

F32 = jnp.float32
BF16 = jnp.bfloat16
VMEM = pl.BlockSpec(memory_space=pltpu.VMEM)
SMEM = pl.BlockSpec(memory_space=pltpu.SMEM)
ANY = pl.BlockSpec(memory_space=pl.ANY)


def hint(microseconds):
    return pl.CostEstimate(
        flops=int(microseconds * 1e9), bytes_accessed=int(microseconds * 3.6e6), transcendentals=0
    )


def shape(*dims, dtype=BF16):
    return jax.ShapeDtypeStruct(dims, dtype)


def rows_of(index, slab):
    return pl.ds(pl.multiple_of(index * slab, slab), slab)


def summed(refs):
    total = refs[0][...].astype(F32)
    for ref in refs[1:]:
        total = total + ref[...].astype(F32)
    return total


def dense_kernel(slots_ref, count_ref, tiles_ref, adj_ref, sems):
    slot_count, tile, _ = tiles_ref.shape
    col_tiles = adj_ref.shape[1] // tile
    live = jnp.minimum(count_ref[0], slot_count)
    adj_ref[...] = jnp.zeros_like(adj_ref)

    def copy(k):
        slot = slots_ref[k]
        row = pl.multiple_of((slot // col_tiles) * tile, tile)
        col = pl.multiple_of((slot % col_tiles) * tile, tile)
        place = adj_ref.at[pl.ds(row, tile), pl.ds(col, tile)]
        return pltpu.make_async_copy(tiles_ref.at[k], place, sems.at[k])

    def start(k, carry):
        copy(k).start()
        return carry

    def wait(k, carry):
        copy(k).wait()
        return carry

    lax.fori_loop(0, live, start, 0)
    lax.fori_loop(0, live, wait, 0)


def stack_kernel(*refs):
    out_ref = refs[-1]
    for k in range(out_ref.shape[0]):
        out_ref[k] = refs[k][...]


def place_cots(me_ref, near_ref, other_ref, out_ref):
    slab = near_ref.shape[1]
    for k in range(near_ref.shape[0]):
        out_ref[rows_of(me_ref[1] ^ (2 * k), slab), :] = near_ref[k]
        out_ref[rows_of(me_ref[1] ^ (2 * k + 1), slab), :] = other_ref[k]


def forward_kernel(me_ref, adj_ref, near_ref, other_ref, *refs, half):
    pair_refs, (*out_refs, column, cots, part, grad) = refs[:half], refs[half:]
    slab = near_ref.shape[1]
    col_devices = len(out_refs) // 2
    place_cots(me_ref, near_ref, other_ref, cots)
    for k, ref in enumerate(pair_refs):
        column[rows_of(me_ref[0] ^ k, slab), :] = ref[0]
        column[rows_of(me_ref[0] ^ k ^ half, slab), :] = ref[1]
    product = jnp.dot(adj_ref[...], column[...], preferred_element_type=F32).astype(BF16)
    part[...] = product
    grad[...] = lax.dot_general(
        product, cots[...], (((0,), (0,)), ((), ())), preferred_element_type=F32
    ).astype(BF16)
    for k in range(col_devices):
        chunk_ref, piece_ref = out_refs[k], out_refs[col_devices + k]
        chunk_ref[...] = part[rows_of(me_ref[1] ^ k, slab), :]
        piece_ref[...] = grad[rows_of(me_ref[1] ^ k, piece_ref.shape[0]), :]


def backward_kernel(me_ref, adj_ref, near_ref, other_ref, *refs):
    *pair_refs, cots, total = refs
    half, slab = len(pair_refs), pair_refs[0].shape[1]
    place_cots(me_ref, near_ref, other_ref, cots)
    total[...] = lax.dot_general(
        adj_ref[...], cots[...], (((0,), (0,)), ((), ())), preferred_element_type=F32
    ).astype(BF16)
    for k, ref in enumerate(pair_refs):
        ref[0] = total[rows_of(me_ref[0] ^ k, slab), :]
        ref[1] = total[rows_of(me_ref[0] ^ k ^ half, slab), :]


def pair_sum_kernel(*refs):
    *pair_refs, keep_ref, send_ref = refs
    total = summed(pair_refs)
    keep_ref[...] = total[0]
    send_ref[...] = total[1].astype(BF16)


def weighted(weight_ref, term_refs, contract):
    return lax.dot_general(
        summed(term_refs).astype(BF16),
        weight_ref[...],
        (((1,), (contract,)), ((), ())),
        preferred_element_type=F32,
    ).astype(BF16)


def output_kernel(weight_ref, *refs):
    *term_refs, out_ref = refs
    out_ref[...] = weighted(weight_ref, term_refs, 0)


def hold_kernel(*refs):
    count = len(refs) // 2
    for src_ref, dst_ref in zip(refs[:count], refs[count + 1 :]):
        dst_ref[...] = src_ref[...]


def sum_kernel(*refs, terms):
    refs[-1][...] = summed(refs[:terms]).astype(BF16)


def finish_kernel(me_ref, weight_ref, keep_ref, got_ref, *refs, scale):
    *piece_refs, feature_ref, grad_ref = refs
    piece = piece_refs[0].shape[0]
    for k, ref in enumerate(piece_refs):
        grad_ref[rows_of(me_ref[1] ^ k, piece), :] = ref[...].astype(F32) * scale
    feature_ref[...] = weighted(weight_ref, [keep_ref, got_ref], 1)


def swap(array, axis, distance):
    pairs = [(i, i ^ distance) for i in range(lax.axis_size(axis))]
    return lax.ppermute(array, axis, pairs)


def exchange(chunks, axis, stride=1):
    return [chunks[0]] + [swap(chunks[k], axis, k * stride) for k in range(1, len(chunks))]


def body(features, weight, tile_values, tile_slots, tile_counts, cotangent):
    row_devices = lax.axis_size("row")
    col_devices = lax.axis_size("col")
    half = row_devices // 2
    slots, tile = tile_values.shape[2:4]
    slab, width = features.shape[1:]
    rows, cols = col_devices * slab, row_devices * slab
    piece = width // col_devices
    me = jnp.stack([lax.axis_index("row"), lax.axis_index("col")]).astype(jnp.int32)

    def call(kernel, name, out_shape, in_specs, args, scratch=(), micros=None):
        many = isinstance(out_shape, list)
        return pl.pallas_call(
            kernel,
            out_shape=out_shape,
            in_specs=in_specs,
            out_specs=[VMEM] * len(out_shape) if many else VMEM,
            scratch_shapes=scratch,
            compiler_params=pltpu.CompilerParams(
                vmem_limit_bytes=min(8 * 2**20 + 6 * rows * cols, 56 * 2**20)
            ),
            cost_estimate=None if micros is None else hint(micros),
            name=name,
        )(*args)

    own = features[0]
    far = swap(own, "row", half)
    adj = call(
        dense_kernel, "dense", shape(rows, cols), [SMEM, SMEM, ANY],
        (tile_slots[0, 0], tile_counts[0], tile_values[0, 0]),
        scratch=[pltpu.SemaphoreType.DMA((slots,))],
    )

    def hold(arrays, after, name):
        return call(
            hold_kernel, name, [shape(slab, width)] * len(arrays),
            [VMEM] * len(arrays) + [ANY], (*arrays, after),
        )

    def stack(arrays, name, after=()):
        return call(
            stack_kernel, name, shape(len(arrays), slab, width),
            [VMEM] * len(arrays) + [ANY] * len(after), (*arrays, *after), micros=3,
        )

    kept = hold([own, cotangent[0]], tile_counts, "own")
    pair = stack([kept[0], far], "pair")
    features_got = exchange([pair] * half, "row")
    cot_near = stack(
        [kept[1]] + exchange([cotangent[0]] * (col_devices // 2), "col", 2)[1:], "cot_near"
    )
    cot_other = swap(cot_near, "col", 1)

    outs = call(
        lambda *refs: forward_kernel(*refs, half=half), "forward",
        [shape(slab, width)] * col_devices + [shape(piece, width)] * col_devices,
        [SMEM] + [VMEM] * (3 + half), (me, adj, cot_near, cot_other, *features_got),
        scratch=[
            pltpu.VMEM((cols, width), BF16),
            pltpu.VMEM((rows, width), BF16),
            pltpu.VMEM((rows, width), BF16),
            pltpu.VMEM((width, width), BF16),
        ],
    )
    column_pairs = call(
        backward_kernel, "backward", [shape(2, slab, width)] * half,
        [SMEM] + [VMEM] * 3, (me, adj, cot_near, cot_other),
        scratch=[pltpu.VMEM((rows, width), BF16), pltpu.VMEM((cols, width), BF16)],
    )
    column_keep, column_send = call(
        pair_sum_kernel, "pair_sum", [shape(slab, width, dtype=F32), shape(slab, width)],
        [VMEM] * half, exchange(column_pairs, "row"), micros=5,
    )
    def add(name, terms, after=()):
        return call(
            lambda *refs: sum_kernel(*refs, terms=len(terms)), name, shape(piece, width),
            [VMEM] * len(terms) + [ANY] * len(after), (*terms, *after),
        )

    grad_col = add("grad_col", exchange(outs[col_devices:], "col"), [column_send])
    near_terms = exchange([grad_col] * half, "row")
    chunks = hold(outs[1:col_devices], near_terms[1], "hold_chunks")
    row_got = exchange([outs[0], *chunks], "col")
    grad_near = add("grad_near", near_terms, [])
    column_far = swap(hold([column_send], grad_near, "hold_sum")[0], "row", half)
    grad_row = add(
        "grad_row", [grad_near, swap(grad_near, "row", half)], []
    )
    scale = 1.0 / math.sqrt(row_devices * col_devices * slab)
    layer_out = call(
        output_kernel, "layer_out", shape(slab, width),
        [VMEM] * (1 + col_devices), (weight, *row_got),
    )
    feature_grad, weight_grad = call(
        lambda *refs: finish_kernel(*refs, scale=scale), "finish",
        [shape(slab, width), shape(width, width, dtype=F32)],
        [SMEM] + [VMEM] * (3 + col_devices),
        (me, weight, column_keep, column_far, *exchange([grad_row] * col_devices, "col")),
    )
    return (layer_out[None], feature_grad[None], weight_grad)


def solution(mesh):
    placed = (
        P("col", "row", None),
        P(),
        P("row", "col", None, None, None),
        P("row", "col", None),
        P("row", "col"),
        P("row", "col", None),
    )
    return jax.shard_map(
        body,
        mesh=mesh,
        in_specs=placed,
        out_specs=(P("row", "col", None), P("col", "row", None), P()),
        check_vma=False,
    )
```

```python
import math

import jax
import jax.numpy as jnp
from jax import lax
from jax.experimental import pallas as pl
from jax.experimental.pallas import tpu as pltpu
from jax.sharding import PartitionSpec as P

F32 = jnp.float32
BF16 = jnp.bfloat16
VMEM = pl.BlockSpec(memory_space=pltpu.VMEM)
SMEM = pl.BlockSpec(memory_space=pltpu.SMEM)
ANY = pl.BlockSpec(memory_space=pl.ANY)


def hint(microseconds):
    return pl.CostEstimate(
        flops=int(microseconds * 1e9), bytes_accessed=int(microseconds * 3.6e6), transcendentals=0
    )


def shape(*dims, dtype=BF16):
    return jax.ShapeDtypeStruct(dims, dtype)


def rows_of(index, slab):
    return pl.ds(pl.multiple_of(index * slab, slab), slab)


def summed(refs):
    total = refs[0][...].astype(F32)
    for ref in refs[1:]:
        total = total + ref[...].astype(F32)
    return total


def dense_kernel(slots_ref, count_ref, tiles_ref, adj_ref, sems):
    slot_count, tile, _ = tiles_ref.shape
    col_tiles = adj_ref.shape[1] // tile
    live = jnp.minimum(count_ref[0], slot_count)
    adj_ref[...] = jnp.zeros_like(adj_ref)

    def copy(k):
        slot = slots_ref[k]
        row = pl.multiple_of((slot // col_tiles) * tile, tile)
        col = pl.multiple_of((slot % col_tiles) * tile, tile)
        place = adj_ref.at[pl.ds(row, tile), pl.ds(col, tile)]
        return pltpu.make_async_copy(tiles_ref.at[k], place, sems.at[k])

    def start(k, carry):
        copy(k).start()
        return carry

    def wait(k, carry):
        copy(k).wait()
        return carry

    lax.fori_loop(0, live, start, 0)
    lax.fori_loop(0, live, wait, 0)


def stack_kernel(*refs):
    out_ref = refs[-1]
    for k in range(out_ref.shape[0]):
        out_ref[k] = refs[k][...]


def place_cots(me_ref, near_ref, other_ref, out_ref):
    slab = near_ref.shape[1]
    for k in range(near_ref.shape[0]):
        out_ref[rows_of(me_ref[1] ^ (2 * k), slab), :] = near_ref[k]
        out_ref[rows_of(me_ref[1] ^ (2 * k + 1), slab), :] = other_ref[k]


def forward_kernel(me_ref, adj_ref, near_ref, other_ref, *refs, half):
    pair_refs, (*out_refs, both_ref, column, cots, part, grad) = refs[:half], refs[half:]
    slab = near_ref.shape[1]
    others = len(out_refs) // 2
    piece = both_ref.shape[0] - slab
    place_cots(me_ref, near_ref, other_ref, cots)
    for k, ref in enumerate(pair_refs[::-1]):
        column[rows_of(me_ref[0] ^ k, slab), :] = ref[0]
        column[rows_of(me_ref[0] ^ k ^ half, slab), :] = ref[1]
    product = jnp.dot(adj_ref[...], column[...], preferred_element_type=F32).astype(BF16)
    part[...] = product
    grad[...] = lax.dot_general(
        product, cots[...], (((0,), (0,)), ((), ())), preferred_element_type=F32
    ).astype(BF16)
    for n in range(others):
        k = n + 1 if n else 0
        out_refs[n][...] = part[rows_of(me_ref[1] ^ k, slab), :]
        out_refs[others + n][...] = grad[rows_of(me_ref[1] ^ k, piece), :]
    both_ref[:slab, :] = part[rows_of(me_ref[1] ^ 1, slab), :]
    both_ref[slab:, :] = grad[rows_of(me_ref[1] ^ 1, piece), :]


def backward_kernel(me_ref, adj_ref, near_ref, other_ref, *refs):
    *pair_refs, cots, total = refs
    half, slab = len(pair_refs), pair_refs[0].shape[1]
    place_cots(me_ref, near_ref, other_ref, cots)
    total[...] = lax.dot_general(
        adj_ref[...], cots[...], (((0,), (0,)), ((), ())), preferred_element_type=F32
    ).astype(BF16)
    for k, ref in enumerate(pair_refs):
        ref[0] = total[rows_of(me_ref[0] ^ k, slab), :]
        ref[1] = total[rows_of(me_ref[0] ^ k ^ half, slab), :]


def pair_sum_kernel(*refs):
    *pair_refs, keep_ref, send_ref = refs
    total = summed(pair_refs)
    keep_ref[...] = total[0]
    send_ref[...] = total[1].astype(BF16)


def weighted(weight_ref, term_refs, contract):
    return lax.dot_general(
        summed(term_refs).astype(BF16),
        weight_ref[...],
        (((1,), (contract,)), ((), ())),
        preferred_element_type=F32,
    ).astype(BF16)


def output_kernel(weight_ref, first_ref, *refs):
    *term_refs, out_ref = refs
    first_ref = first_ref.at[: out_ref.shape[0], :]
    out_ref[...] = weighted(weight_ref, [first_ref, *term_refs], 0)


def col_kernel(first_ref, *refs, terms):
    out_ref = refs[-1]
    first_ref = first_ref.at[first_ref.shape[0] - out_ref.shape[0] :, :]
    out_ref[...] = summed([first_ref, *refs[:terms]]).astype(BF16)


def hold_kernel(*refs):
    count = len(refs) // 2
    for src_ref, dst_ref in zip(refs[:count], refs[count + 1 :]):
        dst_ref[...] = src_ref[...]


def near_kernel(send_ref, *refs, terms):
    slab = send_ref.shape[0]
    refs[-1][:slab, :] = send_ref[...]
    refs[-1][slab:, :] = summed(refs[:terms]).astype(BF16)


def row_kernel(held_ref, got_ref, out_ref):
    slab = held_ref.shape[0] - out_ref.shape[0]
    out_ref[...] = summed([held_ref.at[slab:, :], got_ref.at[slab:, :]]).astype(BF16)


def finish_kernel(me_ref, weight_ref, keep_ref, got_ref, *refs, scale):
    *piece_refs, feature_ref, grad_ref = refs
    got_ref = got_ref.at[: feature_ref.shape[0], :]
    piece = piece_refs[0].shape[0]
    for k, ref in enumerate(piece_refs):
        grad_ref[rows_of(me_ref[1] ^ k, piece), :] = ref[...].astype(F32) * scale
    feature_ref[...] = weighted(weight_ref, [keep_ref, got_ref], 1)


def swap(array, axis, distance):
    pairs = [(i, i ^ distance) for i in range(lax.axis_size(axis))]
    return lax.ppermute(array, axis, pairs)


def exchange(chunks, axis, stride=1):
    return [chunks[0]] + [swap(chunks[k], axis, k * stride) for k in range(1, len(chunks))]


def body(features, weight, tile_values, tile_slots, tile_counts, cotangent):
    row_devices = lax.axis_size("row")
    col_devices = lax.axis_size("col")
    half = row_devices // 2
    slots, tile = tile_values.shape[2:4]
    slab, width = features.shape[1:]
    rows, cols = col_devices * slab, row_devices * slab
    piece = width // col_devices
    me = jnp.stack([lax.axis_index("row"), lax.axis_index("col")]).astype(jnp.int32)

    def call(kernel, name, out_shape, in_specs, args, scratch=(), micros=None):
        many = isinstance(out_shape, list)
        return pl.pallas_call(
            kernel,
            out_shape=out_shape,
            in_specs=in_specs,
            out_specs=[VMEM] * len(out_shape) if many else VMEM,
            scratch_shapes=scratch,
            compiler_params=pltpu.CompilerParams(
                vmem_limit_bytes=min(8 * 2**20 + 6 * rows * cols, 56 * 2**20)
            ),
            cost_estimate=None if micros is None else hint(micros),
            name=name,
        )(*args)

    own = features[0]
    far = swap(own, "row", half)
    adj = call(
        dense_kernel, "dense", shape(rows, cols), [SMEM, SMEM, ANY],
        (tile_slots[0, 0], tile_counts[0], tile_values[0, 0]),
        scratch=[pltpu.SemaphoreType.DMA((slots,))],
    )

    def hold(arrays, after, name):
        return call(
            hold_kernel, name, [shape(slab, width)] * len(arrays),
            [VMEM] * len(arrays) + [ANY], (*arrays, after),
        )

    def stack(arrays, name, after=()):
        return call(
            stack_kernel, name, shape(len(arrays), slab, width),
            [VMEM] * len(arrays) + [ANY] * len(after), (*arrays, *after), micros=3,
        )

    kept = hold([own, cotangent[0]], tile_counts, "own")
    pair = stack([kept[0], far], "pair")
    features_got = exchange([pair] * half, "row")
    cot_near = stack(
        [kept[1]] + exchange([cotangent[0]] * (col_devices // 2), "col", 2)[1:], "cot_near"
    )
    cot_other = swap(cot_near, "col", 1)

    outs = call(
        lambda *refs: forward_kernel(*refs, half=half), "forward",
        [shape(slab, width)] * (col_devices - 1)
        + [shape(piece, width)] * (col_devices - 1)
        + [shape(slab + piece, width)],
        [SMEM] + [VMEM] * (3 + half), (me, adj, cot_near, cot_other, *features_got[::-1]),
        scratch=[
            pltpu.VMEM((cols, width), BF16),
            pltpu.VMEM((rows, width), BF16),
            pltpu.VMEM((rows, width), BF16),
            pltpu.VMEM((width, width), BF16),
        ],
    )
    column_pairs = call(
        backward_kernel, "backward", [shape(2, slab, width)] * half,
        [SMEM] + [VMEM] * 3, (me, adj, cot_near, cot_other),
        scratch=[pltpu.VMEM((rows, width), BF16), pltpu.VMEM((cols, width), BF16)],
    )
    column_keep, column_send = call(
        pair_sum_kernel, "pair_sum", [shape(slab, width, dtype=F32), shape(slab, width)],
        [VMEM] * half, exchange(column_pairs, "row")[::-1], micros=5,
    )
    chunks, pieces = outs[: col_devices - 1], outs[col_devices - 1 : -1]
    first = swap(outs[-1], "col", 1)

    def fetch(arrays):
        return [arrays[0]] + [swap(arrays[k - 1], "col", k) for k in range(2, col_devices)]

    grad_col = call(
        lambda *refs: col_kernel(*refs, terms=col_devices - 1), "grad_col", shape(piece, width),
        [VMEM] * col_devices + [ANY], (first, *fetch(pieces), column_send),
    )
    near_terms = exchange([grad_col] * half, "row")
    row_got = fetch([chunks[0], *hold(chunks[1:], near_terms[3], "hold_chunks")])
    both = call(
        lambda *refs: near_kernel(*refs, terms=half), "grad_near", shape(slab + piece, width),
        [VMEM] * (1 + half), (column_send, *near_terms),
    )
    both_far = swap(both, "row", half)
    grad_row = call(
        row_kernel, "grad_row", shape(piece, width), [VMEM] * 2, (both, both_far)
    )
    scale = 1.0 / math.sqrt(row_devices * col_devices * slab)
    layer_out = call(
        output_kernel, "layer_out", shape(slab, width),
        [VMEM] * (1 + col_devices), (weight, first, *row_got),
    )
    feature_grad, weight_grad = call(
        lambda *refs: finish_kernel(*refs, scale=scale), "finish",
        [shape(slab, width), shape(width, width, dtype=F32)],
        [SMEM] + [VMEM] * (3 + col_devices),
        (me, weight, column_keep, both_far, *exchange([grad_row] * col_devices, "col")),
    )
    return (layer_out[None], feature_grad[None], weight_grad)


def solution(mesh):
    placed = (
        P("col", "row", None),
        P(),
        P("row", "col", None, None, None),
        P("row", "col", None),
        P("row", "col"),
        P("row", "col", None),
    )
    return jax.shard_map(
        body,
        mesh=mesh,
        in_specs=placed,
        out_specs=(P("row", "col", None), P("col", "row", None), P()),
        check_vma=False,
    )
```

```python
import math

import jax
import jax.numpy as jnp
from jax import lax
from jax.experimental import pallas as pl
from jax.experimental.pallas import tpu as pltpu
from jax.sharding import PartitionSpec as P

F32 = jnp.float32
BF16 = jnp.bfloat16
VMEM = pl.BlockSpec(memory_space=pltpu.VMEM)
SMEM = pl.BlockSpec(memory_space=pltpu.SMEM)
ANY = pl.BlockSpec(memory_space=pl.ANY)


def hint(microseconds):
    return pl.CostEstimate(
        flops=int(microseconds * 1e9), bytes_accessed=int(microseconds * 3.6e6), transcendentals=0
    )


def shape(*dims, dtype=BF16):
    return jax.ShapeDtypeStruct(dims, dtype)


def rows_of(index, slab):
    return pl.ds(pl.multiple_of(index * slab, slab), slab)


def summed(refs):
    total = refs[0][...].astype(F32)
    for ref in refs[1:]:
        total = total + ref[...].astype(F32)
    return total


def dense_kernel(meta_ref, tiles_ref, adj_ref, sems):
    slot_count, tile, _ = tiles_ref.shape
    col_tiles = adj_ref.shape[1] // tile
    live = jnp.minimum(meta_ref[2], slot_count)
    adj_ref[...] = jnp.zeros_like(adj_ref)

    def copy(k):
        slot = meta_ref[3 + k]
        row = pl.multiple_of((slot // col_tiles) * tile, tile)
        col = pl.multiple_of((slot % col_tiles) * tile, tile)
        place = adj_ref.at[pl.ds(row, tile), pl.ds(col, tile)]
        return pltpu.make_async_copy(tiles_ref.at[k], place, sems.at[k])

    def start(k, carry):
        copy(k).start()
        return carry

    def wait(k, carry):
        copy(k).wait()
        return carry

    lax.fori_loop(0, live, start, 0)
    lax.fori_loop(0, live, wait, 0)


def stack_kernel(*refs):
    out_ref = refs[-1]
    for k in range(out_ref.shape[0]):
        out_ref[k] = refs[k][...]


def place_cots(meta_ref, near_ref, other_ref, out_ref):
    slab = near_ref.shape[1]
    for k in range(near_ref.shape[0]):
        out_ref[rows_of(meta_ref[1] ^ (2 * k), slab), :] = near_ref[k]
        out_ref[rows_of(meta_ref[1] ^ (2 * k + 1), slab), :] = other_ref[k]


def forward_kernel(meta_ref, adj_ref, near_ref, other_ref, *refs, half):
    pair_refs, (*out_refs, both_ref, column, cots, part, grad) = refs[:half], refs[half:]
    slab = near_ref.shape[1]
    others = len(out_refs) // 2
    piece = both_ref.shape[0] - slab
    place_cots(meta_ref, near_ref, other_ref, cots)
    for k, ref in enumerate(pair_refs[::-1]):
        column[rows_of(meta_ref[0] ^ k, slab), :] = ref[0]
        column[rows_of(meta_ref[0] ^ k ^ half, slab), :] = ref[1]
    product = jnp.dot(adj_ref[...], column[...], preferred_element_type=F32).astype(BF16)
    part[...] = product
    grad[...] = lax.dot_general(
        product, cots[...], (((0,), (0,)), ((), ())), preferred_element_type=F32
    ).astype(BF16)
    for n in range(others):
        k = n + 1 if n else 0
        out_refs[n][...] = part[rows_of(meta_ref[1] ^ k, slab), :]
        out_refs[others + n][...] = grad[rows_of(meta_ref[1] ^ k, piece), :]
    both_ref[:slab, :] = part[rows_of(meta_ref[1] ^ 1, slab), :]
    both_ref[slab:, :] = grad[rows_of(meta_ref[1] ^ 1, piece), :]


def backward_kernel(meta_ref, adj_ref, near_ref, other_ref, *refs):
    *pair_refs, cots, total = refs
    half, slab = len(pair_refs), pair_refs[0].shape[1]
    place_cots(meta_ref, near_ref, other_ref, cots)
    total[...] = lax.dot_general(
        adj_ref[...], cots[...], (((0,), (0,)), ((), ())), preferred_element_type=F32
    ).astype(BF16)
    for k, ref in enumerate(pair_refs):
        ref[0] = total[rows_of(meta_ref[0] ^ k, slab), :]
        ref[1] = total[rows_of(meta_ref[0] ^ k ^ half, slab), :]


def pair_sum_kernel(*refs):
    *pair_refs, keep_ref, send_ref = refs
    total = summed(pair_refs)
    keep_ref[...] = total[0]
    send_ref[...] = total[1].astype(BF16)


def weighted(weight_ref, term_refs, contract):
    return lax.dot_general(
        summed(term_refs).astype(BF16),
        weight_ref[...],
        (((1,), (contract,)), ((), ())),
        preferred_element_type=F32,
    ).astype(BF16)


def output_kernel(weight_ref, keep_ref, far_ref, first_ref, *refs):
    *chunk_refs, layer_ref, feature_ref = refs
    slab = layer_ref.shape[0]
    layer_ref[...] = weighted(weight_ref, [first_ref.at[:slab, :], *chunk_refs], 0)
    feature_ref[...] = weighted(weight_ref, [keep_ref, far_ref.at[:slab, :]], 1)


def col_kernel(first_ref, *refs, terms):
    out_ref = refs[-1]
    first_ref = first_ref.at[first_ref.shape[0] - out_ref.shape[0] :, :]
    out_ref[...] = summed([first_ref, *refs[:terms]]).astype(BF16)


def hold_kernel(*refs):
    count = len(refs) // 2
    for src_ref, dst_ref in zip(refs[:count], refs[count + 1 :]):
        dst_ref[...] = src_ref[...]


def near_kernel(send_ref, *refs, terms):
    slab = send_ref.shape[0]
    refs[-1][:slab, :] = send_ref[...]
    refs[-1][slab:, :] = summed(refs[:terms]).astype(BF16)


def row_kernel(held_ref, got_ref, out_ref):
    slab = held_ref.shape[0] - out_ref.shape[0]
    out_ref[...] = summed([held_ref.at[slab:, :], got_ref.at[slab:, :]]).astype(BF16)


def gather_kernel(meta_ref, *refs):
    *piece_refs, out_ref = refs
    piece = piece_refs[0].shape[0]
    for k, ref in enumerate(piece_refs):
        out_ref[rows_of(meta_ref[1] ^ k, piece), :] = ref[...]


def swap(array, axis, distance):
    pairs = [(i, i ^ distance) for i in range(lax.axis_size(axis))]
    return lax.ppermute(array, axis, pairs)


def exchange(chunks, axis, stride=1):
    return [chunks[0]] + [swap(chunks[k], axis, k * stride) for k in range(1, len(chunks))]


def body(features, weight, tile_values, tile_slots, tile_counts, cotangent):
    row_devices = lax.axis_size("row")
    col_devices = lax.axis_size("col")
    half = row_devices // 2
    slots, tile = tile_values.shape[2:4]
    slab, width = features.shape[1:]
    rows, cols = col_devices * slab, row_devices * slab
    piece = width // col_devices
    place = jnp.stack([lax.axis_index("row"), lax.axis_index("col")]).astype(jnp.int32)
    me = jnp.concatenate([place, tile_counts[0], tile_slots[0, 0]])

    def call(kernel, name, out_shape, in_specs, args, scratch=(), micros=None):
        many = isinstance(out_shape, list)
        return pl.pallas_call(
            kernel,
            out_shape=out_shape,
            in_specs=in_specs,
            out_specs=[VMEM] * len(out_shape) if many else VMEM,
            scratch_shapes=scratch,
            compiler_params=pltpu.CompilerParams(
                vmem_limit_bytes=min(8 * 2**20 + 6 * rows * cols, 56 * 2**20)
            ),
            cost_estimate=None if micros is None else hint(micros),
            name=name,
        )(*args)

    own = features[0]
    far = swap(own, "row", half)
    adj = call(
        dense_kernel, "dense", shape(rows, cols), [SMEM, ANY], (me, tile_values[0, 0]),
        scratch=[pltpu.SemaphoreType.DMA((slots,))],
    )

    def hold(arrays, after, name):
        return call(
            hold_kernel, name, [shape(*array.shape) for array in arrays],
            [VMEM] * len(arrays) + [ANY], (*arrays, after),
        )

    def stack(arrays, name, after=()):
        return call(
            stack_kernel, name, shape(len(arrays), slab, width),
            [VMEM] * len(arrays) + [ANY] * len(after), (*arrays, *after), micros=3,
        )

    kept = hold([own, cotangent[0]], tile_counts, "own")
    pair = stack([kept[0], far], "pair")
    features_got = exchange([pair] * half, "row")
    cot_near = stack(
        [kept[1]] + exchange([cotangent[0]] * (col_devices // 2), "col", 2)[1:], "cot_near"
    )
    cot_other = swap(cot_near, "col", 1)

    outs = call(
        lambda *refs: forward_kernel(*refs, half=half), "forward",
        [shape(slab, width)] * (col_devices - 1)
        + [shape(piece, width)] * (col_devices - 1)
        + [shape(slab + piece, width)],
        [SMEM] + [VMEM] * (3 + half), (me, adj, cot_near, cot_other, *features_got[::-1]),
        scratch=[
            pltpu.VMEM((cols, width), BF16),
            pltpu.VMEM((rows, width), BF16),
            pltpu.VMEM((rows, width), BF16),
            pltpu.VMEM((width, width), BF16),
        ],
    )
    column_pairs = call(
        backward_kernel, "backward", [shape(2, slab, width)] * half,
        [SMEM] + [VMEM] * 3, (me, adj, cot_near, cot_other),
        scratch=[pltpu.VMEM((rows, width), BF16), pltpu.VMEM((cols, width), BF16)],
    )
    chunks, pieces = outs[: col_devices - 1], outs[col_devices - 1 : -1]
    first = swap(outs[-1], "col", 1)

    column_keep, column_send = call(
        pair_sum_kernel, "pair_sum", [shape(slab, width, dtype=F32), shape(slab, width)],
        [VMEM] * half, exchange(column_pairs, "row")[::-1], micros=5,
    )
    def fetch(arrays):
        return [arrays[0]] + [swap(arrays[k - 1], "col", k) for k in range(2, col_devices)]

    grad_col = call(
        lambda *refs: col_kernel(*refs, terms=col_devices - 1), "grad_col", shape(piece, width),
        [VMEM] * col_devices + [ANY], (first, *fetch(pieces), column_send),
    )
    near_terms = exchange([grad_col] * half, "row")
    row_got = fetch([chunks[0], *hold(chunks[1:], near_terms[3], "hold_chunks")])
    both = call(
        lambda *refs: near_kernel(*refs, terms=half), "grad_near", shape(slab + piece, width),
        [VMEM] * (1 + half), (column_send, *near_terms),
    )
    both_far = swap(both, "row", half)
    grad_row = call(
        row_kernel, "grad_row", shape(piece, width), [VMEM] * 2, (both, both_far)
    )
    layer_out, feature_grad = call(
        output_kernel, "outputs", [shape(slab, width)] * 2, [VMEM] * (3 + col_devices),
        (weight, column_keep, both_far, first, *row_got),
    )
    gathered = call(
        gather_kernel, "weight_grad", shape(width, width), [SMEM] + [VMEM] * col_devices,
        (me, *exchange([grad_row] * col_devices, "col")),
    )
    weight_grad = gathered.astype(F32) * (1.0 / math.sqrt(row_devices * col_devices * slab))
    return (layer_out[None], feature_grad[None], weight_grad)


def solution(mesh):
    placed = (
        P("col", "row", None),
        P(),
        P("row", "col", None, None, None),
        P("row", "col", None),
        P("row", "col"),
        P("row", "col", None),
    )
    return jax.shard_map(
        body,
        mesh=mesh,
        in_specs=placed,
        out_specs=(P("row", "col", None), P("col", "row", None), P()),
        check_vma=False,
    )
```

```python
import math

import jax
import jax.numpy as jnp
from jax import lax
from jax.experimental import pallas as pl
from jax.experimental.pallas import tpu as pltpu
from jax.sharding import PartitionSpec as P

F32 = jnp.float32
BF16 = jnp.bfloat16
VMEM = pl.BlockSpec(memory_space=pltpu.VMEM)
SMEM = pl.BlockSpec(memory_space=pltpu.SMEM)
ANY = pl.BlockSpec(memory_space=pl.ANY)


def hint(microseconds):
    return pl.CostEstimate(
        flops=int(microseconds * 1e9), bytes_accessed=int(microseconds * 3.6e6), transcendentals=0
    )


def shape(*dims, dtype=BF16):
    return jax.ShapeDtypeStruct(dims, dtype)


def rows_of(index, slab):
    return pl.ds(pl.multiple_of(index * slab, slab), slab)


def summed(refs):
    total = refs[0][...].astype(F32)
    for ref in refs[1:]:
        total = total + ref[...].astype(F32)
    return total


def dense_kernel(meta_ref, tiles_ref, adj_ref, sems):
    slot_count, tile, _ = tiles_ref.shape
    col_tiles = adj_ref.shape[1] // tile
    live = jnp.minimum(meta_ref[2], slot_count)
    adj_ref[...] = jnp.zeros_like(adj_ref)

    def copy(k):
        slot = meta_ref[3 + k]
        row = pl.multiple_of((slot // col_tiles) * tile, tile)
        col = pl.multiple_of((slot % col_tiles) * tile, tile)
        place = adj_ref.at[pl.ds(row, tile), pl.ds(col, tile)]
        return pltpu.make_async_copy(tiles_ref.at[k], place, sems.at[k])

    def start(k, carry):
        copy(k).start()
        return carry

    def wait(k, carry):
        copy(k).wait()
        return carry

    lax.fori_loop(0, live, start, 0)
    lax.fori_loop(0, live, wait, 0)


def stack_kernel(*refs):
    out_ref = refs[-1]
    for k in range(out_ref.shape[0]):
        out_ref[k] = refs[k][...]


def place_cots(meta_ref, near_ref, other_ref, out_ref):
    slab = near_ref.shape[1]
    for k in range(near_ref.shape[0]):
        out_ref[rows_of(meta_ref[1] ^ (2 * k), slab), :] = near_ref[k]
        out_ref[rows_of(meta_ref[1] ^ (2 * k + 1), slab), :] = other_ref[k]


def forward_kernel(meta_ref, adj_ref, near_ref, other_ref, *refs, half):
    pair_refs, (*out_refs, both_ref, column, cots, part, grad) = refs[:half], refs[half:]
    slab = near_ref.shape[1]
    others = len(out_refs) // 2
    piece = both_ref.shape[0] - slab
    place_cots(meta_ref, near_ref, other_ref, cots)
    for k, ref in enumerate(pair_refs[::-1]):
        column[rows_of(meta_ref[0] ^ k, slab), :] = ref[0]
        column[rows_of(meta_ref[0] ^ k ^ half, slab), :] = ref[1]
    product = jnp.dot(adj_ref[...], column[...], preferred_element_type=F32).astype(BF16)
    part[...] = product
    grad[...] = lax.dot_general(
        product, cots[...], (((0,), (0,)), ((), ())), preferred_element_type=F32
    ).astype(BF16)
    for n in range(others):
        k = n + 1 if n else 0
        out_refs[n][...] = part[rows_of(meta_ref[1] ^ k, slab), :]
        out_refs[others + n][...] = grad[rows_of(meta_ref[1] ^ k, piece), :]
    both_ref[:slab, :] = part[rows_of(meta_ref[1] ^ 1, slab), :]
    both_ref[slab:, :] = grad[rows_of(meta_ref[1] ^ 1, piece), :]


def backward_kernel(meta_ref, adj_ref, near_ref, other_ref, *refs):
    *pair_refs, cots, total = refs
    half, slab = len(pair_refs), pair_refs[0].shape[1]
    place_cots(meta_ref, near_ref, other_ref, cots)
    total[...] = lax.dot_general(
        adj_ref[...], cots[...], (((0,), (0,)), ((), ())), preferred_element_type=F32
    ).astype(BF16)
    for k, ref in enumerate(pair_refs):
        ref[0] = total[rows_of(meta_ref[0] ^ k, slab), :]
        ref[1] = total[rows_of(meta_ref[0] ^ k ^ half, slab), :]


def pair_sum_kernel(*refs):
    *pair_refs, keep_ref, send_ref = refs
    total = summed(pair_refs)
    keep_ref[...] = total[0]
    send_ref[...] = total[1].astype(BF16)


def weighted(weight_ref, term_refs, contract):
    return lax.dot_general(
        summed(term_refs).astype(BF16),
        weight_ref[...],
        (((1,), (contract,)), ((), ())),
        preferred_element_type=F32,
    ).astype(BF16)


def output_kernel(weight_ref, keep_ref, far_ref, first_ref, *refs):
    *chunk_refs, layer_ref, feature_ref = refs
    slab = layer_ref.shape[0]
    layer_ref[...] = weighted(weight_ref, [first_ref.at[:slab, :], *chunk_refs], 0)
    feature_ref[...] = weighted(weight_ref, [keep_ref, far_ref.at[:slab, :]], 1)


def col_kernel(first_ref, *refs, terms):
    out_ref = refs[-1]
    first_ref = first_ref.at[first_ref.shape[0] - out_ref.shape[0] :, :]
    out_ref[...] = summed([first_ref, *refs[:terms]]).astype(BF16)


def hold_kernel(*refs):
    count = len(refs) // 2
    for src_ref, dst_ref in zip(refs[:count], refs[count + 1 :]):
        dst_ref[...] = src_ref[...]


def near_kernel(send_ref, *refs, terms):
    slab = send_ref.shape[0]
    refs[-1][:slab, :] = send_ref[...]
    refs[-1][slab:, :] = summed(refs[:terms]).astype(BF16)


def row_kernel(held_ref, got_ref, out_ref):
    slab = held_ref.shape[0] - out_ref.shape[0]
    out_ref[...] = summed([held_ref.at[slab:, :], got_ref.at[slab:, :]]).astype(BF16)


def gather_kernel(meta_ref, *refs):
    *piece_refs, out_ref = refs
    piece = piece_refs[0].shape[0]
    for k, ref in enumerate(piece_refs):
        out_ref[rows_of(meta_ref[1] ^ k, piece), :] = ref[...]


def swap(array, axis, distance):
    pairs = [(i, i ^ distance) for i in range(lax.axis_size(axis))]
    return lax.ppermute(array, axis, pairs)


def exchange(chunks, axis, stride=1):
    return [chunks[0]] + [swap(chunks[k], axis, k * stride) for k in range(1, len(chunks))]


def body(features, weight, tile_values, tile_slots, tile_counts, cotangent):
    row_devices = lax.axis_size("row")
    col_devices = lax.axis_size("col")
    half = row_devices // 2
    slots, tile = tile_values.shape[2:4]
    slab, width = features.shape[1:]
    rows, cols = col_devices * slab, row_devices * slab
    piece = width // col_devices
    place = jnp.stack([lax.axis_index("row"), lax.axis_index("col")]).astype(jnp.int32)
    me = jnp.concatenate([place, tile_counts[0], tile_slots[0, 0]])

    def call(kernel, name, out_shape, in_specs, args, scratch=(), micros=None):
        many = isinstance(out_shape, list)
        return pl.pallas_call(
            kernel,
            out_shape=out_shape,
            in_specs=in_specs,
            out_specs=[VMEM] * len(out_shape) if many else VMEM,
            scratch_shapes=scratch,
            compiler_params=pltpu.CompilerParams(
                vmem_limit_bytes=min(8 * 2**20 + 6 * rows * cols, 56 * 2**20)
            ),
            cost_estimate=None if micros is None else hint(micros),
            name=name,
        )(*args)

    own = features[0]
    far = swap(own, "row", half)
    adj = call(
        dense_kernel, "dense", shape(rows, cols), [SMEM, ANY], (me, tile_values[0, 0]),
        scratch=[pltpu.SemaphoreType.DMA((slots,))],
    )

    def hold(arrays, after, name):
        return call(
            hold_kernel, name, [shape(*array.shape) for array in arrays],
            [VMEM] * len(arrays) + [ANY], (*arrays, after),
        )

    def stack(arrays, name, after=()):
        return call(
            stack_kernel, name, shape(len(arrays), slab, width),
            [VMEM] * len(arrays) + [ANY] * len(after), (*arrays, *after), micros=3,
        )

    kept = hold([own, cotangent[0]], me, "own")
    pair = stack([kept[0], far], "pair")
    features_got = exchange([pair] * half, "row")
    cot_near = stack(
        [kept[1]] + exchange([cotangent[0]] * (col_devices // 2), "col", 2)[1:], "cot_near"
    )
    cot_other = swap(cot_near, "col", 1)

    outs = call(
        lambda *refs: forward_kernel(*refs, half=half), "forward",
        [shape(slab, width)] * (col_devices - 1)
        + [shape(piece, width)] * (col_devices - 1)
        + [shape(slab + piece, width)],
        [SMEM] + [VMEM] * (3 + half), (me, adj, cot_near, cot_other, *features_got[::-1]),
        scratch=[
            pltpu.VMEM((cols, width), BF16),
            pltpu.VMEM((rows, width), BF16),
            pltpu.VMEM((rows, width), BF16),
            pltpu.VMEM((width, width), BF16),
        ],
    )
    column_pairs = call(
        backward_kernel, "backward", [shape(2, slab, width)] * half,
        [SMEM] + [VMEM] * 3, (me, adj, cot_near, cot_other),
        scratch=[pltpu.VMEM((rows, width), BF16), pltpu.VMEM((cols, width), BF16)],
    )
    chunks, pieces = outs[: col_devices - 1], outs[col_devices - 1 : -1]
    first = swap(outs[-1], "col", 1)

    column_keep, column_send = call(
        pair_sum_kernel, "pair_sum", [shape(slab, width, dtype=F32), shape(slab, width)],
        [VMEM] * half, exchange(column_pairs, "row")[::-1], micros=5,
    )
    def fetch(arrays):
        return [arrays[0]] + [swap(arrays[k - 1], "col", k) for k in range(2, col_devices)]

    grad_col = call(
        lambda *refs: col_kernel(*refs, terms=col_devices - 1), "grad_col", shape(piece, width),
        [VMEM] * col_devices + [ANY], (first, *fetch(pieces), column_send),
    )
    near_terms = exchange([grad_col] * half, "row")
    row_got = fetch([chunks[0], *hold(chunks[1:], near_terms[3], "hold_chunks")])
    both = call(
        lambda *refs: near_kernel(*refs, terms=half), "grad_near", shape(slab + piece, width),
        [VMEM] * (1 + half), (column_send, *near_terms),
    )
    both_far = swap(both, "row", half)
    grad_row = call(
        row_kernel, "grad_row", shape(piece, width), [VMEM] * 2, (both, both_far)
    )
    layer_out, feature_grad = call(
        output_kernel, "outputs", [shape(slab, width)] * 2, [VMEM] * (3 + col_devices),
        (weight, column_keep, both_far, first, *row_got),
    )
    gathered = call(
        gather_kernel, "weight_grad", shape(width, width), [SMEM] + [VMEM] * col_devices,
        (me, *exchange([grad_row] * col_devices, "col")),
    )
    weight_grad = gathered.astype(F32) * (1.0 / math.sqrt(row_devices * col_devices * slab))
    return (layer_out[None], feature_grad[None], weight_grad)


def solution(mesh):
    placed = (
        P("col", "row", None),
        P(),
        P("row", "col", None, None, None),
        P("row", "col", None),
        P("row", "col"),
        P("row", "col", None),
    )
    return jax.shard_map(
        body,
        mesh=mesh,
        in_specs=placed,
        out_specs=(P("row", "col", None), P("col", "row", None), P()),
        check_vma=False,
    )
```

```python
import math

import jax
import jax.numpy as jnp
from jax import lax
from jax.experimental import pallas as pl
from jax.experimental.pallas import tpu as pltpu
from jax.sharding import PartitionSpec as P

F32 = jnp.float32
BF16 = jnp.bfloat16
VMEM = pl.BlockSpec(memory_space=pltpu.VMEM)
SMEM = pl.BlockSpec(memory_space=pltpu.SMEM)
ANY = pl.BlockSpec(memory_space=pl.ANY)


def hint(microseconds):
    return pl.CostEstimate(
        flops=int(microseconds * 1e9), bytes_accessed=int(microseconds * 3.6e6), transcendentals=0
    )


def shape(*dims, dtype=BF16):
    return jax.ShapeDtypeStruct(dims, dtype)


def rows_of(index, slab):
    return pl.ds(pl.multiple_of(index * slab, slab), slab)


def summed(refs):
    total = refs[0][...].astype(F32)
    for ref in refs[1:]:
        total = total + ref[...].astype(F32)
    return total


def dense_kernel(meta_ref, tiles_ref, adj_ref, sems):
    slot_count, tile, _ = tiles_ref.shape
    col_tiles = adj_ref.shape[1] // tile
    live = jnp.minimum(meta_ref[0], slot_count)
    adj_ref[...] = jnp.zeros_like(adj_ref)

    def copy(k):
        slot = meta_ref[1 + k]
        row = pl.multiple_of((slot // col_tiles) * tile, tile)
        col = pl.multiple_of((slot % col_tiles) * tile, tile)
        place = adj_ref.at[pl.ds(row, tile), pl.ds(col, tile)]
        return pltpu.make_async_copy(tiles_ref.at[k], place, sems.at[k])

    def start(k, carry):
        copy(k).start()
        return carry

    def wait(k, carry):
        copy(k).wait()
        return carry

    lax.fori_loop(0, live, start, 0)
    lax.fori_loop(0, live, wait, 0)


def stack_kernel(*refs):
    out_ref = refs[-1]
    for k in range(out_ref.shape[0]):
        out_ref[k] = refs[k][...]


def place_cots(near_ref, other_ref, out_ref):
    slab = near_ref.shape[1]
    for k in range(near_ref.shape[0]):
        out_ref[rows_of(lax.axis_index("col") ^ (2 * k), slab), :] = near_ref[k]
        out_ref[rows_of(lax.axis_index("col") ^ (2 * k + 1), slab), :] = other_ref[k]


def forward_kernel(adj_ref, near_ref, other_ref, *refs, half):
    pair_refs, (*out_refs, both_ref, column, cots, part, grad) = refs[:half], refs[half:]
    slab = near_ref.shape[1]
    others = len(out_refs) // 2
    piece = both_ref.shape[0] - slab
    place_cots(near_ref, other_ref, cots)
    for k, ref in enumerate(pair_refs):
        column[rows_of(lax.axis_index("row") ^ k, slab), :] = ref[0]
        column[rows_of(lax.axis_index("row") ^ k ^ half, slab), :] = ref[1]
    product = jnp.dot(adj_ref[...], column[...], preferred_element_type=F32).astype(BF16)
    part[...] = product
    grad[...] = lax.dot_general(
        product, cots[...], (((0,), (0,)), ((), ())), preferred_element_type=F32
    ).astype(BF16)
    for n in range(others):
        k = n + 1 if n else 0
        out_refs[n][...] = part[rows_of(lax.axis_index("col") ^ k, slab), :]
        out_refs[others + n][...] = grad[rows_of(lax.axis_index("col") ^ k, piece), :]
    both_ref[:slab, :] = part[rows_of(lax.axis_index("col") ^ 1, slab), :]
    both_ref[slab:, :] = grad[rows_of(lax.axis_index("col") ^ 1, piece), :]


def backward_kernel(adj_ref, near_ref, other_ref, *refs):
    *pair_refs, cots, total = refs
    half, slab = len(pair_refs), pair_refs[0].shape[1]
    place_cots(near_ref, other_ref, cots)
    total[...] = lax.dot_general(
        adj_ref[...], cots[...], (((0,), (0,)), ((), ())), preferred_element_type=F32
    ).astype(BF16)
    for k, ref in enumerate(pair_refs):
        ref[0] = total[rows_of(lax.axis_index("row") ^ k, slab), :]
        ref[1] = total[rows_of(lax.axis_index("row") ^ k ^ half, slab), :]


def pair_sum_kernel(*refs):
    *pair_refs, keep_ref, send_ref = refs
    total = summed(pair_refs)
    keep_ref[...] = total[0]
    send_ref[...] = total[1].astype(BF16)


def weighted(weight_ref, term_refs, contract):
    return lax.dot_general(
        summed(term_refs).astype(BF16),
        weight_ref[...],
        (((1,), (contract,)), ((), ())),
        preferred_element_type=F32,
    ).astype(BF16)


def output_kernel(weight_ref, keep_ref, far_ref, first_ref, *refs):
    *chunk_refs, layer_ref, feature_ref = refs
    slab = layer_ref.shape[0]
    layer_ref[...] = weighted(weight_ref, [first_ref.at[:slab, :], *chunk_refs], 0)
    feature_ref[...] = weighted(weight_ref, [keep_ref, far_ref.at[:slab, :]], 1)


def col_kernel(first_ref, *refs, terms):
    out_ref = refs[-1]
    first_ref = first_ref.at[first_ref.shape[0] - out_ref.shape[0] :, :]
    out_ref[...] = summed([first_ref, *refs[:terms]]).astype(BF16)


def hold_kernel(*refs):
    count = len(refs) // 2
    for src_ref, dst_ref in zip(refs[:count], refs[count + 1 :]):
        dst_ref[...] = src_ref[...]


def near_kernel(send_ref, *refs, terms):
    slab = send_ref.shape[0]
    refs[-1][:slab, :] = send_ref[...]
    refs[-1][slab:, :] = summed(refs[:terms]).astype(BF16)


def row_kernel(held_ref, got_ref, out_ref):
    slab = held_ref.shape[0] - out_ref.shape[0]
    out_ref[...] = summed([held_ref.at[slab:, :], got_ref.at[slab:, :]]).astype(BF16)


def gather_kernel(*refs):
    *piece_refs, out_ref = refs
    piece = piece_refs[0].shape[0]
    for k, ref in enumerate(piece_refs):
        out_ref[rows_of(lax.axis_index("col") ^ k, piece), :] = ref[...]


def swap(array, axis, distance):
    pairs = [(i, i ^ distance) for i in range(lax.axis_size(axis))]
    return lax.ppermute(array, axis, pairs)


def exchange(chunks, axis, stride=1):
    return [chunks[0]] + [swap(chunks[k], axis, k * stride) for k in range(1, len(chunks))]


def body(features, weight, tile_values, tile_slots, tile_counts, cotangent):
    row_devices = lax.axis_size("row")
    col_devices = lax.axis_size("col")
    half = row_devices // 2
    slots, tile = tile_values.shape[2:4]
    slab, width = features.shape[1:]
    rows, cols = col_devices * slab, row_devices * slab
    piece = width // col_devices
    live = jnp.concatenate([tile_counts[0], tile_slots[0, 0]])

    def call(kernel, name, out_shape, in_specs, args, scratch=(), micros=None):
        many = isinstance(out_shape, list)
        return pl.pallas_call(
            kernel,
            out_shape=out_shape,
            in_specs=in_specs,
            out_specs=[VMEM] * len(out_shape) if many else VMEM,
            scratch_shapes=scratch,
            compiler_params=pltpu.CompilerParams(
                vmem_limit_bytes=min(8 * 2**20 + 6 * rows * cols, 56 * 2**20)
            ),
            cost_estimate=None if micros is None else hint(micros),
            name=name,
        )(*args)

    own = features[0]
    far = swap(own, "row", half)
    adj = call(
        dense_kernel, "dense", shape(rows, cols), [SMEM, ANY], (live, tile_values[0, 0]),
        scratch=[pltpu.SemaphoreType.DMA((slots,))],
    )

    def hold(arrays, after, name):
        return call(
            hold_kernel, name, [shape(*array.shape) for array in arrays],
            [VMEM] * len(arrays) + [ANY], (*arrays, after),
        )

    def stack(arrays, name, after=()):
        return call(
            stack_kernel, name, shape(len(arrays), slab, width),
            [VMEM] * len(arrays) + [ANY] * len(after), (*arrays, *after), micros=3,
        )

    kept = hold([own, cotangent[0]], live, "own")
    pair = stack([kept[0], far], "pair")
    features_got = exchange([pair] * half, "row")
    cot_near = stack(
        [kept[1]] + exchange([cotangent[0]] * (col_devices // 2), "col", 2)[1:], "cot_near"
    )
    cot_other = swap(cot_near, "col", 1)

    outs = call(
        lambda *refs: forward_kernel(*refs, half=half), "forward",
        [shape(slab, width)] * (col_devices - 1)
        + [shape(piece, width)] * (col_devices - 1)
        + [shape(slab + piece, width)],
        [VMEM] * (3 + half), (adj, cot_near, cot_other, *features_got),
        scratch=[
            pltpu.VMEM((cols, width), BF16),
            pltpu.VMEM((rows, width), BF16),
            pltpu.VMEM((rows, width), BF16),
            pltpu.VMEM((width, width), BF16),
        ],
    )
    column_pairs = call(
        backward_kernel, "backward", [shape(2, slab, width)] * half,
        [VMEM] * 3, (adj, cot_near, cot_other),
        scratch=[pltpu.VMEM((rows, width), BF16), pltpu.VMEM((cols, width), BF16)],
    )
    chunks, pieces = outs[: col_devices - 1], outs[col_devices - 1 : -1]
    first = swap(outs[-1], "col", 1)

    column_keep, column_send = call(
        pair_sum_kernel, "pair_sum", [shape(slab, width, dtype=F32), shape(slab, width)],
        [VMEM] * half, exchange(column_pairs, "row")[::-1], micros=5,
    )
    def fetch(arrays):
        return [arrays[0]] + [swap(arrays[k - 1], "col", k) for k in range(2, col_devices)]

    grad_col = call(
        lambda *refs: col_kernel(*refs, terms=col_devices - 1), "grad_col", shape(piece, width),
        [VMEM] * col_devices + [ANY], (first, *fetch(pieces), column_send),
    )
    near_terms = exchange([grad_col] * half, "row")
    row_got = fetch([chunks[0], *hold(chunks[1:], near_terms[3], "hold_chunks")])
    both = call(
        lambda *refs: near_kernel(*refs, terms=half), "grad_near", shape(slab + piece, width),
        [VMEM] * (1 + half), (column_send, *near_terms),
    )
    both_far = swap(both, "row", half)
    grad_row = call(
        row_kernel, "grad_row", shape(piece, width), [VMEM] * 2, (both, both_far)
    )
    layer_out, feature_grad = call(
        output_kernel, "outputs", [shape(slab, width)] * 2, [VMEM] * (3 + col_devices),
        (weight, column_keep, both_far, first, *row_got),
    )
    gathered = call(
        gather_kernel, "weight_grad", shape(width, width), [VMEM] * col_devices,
        exchange([grad_row] * col_devices, "col"),
    )
    weight_grad = gathered.astype(F32) * (1.0 / math.sqrt(row_devices * col_devices * slab))
    return (layer_out[None], feature_grad[None], weight_grad)


def solution(mesh):
    placed = (
        P("col", "row", None),
        P(),
        P("row", "col", None, None, None),
        P("row", "col", None),
        P("row", "col"),
        P("row", "col", None),
    )
    return jax.shard_map(
        body,
        mesh=mesh,
        in_specs=placed,
        out_specs=(P("row", "col", None), P("col", "row", None), P()),
        check_vma=False,
    )
```

```python
import math

import jax
import jax.numpy as jnp
from jax import lax
from jax.experimental import pallas as pl
from jax.experimental.pallas import tpu as pltpu
from jax.sharding import PartitionSpec as P

F32 = jnp.float32
BF16 = jnp.bfloat16
VMEM = pl.BlockSpec(memory_space=pltpu.VMEM)
SMEM = pl.BlockSpec(memory_space=pltpu.SMEM)
ANY = pl.BlockSpec(memory_space=pl.ANY)


def hint(microseconds):
    return pl.CostEstimate(
        flops=int(microseconds * 1e9), bytes_accessed=int(microseconds * 3.6e6), transcendentals=0
    )


def shape(*dims, dtype=BF16):
    return jax.ShapeDtypeStruct(dims, dtype)


def rows_of(index, slab):
    return pl.ds(pl.multiple_of(index * slab, slab), slab)


def summed(refs):
    total = refs[0][...].astype(F32)
    for ref in refs[1:]:
        total = total + ref[...].astype(F32)
    return total


def dense_kernel(meta_ref, tiles_ref, adj_ref, sems):
    slot_count, tile, _ = tiles_ref.shape
    col_tiles = adj_ref.shape[1] // tile
    live = jnp.minimum(meta_ref[0], slot_count)
    adj_ref[...] = jnp.zeros_like(adj_ref)

    def copy(k):
        slot = meta_ref[1 + k]
        row = pl.multiple_of((slot // col_tiles) * tile, tile)
        col = pl.multiple_of((slot % col_tiles) * tile, tile)
        place = adj_ref.at[pl.ds(row, tile), pl.ds(col, tile)]
        return pltpu.make_async_copy(tiles_ref.at[k], place, sems.at[k])

    def start(k, carry):
        copy(k).start()
        return carry

    def wait(k, carry):
        copy(k).wait()
        return carry

    lax.fori_loop(0, live, start, 0)
    lax.fori_loop(0, live, wait, 0)


def stack_kernel(*refs):
    out_ref = refs[-1]
    for k in range(out_ref.shape[0]):
        out_ref[k] = refs[k][...]


def place_cots(near_ref, other_ref, out_ref):
    slab = near_ref.shape[1]
    for k in range(near_ref.shape[0]):
        out_ref[rows_of(lax.axis_index("col") ^ (2 * k), slab), :] = near_ref[k]
        out_ref[rows_of(lax.axis_index("col") ^ (2 * k + 1), slab), :] = other_ref[k]


def forward_kernel(adj_ref, near_ref, other_ref, *refs, half):
    shard_refs, refs = refs[: 2 * half], refs[2 * half :]
    *out_refs, both_ref, column, cots, part, grad = refs
    slab = near_ref.shape[1]
    others = len(out_refs) // 2
    piece = both_ref.shape[0] - slab
    place_cots(near_ref, other_ref, cots)
    for k, ref in enumerate(shard_refs):
        column[rows_of(lax.axis_index("row") ^ k, slab), :] = ref[...]
    product = jnp.dot(adj_ref[...], column[...], preferred_element_type=F32).astype(BF16)
    part[...] = product
    grad[...] = lax.dot_general(
        product, cots[...], (((0,), (0,)), ((), ())), preferred_element_type=F32
    ).astype(BF16)
    for n in range(others):
        k = n + 1 if n else 0
        out_refs[n][...] = part[rows_of(lax.axis_index("col") ^ k, slab), :]
        out_refs[others + n][...] = grad[rows_of(lax.axis_index("col") ^ k, piece), :]
    both_ref[:slab, :] = part[rows_of(lax.axis_index("col") ^ 1, slab), :]
    both_ref[slab:, :] = grad[rows_of(lax.axis_index("col") ^ 1, piece), :]


def backward_kernel(adj_ref, near_ref, other_ref, *refs):
    *pair_refs, cots, total = refs
    half, slab = len(pair_refs), pair_refs[0].shape[1]
    place_cots(near_ref, other_ref, cots)
    total[...] = lax.dot_general(
        adj_ref[...], cots[...], (((0,), (0,)), ((), ())), preferred_element_type=F32
    ).astype(BF16)
    for k, ref in enumerate(pair_refs):
        ref[0] = total[rows_of(lax.axis_index("row") ^ k, slab), :]
        ref[1] = total[rows_of(lax.axis_index("row") ^ k ^ half, slab), :]


def pair_sum_kernel(*refs):
    *pair_refs, keep_ref, send_ref = refs
    total = summed(pair_refs)
    keep_ref[...] = total[0]
    send_ref[...] = total[1].astype(BF16)


def weighted(weight_ref, term_refs, contract):
    return lax.dot_general(
        summed(term_refs).astype(BF16),
        weight_ref[...],
        (((1,), (contract,)), ((), ())),
        preferred_element_type=F32,
    ).astype(BF16)


def output_kernel(weight_ref, keep_ref, far_ref, first_ref, *refs):
    *chunk_refs, layer_ref, feature_ref = refs
    slab = layer_ref.shape[0]
    layer_ref[...] = weighted(weight_ref, [first_ref.at[:slab, :], *chunk_refs], 0)
    feature_ref[...] = weighted(weight_ref, [keep_ref, far_ref.at[:slab, :]], 1)


def col_kernel(first_ref, *refs, terms):
    out_ref = refs[-1]
    first_ref = first_ref.at[first_ref.shape[0] - out_ref.shape[0] :, :]
    out_ref[...] = summed([first_ref, *refs[:terms]]).astype(BF16)


def hold_kernel(*refs):
    count = len(refs) // 2
    for src_ref, dst_ref in zip(refs[:count], refs[count + 1 :]):
        dst_ref[...] = src_ref[...]


def near_kernel(send_ref, *refs, terms):
    slab = send_ref.shape[0]
    refs[-1][:slab, :] = send_ref[...]
    refs[-1][slab:, :] = summed(refs[:terms]).astype(BF16)


def row_kernel(held_ref, got_ref, out_ref):
    slab = held_ref.shape[0] - out_ref.shape[0]
    out_ref[...] = summed([held_ref.at[slab:, :], got_ref.at[slab:, :]]).astype(BF16)


def gather_kernel(*refs):
    *piece_refs, out_ref = refs
    piece = piece_refs[0].shape[0]
    for k, ref in enumerate(piece_refs):
        out_ref[rows_of(lax.axis_index("col") ^ k, piece), :] = ref[...]


def swap(array, axis, distance):
    pairs = [(i, i ^ distance) for i in range(lax.axis_size(axis))]
    return lax.ppermute(array, axis, pairs)


def exchange(chunks, axis, stride=1):
    return [chunks[0]] + [swap(chunks[k], axis, k * stride) for k in range(1, len(chunks))]


def body(features, weight, tile_values, tile_slots, tile_counts, cotangent):
    row_devices = lax.axis_size("row")
    col_devices = lax.axis_size("col")
    half = row_devices // 2
    slots, tile = tile_values.shape[2:4]
    slab, width = features.shape[1:]
    rows, cols = col_devices * slab, row_devices * slab
    piece = width // col_devices
    live = jnp.concatenate([tile_counts[0], tile_slots[0, 0]])

    def call(kernel, name, out_shape, in_specs, args, scratch=(), micros=None):
        many = isinstance(out_shape, list)
        return pl.pallas_call(
            kernel,
            out_shape=out_shape,
            in_specs=in_specs,
            out_specs=[VMEM] * len(out_shape) if many else VMEM,
            scratch_shapes=scratch,
            compiler_params=pltpu.CompilerParams(
                vmem_limit_bytes=min(8 * 2**20 + 6 * rows * cols, 56 * 2**20)
            ),
            cost_estimate=None if micros is None else hint(micros),
            name=name,
        )(*args)

    own = features[0]
    far = swap(own, "row", half)
    adj = call(
        dense_kernel, "dense", shape(rows, cols), [SMEM, ANY], (live, tile_values[0, 0]),
        scratch=[pltpu.SemaphoreType.DMA((slots,))],
    )

    def hold(arrays, after, name):
        return call(
            hold_kernel, name, [shape(*array.shape) for array in arrays],
            [VMEM] * len(arrays) + [ANY], (*arrays, after),
        )

    def stack(arrays, name, after=()):
        return call(
            stack_kernel, name, shape(len(arrays), slab, width),
            [VMEM] * len(arrays) + [ANY] * len(after), (*arrays, *after), micros=3,
        )

    near = exchange([own] * half, "row")
    ready = stack([far], "ready", near[1:]).reshape(own.shape)
    shards = near + exchange([ready] * half, "row")
    (cot_own,) = hold([cotangent[0]], live, "own")
    cot_near = stack(
        [cot_own] + exchange([cotangent[0]] * (col_devices // 2), "col", 2)[1:], "cot_near"
    )
    cot_other = swap(cot_near, "col", 1)

    outs = call(
        lambda *refs: forward_kernel(*refs, half=half), "forward",
        [shape(slab, width)] * (col_devices - 1)
        + [shape(piece, width)] * (col_devices - 1)
        + [shape(slab + piece, width)],
        [VMEM] * (3 + 2 * half), (adj, cot_near, cot_other, *shards),
        scratch=[
            pltpu.VMEM((cols, width), BF16),
            pltpu.VMEM((rows, width), BF16),
            pltpu.VMEM((rows, width), BF16),
            pltpu.VMEM((width, width), BF16),
        ],
    )
    column_pairs = call(
        backward_kernel, "backward", [shape(2, slab, width)] * half,
        [VMEM] * 3, (adj, cot_near, cot_other),
        scratch=[pltpu.VMEM((rows, width), BF16), pltpu.VMEM((cols, width), BF16)],
    )
    chunks, pieces = outs[: col_devices - 1], outs[col_devices - 1 : -1]
    first = swap(outs[-1], "col", 1)

    column_keep, column_send = call(
        pair_sum_kernel, "pair_sum", [shape(slab, width, dtype=F32), shape(slab, width)],
        [VMEM] * half, exchange(column_pairs, "row")[::-1], micros=None,
    )
    def fetch(arrays):
        return [arrays[0]] + [swap(arrays[k - 1], "col", k) for k in range(2, col_devices)]

    grad_col = call(
        lambda *refs: col_kernel(*refs, terms=col_devices - 1), "grad_col", shape(piece, width),
        [VMEM] * col_devices + [ANY], (first, *fetch(pieces), column_send),
    )
    near_terms = exchange([grad_col] * half, "row")
    row_got = fetch([chunks[0], *hold(chunks[1:], near_terms[3], "hold_chunks")])
    both = call(
        lambda *refs: near_kernel(*refs, terms=half), "grad_near", shape(slab + piece, width),
        [VMEM] * (1 + half), (column_send, *near_terms),
    )
    both_far = swap(both, "row", half)
    grad_row = call(
        row_kernel, "grad_row", shape(piece, width), [VMEM] * 2, (both, both_far)
    )
    layer_out, feature_grad = call(
        output_kernel, "outputs", [shape(slab, width)] * 2, [VMEM] * (3 + col_devices),
        (weight, column_keep, both_far, first, *row_got),
    )
    gathered = call(
        gather_kernel, "weight_grad", shape(width, width), [VMEM] * col_devices,
        exchange([grad_row] * col_devices, "col"),
    )
    weight_grad = gathered.astype(F32) * (1.0 / math.sqrt(row_devices * col_devices * slab))
    return (layer_out[None], feature_grad[None], weight_grad)


def solution(mesh):
    placed = (
        P("col", "row", None),
        P(),
        P("row", "col", None, None, None),
        P("row", "col", None),
        P("row", "col"),
        P("row", "col", None),
    )
    return jax.shard_map(
        body,
        mesh=mesh,
        in_specs=placed,
        out_specs=(P("row", "col", None), P("col", "row", None), P()),
        check_vma=False,
    )
```

```python
import math

import jax
import jax.numpy as jnp
from jax import lax
from jax.experimental import pallas as pl
from jax.experimental.pallas import tpu as pltpu
from jax.sharding import PartitionSpec as P

F32 = jnp.float32
BF16 = jnp.bfloat16
VMEM = pl.BlockSpec(memory_space=pltpu.VMEM)
SMEM = pl.BlockSpec(memory_space=pltpu.SMEM)
ANY = pl.BlockSpec(memory_space=pl.ANY)


def hint(microseconds):
    return pl.CostEstimate(
        flops=int(microseconds * 1e9), bytes_accessed=int(microseconds * 3.6e6), transcendentals=0
    )


def shape(*dims, dtype=BF16):
    return jax.ShapeDtypeStruct(dims, dtype)


def rows_of(index, slab):
    return pl.ds(pl.multiple_of(index * slab, slab), slab)


def summed(refs):
    total = refs[0][...].astype(F32)
    for ref in refs[1:]:
        total = total + ref[...].astype(F32)
    return total


def dense_kernel(meta_ref, tiles_ref, adj_ref, sems):
    slot_count, tile, _ = tiles_ref.shape
    col_tiles = adj_ref.shape[1] // tile
    live = jnp.minimum(meta_ref[0], slot_count)
    adj_ref[...] = jnp.zeros_like(adj_ref)

    def copy(k):
        slot = meta_ref[1 + k]
        row = pl.multiple_of((slot // col_tiles) * tile, tile)
        col = pl.multiple_of((slot % col_tiles) * tile, tile)
        place = adj_ref.at[pl.ds(row, tile), pl.ds(col, tile)]
        return pltpu.make_async_copy(tiles_ref.at[k], place, sems.at[k])

    def start(k, carry):
        copy(k).start()
        return carry

    def wait(k, carry):
        copy(k).wait()
        return carry

    lax.fori_loop(0, live, start, 0)
    lax.fori_loop(0, live, wait, 0)


def stack_kernel(*refs):
    out_ref = refs[-1]
    for k in range(out_ref.shape[0]):
        out_ref[k] = refs[k][...]


def place_cots(near_ref, other_ref, out_ref):
    slab = near_ref.shape[1]
    for k in range(near_ref.shape[0]):
        out_ref[rows_of(lax.axis_index("col") ^ (2 * k), slab), :] = near_ref[k]
        out_ref[rows_of(lax.axis_index("col") ^ (2 * k + 1), slab), :] = other_ref[k]


def forward_kernel(adj_ref, near_ref, other_ref, *refs, half):
    pair_refs, (*out_refs, both_ref, column, cots, part, grad) = refs[:half], refs[half:]
    slab = near_ref.shape[1]
    others = len(out_refs) // 2
    piece = both_ref.shape[0] - slab
    place_cots(near_ref, other_ref, cots)
    for k, ref in enumerate(pair_refs):
        column[rows_of(lax.axis_index("row") ^ k, slab), :] = ref[0]
        column[rows_of(lax.axis_index("row") ^ k ^ half, slab), :] = ref[1]
    product = jnp.dot(adj_ref[...], column[...], preferred_element_type=F32).astype(BF16)
    part[...] = product
    grad[...] = lax.dot_general(
        product, cots[...], (((0,), (0,)), ((), ())), preferred_element_type=F32
    ).astype(BF16)
    for n in range(others):
        k = n + 1 if n else 0
        out_refs[n][...] = part[rows_of(lax.axis_index("col") ^ k, slab), :]
        out_refs[others + n][...] = grad[rows_of(lax.axis_index("col") ^ k, piece), :]
    both_ref[:slab, :] = part[rows_of(lax.axis_index("col") ^ 1, slab), :]
    both_ref[slab:, :] = grad[rows_of(lax.axis_index("col") ^ 1, piece), :]


def backward_kernel(adj_ref, near_ref, other_ref, *refs):
    *pair_refs, cots, total = refs
    half, slab = len(pair_refs), pair_refs[0].shape[1]
    place_cots(near_ref, other_ref, cots)
    total[...] = lax.dot_general(
        adj_ref[...], cots[...], (((0,), (0,)), ((), ())), preferred_element_type=F32
    ).astype(BF16)
    for k, ref in enumerate(pair_refs):
        ref[0] = total[rows_of(lax.axis_index("row") ^ k, slab), :]
        ref[1] = total[rows_of(lax.axis_index("row") ^ k ^ half, slab), :]


def pair_sum_kernel(*refs):
    *pair_refs, keep_ref, send_ref = refs
    total = summed(pair_refs)
    keep_ref[...] = total[0]
    send_ref[...] = total[1].astype(BF16)


def weighted(weight_ref, term_refs, contract):
    return lax.dot_general(
        summed(term_refs).astype(BF16),
        weight_ref[...],
        (((1,), (contract,)), ((), ())),
        preferred_element_type=F32,
    ).astype(BF16)


def output_kernel(weight_ref, keep_ref, far_ref, first_ref, *refs):
    *chunk_refs, layer_ref, feature_ref = refs
    slab = layer_ref.shape[0]
    layer_ref[...] = weighted(weight_ref, [first_ref.at[:slab, :], *chunk_refs], 0)
    feature_ref[...] = weighted(weight_ref, [keep_ref, far_ref.at[:slab, :]], 1)


def col_kernel(first_ref, *refs, terms):
    out_ref = refs[-1]
    first_ref = first_ref.at[first_ref.shape[0] - out_ref.shape[0] :, :]
    out_ref[...] = summed([first_ref, *refs[:terms]]).astype(BF16)


def hold_kernel(*refs, count):
    for src_ref, dst_ref in zip(refs[:count], refs[-count:]):
        dst_ref[...] = src_ref[...]


def near_kernel(send_ref, *refs, terms):
    slab = send_ref.shape[0]
    refs[-1][:slab, :] = send_ref[...]
    refs[-1][slab:, :] = summed(refs[:terms]).astype(BF16)


def row_kernel(held_ref, got_ref, out_ref):
    slab = held_ref.shape[0] - out_ref.shape[0]
    out_ref[...] = summed([held_ref.at[slab:, :], got_ref.at[slab:, :]]).astype(BF16)


def gather_kernel(*refs):
    *piece_refs, out_ref = refs
    piece = piece_refs[0].shape[0]
    for k, ref in enumerate(piece_refs):
        out_ref[rows_of(lax.axis_index("col") ^ k, piece), :] = ref[...]


def swap(array, axis, distance):
    pairs = [(i, i ^ distance) for i in range(lax.axis_size(axis))]
    return lax.ppermute(array, axis, pairs)


def exchange(chunks, axis, stride=1):
    return [chunks[0]] + [swap(chunks[k], axis, k * stride) for k in range(1, len(chunks))]


def body(features, weight, tile_values, tile_slots, tile_counts, cotangent):
    row_devices = lax.axis_size("row")
    col_devices = lax.axis_size("col")
    half = row_devices // 2
    slots, tile = tile_values.shape[2:4]
    slab, width = features.shape[1:]
    rows, cols = col_devices * slab, row_devices * slab
    piece = width // col_devices
    live = jnp.concatenate([tile_counts[0], tile_slots[0, 0]])

    def call(kernel, name, out_shape, in_specs, args, scratch=(), micros=None):
        many = isinstance(out_shape, list)
        return pl.pallas_call(
            kernel,
            out_shape=out_shape,
            in_specs=in_specs,
            out_specs=[VMEM] * len(out_shape) if many else VMEM,
            scratch_shapes=scratch,
            compiler_params=pltpu.CompilerParams(
                vmem_limit_bytes=min(8 * 2**20 + 6 * rows * cols, 56 * 2**20)
            ),
            cost_estimate=None if micros is None else hint(micros),
            name=name,
        )(*args)

    own = features[0]
    far = swap(own, "row", half)
    adj = call(
        dense_kernel, "dense", shape(rows, cols), [SMEM, ANY], (live, tile_values[0, 0]),
        scratch=[pltpu.SemaphoreType.DMA((slots,))],
    )

    def hold(arrays, after, name):
        return call(
            lambda *refs: hold_kernel(*refs, count=len(arrays)), name, [shape(*array.shape) for array in arrays],
            [VMEM] * len(arrays) + [ANY] * len(after), (*arrays, *after),
        )

    def stack(arrays, name, after=()):
        return call(
            stack_kernel, name, shape(len(arrays), slab, width),
            [VMEM] * len(arrays) + [ANY] * len(after), (*arrays, *after), micros=3,
        )

    kept = hold([own, cotangent[0]], [live], "own")
    pair = stack([kept[0], far], "pair")
    features_got = exchange([pair] * half, "row")
    cot_near = stack(
        [kept[1]] + exchange([cotangent[0]] * (col_devices // 2), "col", 2)[1:], "cot_near"
    )
    cot_other = swap(cot_near, "col", 1)

    outs = call(
        lambda *refs: forward_kernel(*refs, half=half), "forward",
        [shape(slab, width)] * (col_devices - 1)
        + [shape(piece, width)] * (col_devices - 1)
        + [shape(slab + piece, width)],
        [VMEM] * (3 + half), (adj, cot_near, cot_other, *features_got),
        scratch=[
            pltpu.VMEM((cols, width), BF16),
            pltpu.VMEM((rows, width), BF16),
            pltpu.VMEM((rows, width), BF16),
            pltpu.VMEM((width, width), BF16),
        ],
    )
    column_pairs = call(
        backward_kernel, "backward", [shape(2, slab, width)] * half,
        [VMEM] * 3, (adj, cot_near, cot_other),
        scratch=[pltpu.VMEM((rows, width), BF16), pltpu.VMEM((cols, width), BF16)],
    )
    chunks, pieces = outs[: col_devices - 1], outs[col_devices - 1 : -1]
    first = swap(outs[-1], "col", 1)

    def fetch(arrays):
        return [arrays[0]] + [swap(arrays[k - 1], "col", k) for k in range(2, col_devices)]

    grad_got = fetch(pieces)
    column_pairs = [*column_pairs[:1], *hold(column_pairs[1:2], [first, *grad_got[1:]], "hold_pair"), *column_pairs[2:]]
    column_got = exchange(column_pairs, "row")
    column_keep, column_send = call(
        pair_sum_kernel, "pair_sum", [shape(slab, width, dtype=F32), shape(slab, width)],
        [VMEM] * half, column_got[::-1], micros=5,
    )

    grad_col = call(
        lambda *refs: col_kernel(*refs, terms=col_devices - 1), "grad_col", shape(piece, width),
        [VMEM] * col_devices, (first, *grad_got),
    )
    near_terms = exchange([grad_col] * half, "row")
    row_got = fetch([chunks[0], *hold(chunks[1:], [near_terms[3]], "hold_chunks")])
    both = call(
        lambda *refs: near_kernel(*refs, terms=half), "grad_near", shape(slab + piece, width),
        [VMEM] * (1 + half), (column_send, *near_terms),
    )
    both_far = swap(both, "row", half)
    grad_row = call(
        row_kernel, "grad_row", shape(piece, width), [VMEM] * 2, (both, both_far)
    )
    layer_out, feature_grad = call(
        output_kernel, "outputs", [shape(slab, width)] * 2, [VMEM] * (3 + col_devices),
        (weight, column_keep, both_far, first, *row_got),
    )
    gathered = call(
        gather_kernel, "weight_grad", shape(width, width), [VMEM] * col_devices,
        exchange([grad_row] * col_devices, "col"),
    )
    weight_grad = gathered.astype(F32) * (1.0 / math.sqrt(row_devices * col_devices * slab))
    return (layer_out[None], feature_grad[None], weight_grad)


def solution(mesh):
    placed = (
        P("col", "row", None),
        P(),
        P("row", "col", None, None, None),
        P("row", "col", None),
        P("row", "col"),
        P("row", "col", None),
    )
    return jax.shard_map(
        body,
        mesh=mesh,
        in_specs=placed,
        out_specs=(P("row", "col", None), P("col", "row", None), P()),
        check_vma=False,
    )
```

```python
import math

import jax
import jax.numpy as jnp
from jax import lax
from jax.experimental import pallas as pl
from jax.experimental.pallas import tpu as pltpu
from jax.sharding import PartitionSpec as P

F32 = jnp.float32
BF16 = jnp.bfloat16
VMEM = pl.BlockSpec(memory_space=pltpu.VMEM)
SMEM = pl.BlockSpec(memory_space=pltpu.SMEM)
ANY = pl.BlockSpec(memory_space=pl.ANY)


def hint(microseconds):
    return pl.CostEstimate(
        flops=int(microseconds * 1e9), bytes_accessed=int(microseconds * 3.6e6), transcendentals=0
    )


def shape(*dims, dtype=BF16):
    return jax.ShapeDtypeStruct(dims, dtype)


def rows_of(index, slab):
    return pl.ds(pl.multiple_of(index * slab, slab), slab)


def summed(refs):
    total = refs[0][...].astype(F32)
    for ref in refs[1:]:
        total = total + ref[...].astype(F32)
    return total


def dense_kernel(meta_ref, tiles_ref, adj_ref, sems):
    slot_count, tile, _ = tiles_ref.shape
    col_tiles = adj_ref.shape[1] // tile
    live = jnp.minimum(meta_ref[0], slot_count)
    adj_ref[...] = jnp.zeros_like(adj_ref)

    def copy(k):
        slot = meta_ref[1 + k]
        row = pl.multiple_of((slot // col_tiles) * tile, tile)
        col = pl.multiple_of((slot % col_tiles) * tile, tile)
        place = adj_ref.at[pl.ds(row, tile), pl.ds(col, tile)]
        return pltpu.make_async_copy(tiles_ref.at[k], place, sems.at[k])

    def start(k, carry):
        copy(k).start()
        return carry

    def wait(k, carry):
        copy(k).wait()
        return carry

    lax.fori_loop(0, live, start, 0)
    lax.fori_loop(0, live, wait, 0)


def stack_kernel(*refs):
    out_ref = refs[-1]
    for k in range(out_ref.shape[0]):
        out_ref[k] = refs[k][...]


def place_cots(near_ref, other_ref, out_ref):
    slab = near_ref.shape[1]
    for k in range(near_ref.shape[0]):
        out_ref[rows_of(lax.axis_index("col") ^ (2 * k), slab), :] = near_ref[k]
        out_ref[rows_of(lax.axis_index("col") ^ (2 * k + 1), slab), :] = other_ref[k]


def forward_kernel(adj_ref, near_ref, other_ref, *refs, half):
    pair_refs, (*out_refs, both_ref, column, cots, part, grad) = refs[:half], refs[half:]
    slab = near_ref.shape[1]
    others = len(out_refs) // 2
    piece = both_ref.shape[0] - slab
    place_cots(near_ref, other_ref, cots)
    for k, ref in enumerate(pair_refs):
        column[rows_of(lax.axis_index("row") ^ k, slab), :] = ref[0]
        column[rows_of(lax.axis_index("row") ^ k ^ half, slab), :] = ref[1]
    product = jnp.dot(adj_ref[...], column[...], preferred_element_type=F32).astype(BF16)
    part[...] = product
    grad[...] = lax.dot_general(
        product, cots[...], (((0,), (0,)), ((), ())), preferred_element_type=F32
    ).astype(BF16)
    for n in range(others):
        k = n + 1 if n else 0
        out_refs[n][...] = part[rows_of(lax.axis_index("col") ^ k, slab), :]
        out_refs[others + n][...] = grad[rows_of(lax.axis_index("col") ^ k, piece), :]
    both_ref[:slab, :] = part[rows_of(lax.axis_index("col") ^ 1, slab), :]
    both_ref[slab:, :] = grad[rows_of(lax.axis_index("col") ^ 1, piece), :]


def backward_kernel(adj_ref, near_ref, other_ref, keep_ref, *refs):
    *send_refs, cots, total = refs
    slab = near_ref.shape[1]
    place_cots(near_ref, other_ref, cots)
    total[...] = lax.dot_general(
        adj_ref[...], cots[...], (((0,), (0,)), ((), ())), preferred_element_type=F32
    ).astype(BF16)
    sends = [ref.at[m] for ref in send_refs for m in range(ref.shape[0])]
    for m, send in enumerate(sends):
        keep_ref[m] = total[rows_of(lax.axis_index("row") ^ (2 * m), slab), :]
        send[...] = total[rows_of(lax.axis_index("row") ^ (2 * m + 1), slab), :]


def halve_kernel(held_ref, *refs, count):
    got_refs, (keep_ref, send_ref) = refs[:count], refs[-2:]
    got = [ref.at[m] for ref in got_refs for m in range(ref.shape[0])]
    for m in range(keep_ref.shape[0]):
        keep_ref[m] = summed([held_ref.at[2 * m], got[2 * m]]).astype(BF16)
        send_ref[m] = summed([held_ref.at[2 * m + 1], got[2 * m + 1]]).astype(BF16)


def weighted(weight_ref, term_refs, contract):
    return lax.dot_general(
        summed(term_refs).astype(BF16),
        weight_ref[...],
        (((1,), (contract,)), ((), ())),
        preferred_element_type=F32,
    ).astype(BF16)


def output_kernel(weight_ref, keep_ref, far_ref, first_ref, *refs):
    *chunk_refs, layer_ref, feature_ref = refs
    slab = layer_ref.shape[0]
    layer_ref[...] = weighted(weight_ref, [first_ref.at[:slab, :], *chunk_refs], 0)
    feature_ref[...] = weighted(weight_ref, [keep_ref, far_ref.at[:slab, :]], 1)


def col_kernel(first_ref, *refs, terms):
    out_ref = refs[-1]
    first_ref = first_ref.at[first_ref.shape[0] - out_ref.shape[0] :, :]
    out_ref[...] = summed([first_ref, *refs[:terms]]).astype(BF16)


def hold_kernel(*refs):
    count = len(refs) // 2
    for src_ref, dst_ref in zip(refs[:count], refs[count + 1 :]):
        dst_ref[...] = src_ref[...]


def near_kernel(send_ref, *refs, terms):
    slab = send_ref.shape[0]
    refs[-1][:slab, :] = send_ref[...]
    refs[-1][slab:, :] = summed(refs[:terms]).astype(BF16)


def row_kernel(held_ref, got_ref, out_ref):
    slab = held_ref.shape[0] - out_ref.shape[0]
    out_ref[...] = summed([held_ref.at[slab:, :], got_ref.at[slab:, :]]).astype(BF16)


def gather_kernel(*refs):
    *piece_refs, out_ref = refs
    piece = piece_refs[0].shape[0]
    for k, ref in enumerate(piece_refs):
        out_ref[rows_of(lax.axis_index("col") ^ k, piece), :] = ref[...]


def swap(array, axis, distance):
    pairs = [(i, i ^ distance) for i in range(lax.axis_size(axis))]
    return lax.ppermute(array, axis, pairs)


def exchange(chunks, axis, stride=1):
    return [chunks[0]] + [swap(chunks[k], axis, k * stride) for k in range(1, len(chunks))]


def body(features, weight, tile_values, tile_slots, tile_counts, cotangent):
    row_devices = lax.axis_size("row")
    col_devices = lax.axis_size("col")
    half = row_devices // 2
    slots, tile = tile_values.shape[2:4]
    slab, width = features.shape[1:]
    rows, cols = col_devices * slab, row_devices * slab
    piece = width // col_devices
    live = jnp.concatenate([tile_counts[0], tile_slots[0, 0]])

    def call(kernel, name, out_shape, in_specs, args, scratch=(), micros=None):
        many = isinstance(out_shape, list)
        return pl.pallas_call(
            kernel,
            out_shape=out_shape,
            in_specs=in_specs,
            out_specs=[VMEM] * len(out_shape) if many else VMEM,
            scratch_shapes=scratch,
            compiler_params=pltpu.CompilerParams(
                vmem_limit_bytes=min(8 * 2**20 + 6 * rows * cols, 56 * 2**20)
            ),
            cost_estimate=None if micros is None else hint(micros),
            name=name,
        )(*args)

    own = features[0]
    far = swap(own, "row", half)
    adj = call(
        dense_kernel, "dense", shape(rows, cols), [SMEM, ANY], (live, tile_values[0, 0]),
        scratch=[pltpu.SemaphoreType.DMA((slots,))],
    )

    def hold(arrays, after, name):
        return call(
            hold_kernel, name, [shape(*array.shape) for array in arrays],
            [VMEM] * len(arrays) + [ANY], (*arrays, after),
        )

    def stack(arrays, name, after=()):
        return call(
            stack_kernel, name, shape(len(arrays), slab, width),
            [VMEM] * len(arrays) + [ANY] * len(after), (*arrays, *after), micros=3,
        )

    kept = hold([own, cotangent[0]], live, "own")
    pair = stack([kept[0], far], "pair")
    features_got = exchange([pair] * half, "row")
    cot_near = stack(
        [kept[1]] + exchange([cotangent[0]] * (col_devices // 2), "col", 2)[1:], "cot_near"
    )
    cot_other = swap(cot_near, "col", 1)

    outs = call(
        lambda *refs: forward_kernel(*refs, half=half), "forward",
        [shape(slab, width)] * (col_devices - 1)
        + [shape(piece, width)] * (col_devices - 1)
        + [shape(slab + piece, width)],
        [VMEM] * (3 + half), (adj, cot_near, cot_other, *features_got),
        scratch=[
            pltpu.VMEM((cols, width), BF16),
            pltpu.VMEM((rows, width), BF16),
            pltpu.VMEM((rows, width), BF16),
            pltpu.VMEM((width, width), BF16),
        ],
    )
    keep, *send = call(
        backward_kernel, "backward",
        [shape(half, slab, width)] + [shape(half // 2, slab, width)] * 2,
        [VMEM] * 3, (adj, cot_near, cot_other),
        scratch=[pltpu.VMEM((rows, width), BF16), pltpu.VMEM((cols, width), BF16)],
    )
    chunks, pieces = outs[: col_devices - 1], outs[col_devices - 1 : -1]
    first = swap(outs[-1], "col", 1)

    def fetch(arrays):
        return [arrays[0]] + [swap(arrays[k - 1], "col", k) for k in range(2, col_devices)]

    grad_got = fetch(pieces)
    distance, after = 1, [first, *grad_got[1:]]
    while distance < half:
        got = [swap(array, "row", distance) for array in send]
        keep, *send = call(
            lambda *refs: halve_kernel(*refs, count=len(got)), "halve",
            [shape(half // (2 * distance), slab, width)] * 2,
            [VMEM] * (1 + len(got)) + [ANY] * len(after), (keep, *got, *after), micros=None,
        )
        distance, after = 2 * distance, []
    column_keep, column_send = keep[0], send[0][0]

    grad_col = call(
        lambda *refs: col_kernel(*refs, terms=col_devices - 1), "grad_col", shape(piece, width),
        [VMEM] * col_devices, (first, *grad_got),
    )
    near_terms = exchange([grad_col] * half, "row")
    row_got = fetch([chunks[0], *hold(chunks[1:], near_terms[3], "hold_chunks")])
    both = call(
        lambda *refs: near_kernel(*refs, terms=half), "grad_near", shape(slab + piece, width),
        [VMEM] * (1 + half), (column_send, *near_terms),
    )
    both_far = swap(both, "row", half)
    grad_row = call(
        row_kernel, "grad_row", shape(piece, width), [VMEM] * 2, (both, both_far)
    )
    layer_out, feature_grad = call(
        output_kernel, "outputs", [shape(slab, width)] * 2, [VMEM] * (3 + col_devices),
        (weight, column_keep, both_far, first, *row_got),
    )
    gathered = call(
        gather_kernel, "weight_grad", shape(width, width), [VMEM] * col_devices,
        exchange([grad_row] * col_devices, "col"),
    )
    weight_grad = gathered.astype(F32) * (1.0 / math.sqrt(row_devices * col_devices * slab))
    return (layer_out[None], feature_grad[None], weight_grad)


def solution(mesh):
    placed = (
        P("col", "row", None),
        P(),
        P("row", "col", None, None, None),
        P("row", "col", None),
        P("row", "col"),
        P("row", "col", None),
    )
    return jax.shard_map(
        body,
        mesh=mesh,
        in_specs=placed,
        out_specs=(P("row", "col", None), P("col", "row", None), P()),
        check_vma=False,
    )
```

```python
import math

import jax
import jax.numpy as jnp
from jax import lax
from jax.experimental import pallas as pl
from jax.experimental.pallas import tpu as pltpu
from jax.sharding import PartitionSpec as P

F32 = jnp.float32
BF16 = jnp.bfloat16
VMEM = pl.BlockSpec(memory_space=pltpu.VMEM)
SMEM = pl.BlockSpec(memory_space=pltpu.SMEM)
ANY = pl.BlockSpec(memory_space=pl.ANY)


def hint(microseconds):
    return pl.CostEstimate(
        flops=int(microseconds * 1e9), bytes_accessed=int(microseconds * 3.6e6), transcendentals=0
    )


def shape(*dims, dtype=BF16):
    return jax.ShapeDtypeStruct(dims, dtype)


def rows_of(index, slab):
    return pl.ds(pl.multiple_of(index * slab, slab), slab)


def summed(refs):
    total = refs[0][...].astype(F32)
    for ref in refs[1:]:
        total = total + ref[...].astype(F32)
    return total


def dense_kernel(slots_ref, count_ref, tiles_ref, adj_ref, sems):
    slot_count, tile, _ = tiles_ref.shape
    col_tiles = adj_ref.shape[1] // tile
    live = jnp.minimum(count_ref[0], slot_count)
    adj_ref[...] = jnp.zeros_like(adj_ref)

    def copy(k):
        slot = slots_ref[k]
        row = pl.multiple_of((slot // col_tiles) * tile, tile)
        col = pl.multiple_of((slot % col_tiles) * tile, tile)
        place = adj_ref.at[pl.ds(row, tile), pl.ds(col, tile)]
        return pltpu.make_async_copy(tiles_ref.at[k], place, sems.at[k])

    def start(k, carry):
        copy(k).start()
        return carry

    def wait(k, carry):
        copy(k).wait()
        return carry

    lax.fori_loop(0, live, start, 0)
    lax.fori_loop(0, live, wait, 0)


def stack_kernel(*refs):
    out_ref = refs[-1]
    for k in range(out_ref.shape[0]):
        out_ref[k] = refs[k][...]


def place_cots(near_ref, other_ref, out_ref):
    slab = near_ref.shape[1]
    for k in range(near_ref.shape[0]):
        out_ref[rows_of(lax.axis_index("col") ^ (2 * k), slab), :] = near_ref[k]
        out_ref[rows_of(lax.axis_index("col") ^ (2 * k + 1), slab), :] = other_ref[k]


def forward_kernel(adj_ref, near_ref, other_ref, *refs, half):
    pair_refs, (*out_refs, both_ref, column, cots, part, grad) = refs[:half], refs[half:]
    slab = near_ref.shape[1]
    others = len(out_refs) // 2
    piece = both_ref.shape[0] - slab
    place_cots(near_ref, other_ref, cots)
    for k, ref in enumerate(pair_refs):
        column[rows_of(lax.axis_index("row") ^ k, slab), :] = ref[0]
        column[rows_of(lax.axis_index("row") ^ k ^ half, slab), :] = ref[1]
    product = jnp.dot(adj_ref[...], column[...], preferred_element_type=F32).astype(BF16)
    part[...] = product
    grad[...] = lax.dot_general(
        product, cots[...], (((0,), (0,)), ((), ())), preferred_element_type=F32
    ).astype(BF16)
    for n in range(others):
        k = n + 1 if n else 0
        out_refs[n][...] = part[rows_of(lax.axis_index("col") ^ k, slab), :]
        out_refs[others + n][...] = grad[rows_of(lax.axis_index("col") ^ k, piece), :]
    both_ref[:slab, :] = part[rows_of(lax.axis_index("col") ^ 1, slab), :]
    both_ref[slab:, :] = grad[rows_of(lax.axis_index("col") ^ 1, piece), :]


def backward_kernel(adj_ref, near_ref, other_ref, *refs):
    *pair_refs, cots, total = refs
    half, slab = len(pair_refs), pair_refs[0].shape[1]
    place_cots(near_ref, other_ref, cots)
    total[...] = lax.dot_general(
        adj_ref[...], cots[...], (((0,), (0,)), ((), ())), preferred_element_type=F32
    ).astype(BF16)
    for k, ref in enumerate(pair_refs):
        ref[0] = total[rows_of(lax.axis_index("row") ^ k, slab), :]
        ref[1] = total[rows_of(lax.axis_index("row") ^ k ^ half, slab), :]


def pair_sum_kernel(*refs):
    *pair_refs, keep_ref, send_ref = refs
    total = summed(pair_refs)
    keep_ref[...] = total[0]
    send_ref[...] = total[1].astype(BF16)


def weighted(weight_ref, term_refs, contract):
    return lax.dot_general(
        summed(term_refs).astype(BF16),
        weight_ref[...],
        (((1,), (contract,)), ((), ())),
        preferred_element_type=F32,
    ).astype(BF16)


def output_kernel(weight_ref, keep_ref, far_ref, first_ref, *refs):
    *chunk_refs, layer_ref, feature_ref = refs
    slab = layer_ref.shape[0]
    layer_ref[...] = weighted(weight_ref, [first_ref.at[:slab, :], *chunk_refs], 0)
    feature_ref[...] = weighted(weight_ref, [keep_ref, far_ref.at[:slab, :]], 1)


def col_kernel(first_ref, *refs, terms):
    out_ref = refs[-1]
    first_ref = first_ref.at[first_ref.shape[0] - out_ref.shape[0] :, :]
    out_ref[...] = summed([first_ref, *refs[:terms]]).astype(BF16)


def hold_kernel(*refs):
    count = len(refs) // 2
    for src_ref, dst_ref in zip(refs[:count], refs[count + 1 :]):
        dst_ref[...] = src_ref[...]


def near_kernel(send_ref, *refs, terms):
    slab = send_ref.shape[0]
    refs[-1][:slab, :] = send_ref[...]
    refs[-1][slab:, :] = summed(refs[:terms]).astype(BF16)


def row_kernel(held_ref, got_ref, out_ref):
    slab = held_ref.shape[0] - out_ref.shape[0]
    out_ref[...] = summed([held_ref.at[slab:, :], got_ref.at[slab:, :]]).astype(BF16)


def gather_kernel(*refs):
    *piece_refs, out_ref = refs
    piece = piece_refs[0].shape[0]
    for k, ref in enumerate(piece_refs):
        out_ref[rows_of(lax.axis_index("col") ^ k, piece), :] = ref[...]


def swap(array, axis, distance):
    pairs = [(i, i ^ distance) for i in range(lax.axis_size(axis))]
    return lax.ppermute(array, axis, pairs)


def exchange(chunks, axis, stride=1):
    return [chunks[0]] + [swap(chunks[k], axis, k * stride) for k in range(1, len(chunks))]


def body(features, weight, tile_values, tile_slots, tile_counts, cotangent):
    row_devices = lax.axis_size("row")
    col_devices = lax.axis_size("col")
    half = row_devices // 2
    slots, tile = tile_values.shape[2:4]
    slab, width = features.shape[1:]
    rows, cols = col_devices * slab, row_devices * slab
    piece = width // col_devices

    def call(kernel, name, out_shape, in_specs, args, scratch=(), micros=None):
        many = isinstance(out_shape, list)
        return pl.pallas_call(
            kernel,
            out_shape=out_shape,
            in_specs=in_specs,
            out_specs=[VMEM] * len(out_shape) if many else VMEM,
            scratch_shapes=scratch,
            compiler_params=pltpu.CompilerParams(
                vmem_limit_bytes=min(8 * 2**20 + 6 * rows * cols, 56 * 2**20)
            ),
            cost_estimate=None if micros is None else hint(micros),
            name=name,
        )(*args)

    own = features[0]
    far = swap(own, "row", half)
    adj = call(
        dense_kernel, "dense", shape(rows, cols), [SMEM, SMEM, ANY],
        (tile_slots[0, 0], tile_counts[0], tile_values[0, 0]),
        scratch=[pltpu.SemaphoreType.DMA((slots,))],
    )

    def hold(arrays, after, name):
        return call(
            hold_kernel, name, [shape(*array.shape) for array in arrays],
            [VMEM] * len(arrays) + [ANY], (*arrays, after),
        )

    def stack(arrays, name, after=()):
        return call(
            stack_kernel, name, shape(len(arrays), slab, width),
            [VMEM] * len(arrays) + [ANY] * len(after), (*arrays, *after), micros=3,
        )

    kept = hold([own, cotangent[0]], tile_counts, "own")
    pair = stack([kept[0], far], "pair")
    features_got = exchange([pair] * half, "row")
    cot_near = stack(
        [kept[1]] + exchange([cotangent[0]] * (col_devices // 2), "col", 2)[1:], "cot_near"
    )
    cot_other = swap(cot_near, "col", 1)

    outs = call(
        lambda *refs: forward_kernel(*refs, half=half), "forward",
        [shape(slab, width)] * (col_devices - 1)
        + [shape(piece, width)] * (col_devices - 1)
        + [shape(slab + piece, width)],
        [VMEM] * (3 + half), (adj, cot_near, cot_other, *features_got),
        scratch=[
            pltpu.VMEM((cols, width), BF16),
            pltpu.VMEM((rows, width), BF16),
            pltpu.VMEM((rows, width), BF16),
            pltpu.VMEM((width, width), BF16),
        ],
    )
    column_pairs = call(
        backward_kernel, "backward", [shape(2, slab, width)] * half,
        [VMEM] * 3, (adj, cot_near, cot_other),
        scratch=[pltpu.VMEM((rows, width), BF16), pltpu.VMEM((cols, width), BF16)],
    )
    chunks, pieces = outs[: col_devices - 1], outs[col_devices - 1 : -1]
    first = swap(outs[-1], "col", 1)

    column_keep, column_send = call(
        pair_sum_kernel, "pair_sum", [shape(slab, width, dtype=F32), shape(slab, width)],
        [VMEM] * half, exchange(column_pairs, "row")[::-1], micros=5,
    )
    def fetch(arrays):
        return [arrays[0]] + [swap(arrays[k - 1], "col", k) for k in range(2, col_devices)]

    grad_col = call(
        lambda *refs: col_kernel(*refs, terms=col_devices - 1), "grad_col", shape(piece, width),
        [VMEM] * col_devices + [ANY], (first, *fetch(pieces), column_send),
    )
    near_terms = exchange([grad_col] * half, "row")
    row_got = fetch([chunks[0], *hold(chunks[1:], near_terms[3], "hold_chunks")])
    both = call(
        lambda *refs: near_kernel(*refs, terms=half), "grad_near", shape(slab + piece, width),
        [VMEM] * (1 + half), (column_send, *near_terms),
    )
    both_far = swap(both, "row", half)
    grad_row = call(
        row_kernel, "grad_row", shape(piece, width), [VMEM] * 2, (both, both_far)
    )
    layer_out, feature_grad = call(
        output_kernel, "outputs", [shape(slab, width)] * 2, [VMEM] * (3 + col_devices),
        (weight, column_keep, both_far, first, *row_got),
    )
    gathered = call(
        gather_kernel, "weight_grad", shape(width, width), [VMEM] * col_devices,
        exchange([grad_row] * col_devices, "col"),
    )
    weight_grad = gathered.astype(F32) * (1.0 / math.sqrt(row_devices * col_devices * slab))
    return (layer_out[None], feature_grad[None], weight_grad)


def solution(mesh):
    placed = (
        P("col", "row", None),
        P(),
        P("row", "col", None, None, None),
        P("row", "col", None),
        P("row", "col"),
        P("row", "col", None),
    )
    return jax.shard_map(
        body,
        mesh=mesh,
        in_specs=placed,
        out_specs=(P("row", "col", None), P("col", "row", None), P()),
        check_vma=False,
    )
```

```python
import math

import jax
import jax.numpy as jnp
from jax import lax
from jax.experimental import pallas as pl
from jax.experimental.pallas import tpu as pltpu
from jax.sharding import PartitionSpec as P

F32 = jnp.float32
BF16 = jnp.bfloat16
VMEM = pl.BlockSpec(memory_space=pltpu.VMEM)
SMEM = pl.BlockSpec(memory_space=pltpu.SMEM)
ANY = pl.BlockSpec(memory_space=pl.ANY)


def hint(microseconds):
    return pl.CostEstimate(
        flops=int(microseconds * 1e9), bytes_accessed=int(microseconds * 3.6e6), transcendentals=0
    )


def shape(*dims, dtype=BF16):
    return jax.ShapeDtypeStruct(dims, dtype)


def rows_of(index, slab):
    return pl.ds(pl.multiple_of(index * slab, slab), slab)


def summed(refs):
    total = refs[0][...].astype(F32)
    for ref in refs[1:]:
        total = total + ref[...].astype(F32)
    return total


def dense_kernel(meta_ref, tiles_ref, adj_ref, sems):
    slot_count, tile, _ = tiles_ref.shape
    col_tiles = adj_ref.shape[1] // tile
    live = jnp.minimum(meta_ref[0], slot_count)
    adj_ref[...] = jnp.zeros_like(adj_ref)

    def copy(k):
        slot = meta_ref[1 + k]
        row = pl.multiple_of((slot // col_tiles) * tile, tile)
        col = pl.multiple_of((slot % col_tiles) * tile, tile)
        place = adj_ref.at[pl.ds(row, tile), pl.ds(col, tile)]
        return pltpu.make_async_copy(tiles_ref.at[k], place, sems.at[k])

    def start(k, carry):
        copy(k).start()
        return carry

    def wait(k, carry):
        copy(k).wait()
        return carry

    lax.fori_loop(0, live, start, 0)
    lax.fori_loop(0, live, wait, 0)


def stack_kernel(*refs):
    out_ref = refs[-1]
    for k in range(out_ref.shape[0]):
        out_ref[k] = refs[k][...]


def place_cots(near_ref, other_ref, out_ref):
    slab = near_ref.shape[1]
    for k in range(near_ref.shape[0]):
        out_ref[rows_of(lax.axis_index("col") ^ (2 * k), slab), :] = near_ref[k]
        out_ref[rows_of(lax.axis_index("col") ^ (2 * k + 1), slab), :] = other_ref[k]


def forward_kernel(adj_ref, near_ref, other_ref, *refs, half):
    pair_refs, (*out_refs, both_ref, column, cots, part, grad) = refs[:half], refs[half:]
    slab = near_ref.shape[1]
    others = len(out_refs) // 2
    piece = both_ref.shape[0] - slab
    place_cots(near_ref, other_ref, cots)
    for k, ref in enumerate(pair_refs):
        column[rows_of(lax.axis_index("row") ^ k, slab), :] = ref[0]
        column[rows_of(lax.axis_index("row") ^ k ^ half, slab), :] = ref[1]
    product = jnp.dot(adj_ref[...], column[...], preferred_element_type=F32).astype(BF16)
    part[...] = product
    grad[...] = lax.dot_general(
        product, cots[...], (((0,), (0,)), ((), ())), preferred_element_type=F32
    ).astype(BF16)
    for n in range(others):
        k = n + 1 if n else 0
        out_refs[n][...] = part[rows_of(lax.axis_index("col") ^ k, slab), :]
        out_refs[others + n][...] = grad[rows_of(lax.axis_index("col") ^ k, piece), :]
    both_ref[:slab, :] = part[rows_of(lax.axis_index("col") ^ 1, slab), :]
    both_ref[slab:, :] = grad[rows_of(lax.axis_index("col") ^ 1, piece), :]


def backward_kernel(adj_ref, near_ref, other_ref, *refs):
    *pair_refs, cots, total = refs
    half, slab = len(pair_refs), pair_refs[0].shape[1]
    place_cots(near_ref, other_ref, cots)
    total[...] = lax.dot_general(
        adj_ref[...], cots[...], (((0,), (0,)), ((), ())), preferred_element_type=F32
    ).astype(BF16)
    for k, ref in enumerate(pair_refs):
        ref[0] = total[rows_of(lax.axis_index("row") ^ k, slab), :]
        ref[1] = total[rows_of(lax.axis_index("row") ^ k ^ half, slab), :]


def pair_sum_kernel(*refs):
    *pair_refs, keep_ref, send_ref = refs
    total = summed(pair_refs)
    keep_ref[...] = total[0]
    send_ref[...] = total[1].astype(BF16)


def weighted(weight_ref, term_refs, contract):
    return lax.dot_general(
        summed(term_refs).astype(BF16),
        weight_ref[...],
        (((1,), (contract,)), ((), ())),
        preferred_element_type=F32,
    ).astype(BF16)


def output_kernel(weight_ref, keep_ref, far_ref, first_ref, *refs):
    *chunk_refs, layer_ref, feature_ref = refs
    slab = layer_ref.shape[0]
    layer_ref[...] = weighted(weight_ref, [first_ref.at[:slab, :], *chunk_refs], 0)
    feature_ref[...] = weighted(weight_ref, [keep_ref, far_ref.at[:slab, :]], 1)


def col_kernel(send_ref, first_ref, *refs):
    *term_refs, out_ref = refs
    slab = send_ref.shape[0]
    out_ref[:slab, :] = send_ref[...]
    out_ref[slab:, :] = summed([first_ref.at[slab:, :], *term_refs]).astype(BF16)


def sum_kernel(*refs):
    *term_refs, out_ref = refs
    out_ref[...] = summed(term_refs).astype(BF16)


def hold_kernel(*refs):
    count = len(refs) // 2
    for src_ref, dst_ref in zip(refs[:count], refs[count + 1 :]):
        dst_ref[...] = src_ref[...]


def row_kernel(held_ref, got_ref, out_ref):
    slab = held_ref.shape[0] - out_ref.shape[0]
    out_ref[...] = summed([held_ref.at[slab:, :], got_ref.at[slab:, :]]).astype(BF16)


def gather_kernel(*refs):
    *piece_refs, out_ref = refs
    piece = piece_refs[0].shape[0]
    for k, ref in enumerate(piece_refs):
        out_ref[rows_of(lax.axis_index("col") ^ k, piece), :] = ref[...]


def swap(array, axis, distance):
    pairs = [(i, i ^ distance) for i in range(lax.axis_size(axis))]
    return lax.ppermute(array, axis, pairs)


def exchange(chunks, axis, stride=1):
    return [chunks[0]] + [swap(chunks[k], axis, k * stride) for k in range(1, len(chunks))]


def body(features, weight, tile_values, tile_slots, tile_counts, cotangent):
    row_devices = lax.axis_size("row")
    col_devices = lax.axis_size("col")
    half = row_devices // 2
    slots, tile = tile_values.shape[2:4]
    slab, width = features.shape[1:]
    rows, cols = col_devices * slab, row_devices * slab
    piece = width // col_devices
    live = jnp.concatenate([tile_counts[0], tile_slots[0, 0]])

    def call(kernel, name, out_shape, in_specs, args, scratch=(), micros=None):
        many = isinstance(out_shape, list)
        return pl.pallas_call(
            kernel,
            out_shape=out_shape,
            in_specs=in_specs,
            out_specs=[VMEM] * len(out_shape) if many else VMEM,
            scratch_shapes=scratch,
            compiler_params=pltpu.CompilerParams(
                vmem_limit_bytes=min(8 * 2**20 + 6 * rows * cols, 56 * 2**20)
            ),
            cost_estimate=None if micros is None else hint(micros),
            name=name,
        )(*args)

    own = features[0]
    far = swap(own, "row", half)
    adj = call(
        dense_kernel, "dense", shape(rows, cols), [SMEM, ANY], (live, tile_values[0, 0]),
        scratch=[pltpu.SemaphoreType.DMA((slots,))],
    )

    def hold(arrays, after, name):
        return call(
            hold_kernel, name, [shape(*array.shape) for array in arrays],
            [VMEM] * len(arrays) + [ANY], (*arrays, after),
        )

    def stack(arrays, name, after=()):
        return call(
            stack_kernel, name, shape(len(arrays), slab, width),
            [VMEM] * len(arrays) + [ANY] * len(after), (*arrays, *after), micros=3,
        )

    kept = hold([own, cotangent[0]], live, "own")
    pair = stack([kept[0], far], "pair")
    features_got = exchange([pair] * half, "row")
    cot_near = stack(
        [kept[1]] + exchange([cotangent[0]] * (col_devices // 2), "col", 2)[1:], "cot_near"
    )
    cot_other = swap(cot_near, "col", 1)

    outs = call(
        lambda *refs: forward_kernel(*refs, half=half), "forward",
        [shape(slab, width)] * (col_devices - 1)
        + [shape(piece, width)] * (col_devices - 1)
        + [shape(slab + piece, width)],
        [VMEM] * (3 + half), (adj, cot_near, cot_other, *features_got),
        scratch=[
            pltpu.VMEM((cols, width), BF16),
            pltpu.VMEM((rows, width), BF16),
            pltpu.VMEM((rows, width), BF16),
            pltpu.VMEM((width, width), BF16),
        ],
    )
    column_pairs = call(
        backward_kernel, "backward", [shape(2, slab, width)] * half,
        [VMEM] * 3, (adj, cot_near, cot_other),
        scratch=[pltpu.VMEM((rows, width), BF16), pltpu.VMEM((cols, width), BF16)],
    )
    chunks, pieces = outs[: col_devices - 1], outs[col_devices - 1 : -1]
    first = swap(outs[-1], "col", 1)

    column_keep, column_send = call(
        pair_sum_kernel, "pair_sum", [shape(slab, width, dtype=F32), shape(slab, width)],
        [VMEM] * half, exchange(column_pairs, "row")[::-1], micros=5,
    )
    def fetch(arrays):
        return [arrays[0]] + [swap(arrays[k - 1], "col", k) for k in range(2, col_devices)]

    both = call(
        col_kernel, "grad_col", shape(slab + piece, width),
        [VMEM] * (1 + col_devices), (column_send, first, *fetch(pieces)),
    )
    both_far = swap(both, "row", half)
    grad_far = call(
        row_kernel, "grad_far", shape(piece, width), [VMEM] * 2, (both, both_far)
    )
    row_got = fetch([chunks[0], *hold(chunks[1:], both, "hold_chunks")])
    grad_row = call(
        sum_kernel, "grad_row", shape(piece, width), [VMEM] * half,
        exchange([grad_far] * half, "row"),
    )
    layer_out, feature_grad = call(
        output_kernel, "outputs", [shape(slab, width)] * 2, [VMEM] * (3 + col_devices),
        (weight, column_keep, both_far, first, *row_got),
    )
    gathered = call(
        gather_kernel, "weight_grad", shape(width, width), [VMEM] * col_devices,
        exchange([grad_row] * col_devices, "col"),
    )
    weight_grad = gathered.astype(F32) * (1.0 / math.sqrt(row_devices * col_devices * slab))
    return (layer_out[None], feature_grad[None], weight_grad)


def solution(mesh):
    placed = (
        P("col", "row", None),
        P(),
        P("row", "col", None, None, None),
        P("row", "col", None),
        P("row", "col"),
        P("row", "col", None),
    )
    return jax.shard_map(
        body,
        mesh=mesh,
        in_specs=placed,
        out_specs=(P("row", "col", None), P("col", "row", None), P()),
        check_vma=False,
    )
```

```python
import math

import jax
import jax.numpy as jnp
from jax import lax
from jax.experimental import pallas as pl
from jax.experimental.pallas import tpu as pltpu
from jax.sharding import PartitionSpec as P

F32 = jnp.float32
BF16 = jnp.bfloat16
VMEM = pl.BlockSpec(memory_space=pltpu.VMEM)
SMEM = pl.BlockSpec(memory_space=pltpu.SMEM)
ANY = pl.BlockSpec(memory_space=pl.ANY)


def hint(microseconds):
    return pl.CostEstimate(
        flops=int(microseconds * 1e9), bytes_accessed=int(microseconds * 3.6e6), transcendentals=0
    )


def shape(*dims, dtype=BF16):
    return jax.ShapeDtypeStruct(dims, dtype)


def rows_of(index, slab):
    return pl.ds(pl.multiple_of(index * slab, slab), slab)


def summed(refs):
    total = refs[0][...].astype(F32)
    for ref in refs[1:]:
        total = total + ref[...].astype(F32)
    return total


def dense_kernel(meta_ref, tiles_ref, adj_ref, sems):
    slot_count, tile, _ = tiles_ref.shape
    col_tiles = adj_ref.shape[1] // tile
    live = jnp.minimum(meta_ref[0], slot_count)
    adj_ref[...] = jnp.zeros_like(adj_ref)

    def copy(k):
        slot = meta_ref[1 + k]
        row = pl.multiple_of((slot // col_tiles) * tile, tile)
        col = pl.multiple_of((slot % col_tiles) * tile, tile)
        place = adj_ref.at[pl.ds(row, tile), pl.ds(col, tile)]
        return pltpu.make_async_copy(tiles_ref.at[k], place, sems.at[k])

    def start(k, carry):
        copy(k).start()
        return carry

    def wait(k, carry):
        copy(k).wait()
        return carry

    lax.fori_loop(0, live, start, 0)
    lax.fori_loop(0, live, wait, 0)


def stack_kernel(*refs):
    out_ref = refs[-1]
    for k in range(out_ref.shape[0]):
        out_ref[k] = refs[k][...]


def place_cots(near_ref, other_ref, out_ref):
    slab = near_ref.shape[1]
    for k in range(near_ref.shape[0]):
        out_ref[rows_of(lax.axis_index("col") ^ (2 * k), slab), :] = near_ref[k]
        out_ref[rows_of(lax.axis_index("col") ^ (2 * k + 1), slab), :] = other_ref[k]


def forward_kernel(adj_ref, near_ref, other_ref, *refs, half):
    pair_refs, (*out_refs, both_ref, column, cots, part, grad) = refs[:half], refs[half:]
    slab = near_ref.shape[1]
    others = len(out_refs) // 2
    piece = both_ref.shape[0] - slab
    place_cots(near_ref, other_ref, cots)
    for k, ref in enumerate(pair_refs):
        column[rows_of(lax.axis_index("row") ^ k, slab), :] = ref[0]
        column[rows_of(lax.axis_index("row") ^ k ^ half, slab), :] = ref[1]
    product = jnp.dot(adj_ref[...], column[...], preferred_element_type=F32).astype(BF16)
    part[...] = product
    grad[...] = lax.dot_general(
        product, cots[...], (((0,), (0,)), ((), ())), preferred_element_type=F32
    ).astype(BF16)
    for n in range(others):
        k = n + 1 if n else 0
        out_refs[n][...] = part[rows_of(lax.axis_index("col") ^ k, slab), :]
        out_refs[others + n][...] = grad[rows_of(lax.axis_index("col") ^ k, piece), :]
    both_ref[:slab, :] = part[rows_of(lax.axis_index("col") ^ 1, slab), :]
    both_ref[slab:, :] = grad[rows_of(lax.axis_index("col") ^ 1, piece), :]


def backward_kernel(adj_ref, near_ref, other_ref, *refs):
    *pair_refs, cots, total = refs
    half, slab = len(pair_refs), pair_refs[0].shape[1]
    place_cots(near_ref, other_ref, cots)
    total[...] = lax.dot_general(
        adj_ref[...], cots[...], (((0,), (0,)), ((), ())), preferred_element_type=F32
    ).astype(BF16)
    for k, ref in enumerate(pair_refs):
        ref[0] = total[rows_of(lax.axis_index("row") ^ k, slab), :]
        ref[1] = total[rows_of(lax.axis_index("row") ^ k ^ half, slab), :]


def pair_sum_kernel(*refs):
    *pair_refs, keep_ref, send_ref = refs
    total = summed(pair_refs)
    keep_ref[...] = total[0]
    send_ref[...] = total[1].astype(BF16)


def weighted(weight_ref, term_refs, contract):
    return lax.dot_general(
        summed(term_refs).astype(BF16),
        weight_ref[...],
        (((1,), (contract,)), ((), ())),
        preferred_element_type=F32,
    ).astype(BF16)


def output_kernel(weight_ref, keep_ref, far_ref, first_ref, *refs):
    *chunk_refs, layer_ref, feature_ref = refs
    slab = layer_ref.shape[0]
    layer_ref[...] = weighted(weight_ref, [first_ref.at[:slab, :], *chunk_refs], 0)
    feature_ref[...] = weighted(weight_ref, [keep_ref, far_ref.at[:slab, :]], 1)


def col_kernel(first_ref, *refs, terms):
    out_ref = refs[-1]
    first_ref = first_ref.at[first_ref.shape[0] - out_ref.shape[0] :, :]
    out_ref[...] = summed([first_ref, *refs[:terms]]).astype(BF16)


def hold_kernel(*refs):
    count = len(refs) // 2
    for src_ref, dst_ref in zip(refs[:count], refs[count + 1 :]):
        dst_ref[...] = src_ref[...]


def near_kernel(send_ref, *refs, terms):
    slab = send_ref.shape[0]
    refs[-1][:slab, :] = send_ref[...]
    refs[-1][slab:, :] = summed(refs[:terms]).astype(BF16)


def row_kernel(held_ref, got_ref, out_ref):
    slab = held_ref.shape[0] - out_ref.shape[0]
    out_ref[...] = summed([held_ref.at[slab:, :], got_ref.at[slab:, :]]).astype(BF16)


def gather_kernel(*refs):
    *piece_refs, out_ref = refs
    piece = piece_refs[0].shape[0]
    for k, ref in enumerate(piece_refs):
        out_ref[rows_of(lax.axis_index("col") ^ k, piece), :] = ref[...]


def swap(array, axis, distance):
    pairs = [(i, i ^ distance) for i in range(lax.axis_size(axis))]
    return lax.ppermute(array, axis, pairs)


def exchange(chunks, axis, stride=1):
    return [chunks[0]] + [swap(chunks[k], axis, k * stride) for k in range(1, len(chunks))]


def body(features, weight, tile_values, tile_slots, tile_counts, cotangent):
    row_devices = lax.axis_size("row")
    col_devices = lax.axis_size("col")
    half = row_devices // 2
    slots, tile = tile_values.shape[2:4]
    slab, width = features.shape[1:]
    rows, cols = col_devices * slab, row_devices * slab
    piece = width // col_devices
    live = jnp.concatenate([tile_counts[0], tile_slots[0, 0]])

    def call(kernel, name, out_shape, in_specs, args, scratch=(), micros=None):
        many = isinstance(out_shape, list)
        return pl.pallas_call(
            kernel,
            out_shape=out_shape,
            in_specs=in_specs,
            out_specs=[VMEM] * len(out_shape) if many else VMEM,
            scratch_shapes=scratch,
            compiler_params=pltpu.CompilerParams(
                vmem_limit_bytes=min(8 * 2**20 + 6 * rows * cols, 56 * 2**20)
            ),
            cost_estimate=None if micros is None else hint(micros),
            name=name,
        )(*args)

    own = features[0]
    far = swap(own, "row", half)
    adj = call(
        dense_kernel, "dense", shape(rows, cols), [SMEM, ANY], (live, tile_values[0, 0]),
        scratch=[pltpu.SemaphoreType.DMA((slots,))],
    )

    def hold(arrays, after, name):
        return call(
            hold_kernel, name, [shape(*array.shape) for array in arrays],
            [VMEM] * len(arrays) + [ANY], (*arrays, after),
        )

    def stack(arrays, name, after=()):
        return call(
            stack_kernel, name, shape(len(arrays), slab, width),
            [VMEM] * len(arrays) + [ANY] * len(after), (*arrays, *after), micros=3,
        )

    kept = hold([own, cotangent[0]], live, "own")
    pair = stack([kept[0], far], "pair")
    features_got = exchange([pair] * half, "row")
    cot_near = stack(
        [kept[1]] + exchange([cotangent[0]] * (col_devices // 2), "col", 2)[1:], "cot_near"
    )
    cot_other = swap(cot_near, "col", 1)

    outs = call(
        lambda *refs: forward_kernel(*refs, half=half), "forward",
        [shape(slab, width)] * (col_devices - 1)
        + [shape(piece, width)] * (col_devices - 1)
        + [shape(slab + piece, width)],
        [VMEM] * (3 + half), (adj, cot_near, cot_other, *features_got),
        scratch=[
            pltpu.VMEM((cols, width), BF16),
            pltpu.VMEM((rows, width), BF16),
            pltpu.VMEM((rows, width), BF16),
            pltpu.VMEM((width, width), BF16),
        ],
    )
    column_pairs = call(
        backward_kernel, "backward", [shape(2, slab, width)] * half,
        [VMEM] * 3, (adj, cot_near, cot_other),
        scratch=[pltpu.VMEM((rows, width), BF16), pltpu.VMEM((cols, width), BF16)],
    )
    chunks, pieces = outs[: col_devices - 1], outs[col_devices - 1 : -1]
    first = swap(outs[-1], "col", 1)

    column_keep, column_send = call(
        pair_sum_kernel, "pair_sum", [shape(slab, width, dtype=F32), shape(slab, width)],
        [VMEM] * half, exchange(column_pairs, "row")[::-1], micros=5,
    )
    def fetch(arrays):
        return [arrays[0]] + [swap(arrays[k - 1], "col", k) for k in range(2, col_devices)]

    grad_col = call(
        lambda *refs: col_kernel(*refs, terms=col_devices - 1), "grad_col", shape(piece, width),
        [VMEM] * col_devices + [ANY], (first, *fetch(pieces), column_send),
    )
    near_terms = exchange([grad_col] * half, "row")
    held = hold(chunks[1:], near_terms[3], "hold_chunks")
    row_got = fetch([chunks[0], *held])
    both = call(
        lambda *refs: near_kernel(*refs, terms=half), "grad_near", shape(slab + piece, width),
        [VMEM] * (1 + half) + [ANY] * len(held), (column_send, *near_terms, *held),
    )
    both_far = swap(both, "row", half)
    grad_row = call(
        row_kernel, "grad_row", shape(piece, width), [VMEM] * 2, (both, both_far)
    )
    layer_out, feature_grad = call(
        output_kernel, "outputs", [shape(slab, width)] * 2, [VMEM] * (3 + col_devices),
        (weight, column_keep, both_far, first, *row_got),
    )
    gathered = call(
        gather_kernel, "weight_grad", shape(width, width), [VMEM] * col_devices,
        exchange([grad_row] * col_devices, "col"),
    )
    weight_grad = gathered.astype(F32) * (1.0 / math.sqrt(row_devices * col_devices * slab))
    return (layer_out[None], feature_grad[None], weight_grad)


def solution(mesh):
    placed = (
        P("col", "row", None),
        P(),
        P("row", "col", None, None, None),
        P("row", "col", None),
        P("row", "col"),
        P("row", "col", None),
    )
    return jax.shard_map(
        body,
        mesh=mesh,
        in_specs=placed,
        out_specs=(P("row", "col", None), P("col", "row", None), P()),
        check_vma=False,
    )
```

```python
import math

import jax
import jax.numpy as jnp
from jax import lax
from jax.experimental import pallas as pl
from jax.experimental.pallas import tpu as pltpu
from jax.sharding import PartitionSpec as P

F32 = jnp.float32
BF16 = jnp.bfloat16
VMEM = pl.BlockSpec(memory_space=pltpu.VMEM)
SMEM = pl.BlockSpec(memory_space=pltpu.SMEM)
ANY = pl.BlockSpec(memory_space=pl.ANY)


def hint(microseconds):
    return pl.CostEstimate(
        flops=int(microseconds * 1e9), bytes_accessed=int(microseconds * 3.6e6), transcendentals=0
    )


def shape(*dims, dtype=BF16):
    return jax.ShapeDtypeStruct(dims, dtype)


def rows_of(index, slab):
    return pl.ds(pl.multiple_of(index * slab, slab), slab)


def summed(refs):
    total = refs[0][...].astype(F32)
    for ref in refs[1:]:
        total = total + ref[...].astype(F32)
    return total


def dense_kernel(slots_ref, count_ref, tiles_ref, adj_ref, sems):
    slot_count, tile, _ = tiles_ref.shape
    col_tiles = adj_ref.shape[1] // tile
    live = jnp.minimum(count_ref[0], slot_count)
    adj_ref[...] = jnp.zeros_like(adj_ref)

    def copy(k):
        slot = slots_ref[k]
        row = pl.multiple_of((slot // col_tiles) * tile, tile)
        col = pl.multiple_of((slot % col_tiles) * tile, tile)
        place = adj_ref.at[pl.ds(row, tile), pl.ds(col, tile)]
        return pltpu.make_async_copy(tiles_ref.at[k], place, sems.at[k])

    def start(k, carry):
        copy(k).start()
        return carry

    def wait(k, carry):
        copy(k).wait()
        return carry

    lax.fori_loop(0, live, start, 0)
    lax.fori_loop(0, live, wait, 0)


def stack_kernel(*refs):
    out_ref = refs[-1]
    for k in range(out_ref.shape[0]):
        out_ref[k] = refs[k][...]


def place_cots(near_ref, other_ref, out_ref):
    slab = near_ref.shape[1]
    for k in range(near_ref.shape[0]):
        out_ref[rows_of(lax.axis_index("col") ^ (2 * k), slab), :] = near_ref[k]
        out_ref[rows_of(lax.axis_index("col") ^ (2 * k + 1), slab), :] = other_ref[k]


def forward_kernel(adj_ref, near_ref, other_ref, *refs, half):
    pair_refs, (*out_refs, both_ref, column, cots, part, grad) = refs[:half], refs[half:]
    slab = near_ref.shape[1]
    others = len(out_refs) // 2
    piece = both_ref.shape[0] - slab
    place_cots(near_ref, other_ref, cots)
    for k, ref in enumerate(pair_refs):
        column[rows_of(lax.axis_index("row") ^ k, slab), :] = ref[0]
        column[rows_of(lax.axis_index("row") ^ k ^ half, slab), :] = ref[1]
    product = jnp.dot(adj_ref[...], column[...], preferred_element_type=F32).astype(BF16)
    part[...] = product
    grad[...] = lax.dot_general(
        product, cots[...], (((0,), (0,)), ((), ())), preferred_element_type=F32
    ).astype(BF16)
    for n in range(others):
        k = n + 1 if n else 0
        out_refs[n][...] = part[rows_of(lax.axis_index("col") ^ k, slab), :]
        out_refs[others + n][...] = grad[rows_of(lax.axis_index("col") ^ k, piece), :]
    both_ref[:slab, :] = part[rows_of(lax.axis_index("col") ^ 1, slab), :]
    both_ref[slab:, :] = grad[rows_of(lax.axis_index("col") ^ 1, piece), :]


def backward_kernel(adj_ref, near_ref, other_ref, *refs):
    *pair_refs, cots, total = refs
    half, slab = len(pair_refs), pair_refs[0].shape[1]
    place_cots(near_ref, other_ref, cots)
    total[...] = lax.dot_general(
        adj_ref[...], cots[...], (((0,), (0,)), ((), ())), preferred_element_type=F32
    ).astype(BF16)
    for k, ref in enumerate(pair_refs):
        ref[0] = total[rows_of(lax.axis_index("row") ^ k, slab), :]
        ref[1] = total[rows_of(lax.axis_index("row") ^ k ^ half, slab), :]


def pair_sum_kernel(*refs):
    *pair_refs, keep_ref, send_ref = refs
    total = summed(pair_refs)
    keep_ref[...] = total[0]
    send_ref[...] = total[1].astype(BF16)


def weighted(weight_ref, term_refs, contract):
    return lax.dot_general(
        summed(term_refs).astype(BF16),
        weight_ref[...],
        (((1,), (contract,)), ((), ())),
        preferred_element_type=F32,
    ).astype(BF16)


def output_kernel(weight_ref, keep_ref, far_ref, first_ref, *refs):
    *chunk_refs, layer_ref, feature_ref = refs
    slab = layer_ref.shape[0]
    layer_ref[...] = weighted(weight_ref, [first_ref.at[:slab, :], *chunk_refs], 0)
    feature_ref[...] = weighted(weight_ref, [keep_ref, far_ref.at[:slab, :]], 1)


def col_kernel(first_ref, *refs, terms):
    out_ref = refs[-1]
    first_ref = first_ref.at[first_ref.shape[0] - out_ref.shape[0] :, :]
    out_ref[...] = summed([first_ref, *refs[:terms]]).astype(BF16)


def hold_kernel(*refs):
    count = len(refs) // 2
    for src_ref, dst_ref in zip(refs[:count], refs[count + 1 :]):
        dst_ref[...] = src_ref[...]


def near_kernel(send_ref, *refs, terms):
    slab = send_ref.shape[0]
    refs[-1][:slab, :] = send_ref[...]
    refs[-1][slab:, :] = summed(refs[:terms]).astype(BF16)


def row_kernel(held_ref, got_ref, out_ref):
    slab = held_ref.shape[0] - out_ref.shape[0]
    out_ref[...] = summed([held_ref.at[slab:, :], got_ref.at[slab:, :]]).astype(BF16)


def gather_kernel(*refs):
    *piece_refs, out_ref = refs
    piece = piece_refs[0].shape[0]
    for k, ref in enumerate(piece_refs):
        out_ref[rows_of(lax.axis_index("col") ^ k, piece), :] = ref[...]


def swap(array, axis, distance):
    pairs = [(i, i ^ distance) for i in range(lax.axis_size(axis))]
    return lax.ppermute(array, axis, pairs)


def exchange(chunks, axis, stride=1):
    return [chunks[0]] + [swap(chunks[k], axis, k * stride) for k in range(1, len(chunks))]


def body(features, weight, tile_values, tile_slots, tile_counts, cotangent):
    row_devices = lax.axis_size("row")
    col_devices = lax.axis_size("col")
    half = row_devices // 2
    slots, tile = tile_values.shape[2:4]
    slab, width = features.shape[1:]
    rows, cols = col_devices * slab, row_devices * slab
    piece = width // col_devices

    def call(kernel, name, out_shape, in_specs, args, scratch=(), micros=None):
        many = isinstance(out_shape, list)
        return pl.pallas_call(
            kernel,
            out_shape=out_shape,
            in_specs=in_specs,
            out_specs=[VMEM] * len(out_shape) if many else VMEM,
            scratch_shapes=scratch,
            compiler_params=pltpu.CompilerParams(
                vmem_limit_bytes=min(8 * 2**20 + 6 * rows * cols, 56 * 2**20)
            ),
            cost_estimate=None if micros is None else hint(micros),
            name=name,
        )(*args)

    own = features[0]
    far = swap(own, "row", half)
    adj = call(
        dense_kernel, "dense", shape(rows, cols), [SMEM, SMEM, ANY],
        (tile_slots[0, 0], tile_counts[0], tile_values[0, 0]),
        scratch=[pltpu.SemaphoreType.DMA((slots,))],
    )

    def hold(arrays, after, name):
        return call(
            hold_kernel, name, [shape(*array.shape) for array in arrays],
            [VMEM] * len(arrays) + [ANY], (*arrays, after),
        )

    def stack(arrays, name, after=()):
        return call(
            stack_kernel, name, shape(len(arrays), slab, width),
            [VMEM] * len(arrays) + [ANY] * len(after), (*arrays, *after), micros=3,
        )

    kept = hold([own, cotangent[0]], tile_counts, "own")
    pair = stack([kept[0], far], "pair")
    features_got = exchange([pair] * half, "row")
    cot_near = stack(
        [kept[1]] + exchange([cotangent[0]] * (col_devices // 2), "col", 2)[1:], "cot_near"
    )
    cot_other = swap(cot_near, "col", 1)

    outs = call(
        lambda *refs: forward_kernel(*refs, half=half), "forward",
        [shape(slab, width)] * (col_devices - 1)
        + [shape(piece, width)] * (col_devices - 1)
        + [shape(slab + piece, width)],
        [VMEM] * (3 + half), (adj, cot_near, cot_other, *features_got),
        scratch=[
            pltpu.VMEM((cols, width), BF16),
            pltpu.VMEM((rows, width), BF16),
            pltpu.VMEM((rows, width), BF16),
            pltpu.VMEM((width, width), BF16),
        ],
    )
    column_pairs = call(
        backward_kernel, "backward", [shape(2, slab, width)] * half,
        [VMEM] * 3, (adj, cot_near, cot_other),
        scratch=[pltpu.VMEM((rows, width), BF16), pltpu.VMEM((cols, width), BF16)],
    )
    chunks, pieces = outs[: col_devices - 1], outs[col_devices - 1 : -1]
    first = swap(outs[-1], "col", 1)

    column_keep, column_send = call(
        pair_sum_kernel, "pair_sum", [shape(slab, width, dtype=F32), shape(slab, width)],
        [VMEM] * half, exchange(column_pairs, "row")[::-1], micros=5,
    )
    def fetch(arrays):
        return [arrays[0]] + [swap(arrays[k - 1], "col", k) for k in range(2, col_devices)]

    grad_col = call(
        lambda *refs: col_kernel(*refs, terms=col_devices - 1), "grad_col", shape(piece, width),
        [VMEM] * col_devices + [ANY], (first, *fetch(pieces), column_send),
    )
    near_terms = exchange([grad_col] * half, "row")
    held = hold(chunks[1:], near_terms[3], "hold_chunks")
    row_got = fetch([chunks[0], *held])
    both = call(
        lambda *refs: near_kernel(*refs, terms=half), "grad_near", shape(slab + piece, width),
        [VMEM] * (1 + half) + [ANY] * len(held), (column_send, *near_terms, *held),
    )
    both_far = swap(both, "row", half)
    grad_row = call(
        row_kernel, "grad_row", shape(piece, width), [VMEM] * 2, (both, both_far)
    )
    layer_out, feature_grad = call(
        output_kernel, "outputs", [shape(slab, width)] * 2, [VMEM] * (3 + col_devices),
        (weight, column_keep, both_far, first, *row_got),
    )
    gathered = call(
        gather_kernel, "weight_grad", shape(width, width), [VMEM] * col_devices,
        exchange([grad_row] * col_devices, "col"),
    )
    weight_grad = gathered.astype(F32) * (1.0 / math.sqrt(row_devices * col_devices * slab))
    return (layer_out[None], feature_grad[None], weight_grad)


def solution(mesh):
    placed = (
        P("col", "row", None),
        P(),
        P("row", "col", None, None, None),
        P("row", "col", None),
        P("row", "col"),
        P("row", "col", None),
    )
    return jax.shard_map(
        body,
        mesh=mesh,
        in_specs=placed,
        out_specs=(P("row", "col", None), P("col", "row", None), P()),
        check_vma=False,
    )
```
